32 devices in a mesh: gx: 2 (over y), gy: 4 (over x, core), gz: 4 (over z).
Axes of the slice: x: 2, y: 2, z: 4, core: 2. Of those that a mesh axis runs over, the one named last changes fastest.
Arguments:
- level_set: float32 [32, 64, 512], P('gx', 'gy', 'gz'), may hold values from 0 to 1
- velocity: float32 [3, 32, 64, 512], P(None, 'gx', 'gy', 'gz'), may hold values from -6 to 6
- source: float32 [32, 64, 512], P('gx', 'gy', 'gz'), may hold values from -6 to 6
- coarse_factor: float32 [32, 32], P(('gx', 'gy', 'gz')), may hold values from -0.2 to 0.2
Outputs:
- level_set_new: float32 [32, 64, 512], P('gx', 'gy', 'gz')
- pressure: float32 [32, 64, 512], P('gx', 'gy', 'gz')
The draws below stay inside these ranges and needn't reach their ends.
All inputs are finite; a program needn't handle non-finite values.
Results may differ from the reference program's by a relative error of at most 0.029.
Values sent between devices are 32-bit elements; how exact they have to be, the bound alone decides.
No kernel may reach another device: no remote copies, remote signals or barrier semaphores. Data moves between devices by JAX's collectives and lax.ppermute only.
A program may use at most 64 MiB of HBM per device.

```python
import math
import jax
import jax.numpy as jnp
import numpy as np
from jax import lax

NP = 8
ELX = 2
ELY = 2
ELZ = 16
RSWEEPS = 2
ITERS = 6
NX = 32
NY = 64
NZ = 512
NCOARSE = 32
N_GX = 2
N_GY = 4
N_GZ = 4


def draw_coarse_factor(key, part):
    first_key = jax.random.fold_in(key, 11)
    second_key = jax.random.fold_in(key, 23)
    noise = jax.random.normal(first_key, (NCOARSE, NCOARSE), jnp.float32)
    leading = jax.random.uniform(second_key, (NCOARSE,), jnp.float32, 0.6, 1.4)
    return 0.05 * (jnp.diag(leading) + 0.6 * noise / math.sqrt(NCOARSE))


def block_scale(stream_key, extent, pieces, low, top_value):
    def one(dim, shards_of):
        heights = jax.random.uniform(jax.random.fold_in(jax.random.fold_in(stream_key, 6), dim), (shards_of,), jnp.float32, low / len(pieces), top_value / len(pieces))
        return jnp.repeat(jnp.exp(heights), extent[dim] // shards_of).reshape((-1,) + (1,) * (len(extent) - dim - 1))

    gain = one(*pieces[0])
    for cut in pieces[1:]:
        gain = gain * one(*cut)
    return gain


def normal_values(rng, dims, deviation, reach, pieces=(), dtype=jnp.bfloat16):
    values = jax.random.normal(rng, dims, jnp.float32) * deviation
    if len(pieces) > 0:
        values = block_scale(rng, dims, pieces, -0.22, 0.18) * values
    return jnp.clip(values, min=-reach, max=reach).astype(dtype)


def setup_inputs(seed: int = 0) -> dict:
    arg_keys = jax.random.split(jax.random.key(seed), 5)
    level_set = jnp.clip(1.0 * jax.random.uniform(arg_keys[0], (NX, NY, NZ), jnp.float32) ** block_scale(arg_keys[0], (NX, NY, NZ), ((0, 2), (1, 4), (2, 4)), -0.2, 0.2), 0.0, 1.0)
    velocity = normal_values(arg_keys[1], (3, NX, NY, NZ), 1.0, 6.0, ((1, 2), (2, 4), (3, 4)), jnp.float32)
    source = normal_values(arg_keys[2], (NX, NY, NZ), 1.0, 6.0, ((0, 2), (1, 4), (2, 4)), jnp.float32)
    coarse_factor = draw_coarse_factor(jax.random.fold_in(arg_keys[4], 71), 0)
    return dict(level_set=level_set, velocity=velocity, source=source, coarse_factor=coarse_factor)


GLL_POINTS = (-1.0, -0.8717401485096066, -0.5917001814331423, -0.2092992179024789, 0.2092992179024789, 0.5917001814331423, 0.8717401485096066, 1.0)
GLL_WEIGHTS = (0.03571428571428571, 0.21070422714350603, 0.3411226924835044, 0.4124587946587038, 0.4124587946587038, 0.3411226924835044, 0.21070422714350603, 0.03571428571428571)
HIGHEST = lax.Precision.HIGHEST
TIME_STEP = 0.02
PSEUDO_STEP = 0.004
INTERFACE_WIDTH = 0.5
GAS_DENSITY = 0.1
SOURCE_SCALE = 20.0

def node_tables():
    points = np.array(GLL_POINTS)
    amount = points.shape[0]
    barycentric = np.ones(amount)
    for target in range(amount):
        for partner in range(amount):
            if partner != target:
                barycentric[target] = barycentric[target] / (points[target] - points[partner])
    derivative = np.zeros((amount, amount))
    for target in range(amount):
        for partner in range(amount):
            if partner != target:
                derivative[target, partner] = barycentric[partner] / barycentric[target] / (points[target] - points[partner])
        derivative[target, target] = -np.sum(derivative[target])
    return derivative

def apply_axis(values, matrix, which_axis):
    first_size, second_size, third_size = values.shape
    if which_axis == 0:
        blocks = values.reshape(first_size // NP, NP, second_size, third_size)
        result = jnp.einsum('ai,eiyz->eayz', matrix, blocks, precision=HIGHEST)
    elif which_axis == 1:
        blocks = values.reshape(first_size, second_size // NP, NP, third_size)
        result = jnp.einsum('aj,xejz->xeaz', matrix, blocks, precision=HIGHEST)
    else:
        blocks = values.reshape(first_size, second_size, third_size // NP, NP)
        result = jnp.einsum('ak,xyek->xyea', matrix, blocks, precision=HIGHEST)
    return result.reshape(values.shape)

def edge_passes(padded):
    summed = padded
    for which_axis in (1, 2, 3):
        amount = summed.shape[which_axis] - 2
        center = lax.slice_in_dim(summed, 1, amount + 1, axis=which_axis)
        upper_side = lax.slice_in_dim(summed, 2, amount + 2, axis=which_axis)
        lower_side = lax.slice_in_dim(summed, 0, amount, axis=which_axis)
        shape_list = [1, 1, 1, 1]
        shape_list[which_axis] = amount
        position = (jnp.arange(amount) % NP).reshape(shape_list)
        summed = center + jnp.where(position == NP - 1, upper_side, 0.0) + jnp.where(position == 0, lower_side, 0.0)
    return summed

def assemble(stacked):
    return edge_passes(jnp.pad(stacked, ((0, 0), (1, 1), (1, 1), (1, 1))))

def mass_weights(shape_tuple):
    weights = jnp.asarray(np.array(GLL_WEIGHTS), jnp.float32)
    along_x = jnp.tile(weights, shape_tuple[0] // NP)
    along_y = jnp.tile(weights, shape_tuple[1] // NP)
    along_z = jnp.tile(weights, shape_tuple[2] // NP)
    return along_x[:, None, None] * along_y[None, :, None] * along_z[None, None, :]

def reference(level_set, velocity, source, coarse_factor):
    derivative = node_tables()
    deriv_table = jnp.asarray(derivative, jnp.float32)
    deriv_trans = jnp.asarray(derivative.T, jnp.float32)
    square_trans = jnp.asarray((derivative * derivative).T, jnp.float32)
    bmass = mass_weights(level_set.shape)
    gradient = [apply_axis(level_set, deriv_table, which_axis) for which_axis in range(3)]
    advect = velocity[0] * gradient[0] + velocity[1] * gradient[1] + velocity[2] * gradient[2]
    divergence = apply_axis(bmass * velocity[0], deriv_trans, 0) + apply_axis(bmass * velocity[1], deriv_trans, 1) + apply_axis(bmass * velocity[2], deriv_trans, 2) + bmass * source
    assembled = assemble(jnp.stack([bmass * advect, bmass, divergence]))
    mass_sum = assembled[1]
    weight = bmass / mass_sum
    level_now = level_set - TIME_STEP * assembled[0] / mass_sum
    rhs_field = SOURCE_SCALE * assembled[2]
    for sweep in range(RSWEEPS):
        gradient = [apply_axis(level_now, deriv_table, which_axis) for which_axis in range(3)]
        inv_norm = 1.0 / jnp.sqrt(1.0 + gradient[0] * gradient[0] + gradient[1] * gradient[1] + gradient[2] * gradient[2])
        compress = level_now * (1.0 - level_now) * inv_norm
        weak_form = apply_axis(bmass * (compress * gradient[0] - INTERFACE_WIDTH * gradient[0]), deriv_trans, 0)
        weak_form = weak_form + apply_axis(bmass * (compress * gradient[1] - INTERFACE_WIDTH * gradient[1]), deriv_trans, 1)
        weak_form = weak_form + apply_axis(bmass * (compress * gradient[2] - INTERFACE_WIDTH * gradient[2]), deriv_trans, 2)
        level_now = level_now + PSEUDO_STEP * assemble(weak_form[None])[0] / mass_sum
    inverse_density = 1.0 / (GAS_DENSITY + (1.0 - GAS_DENSITY) * jnp.clip(level_now, 0.0, 1.0))
    scaled = bmass * inverse_density
    diag_local = apply_axis(scaled, square_trans, 0) + apply_axis(scaled, square_trans, 1) + apply_axis(scaled, square_trans, 2) + bmass
    diagonal = assemble(diag_local[None])[0]

    def operator(values):
        local_part = bmass * values
        for which_axis in range(3):
            local_part = local_part + apply_axis(scaled * apply_axis(values, deriv_table, which_axis), deriv_trans, which_axis)
        return assemble(local_part[None])[0]

    def precondition(residual):
        blocked = (weight * residual).reshape(N_GX, ELX * NP, N_GY, ELY * NP, N_GZ, ELZ * NP)
        restricted = lax.optimization_barrier(jnp.sum(blocked, axis=(1, 3, 5))).reshape(-1)
        coarse_mid = jnp.dot(coarse_factor.T, restricted, precision=HIGHEST)
        coarse_value = jnp.dot(coarse_factor, coarse_mid, precision=HIGHEST).reshape(N_GX, 1, N_GY, 1, N_GZ, 1)
        spread = (weight.reshape(N_GX, ELX * NP, N_GY, ELY * NP, N_GZ, ELZ * NP) * coarse_value).reshape(weight.shape)
        result = residual / diagonal + assemble(spread[None])[0]
        return (result, jnp.sum(weight * residual * result))
    pressure = jnp.zeros_like(rhs_field)
    residual = rhs_field
    direction, inner_now = precondition(residual)
    for step in range(ITERS):
        image = operator(direction)
        step_size = inner_now / jnp.sum(weight * direction * image)
        pressure = pressure + step_size * direction
        residual = residual - step_size * image
        if step + 1 < ITERS:
            preconditioned, inner_next = precondition(residual)
            direction = preconditioned + inner_next / inner_now * direction
            inner_now = inner_next
    return (level_now, pressure)
```

```python
import jax
import jax.numpy as jnp
import ml_dtypes
import numpy as np
from jax import lax
from jax.experimental import pallas as pl
from jax.experimental.pallas import tpu as pltpu
from jax.sharding import PartitionSpec as P

NP = 8
RSWEEPS = 2
ITERS = 6
AXES = ("gx", "gy", "gz")

GLL_POINTS = (
    -1.0,
    -0.8717401485096066,
    -0.5917001814331423,
    -0.2092992179024789,
    0.2092992179024789,
    0.5917001814331423,
    0.8717401485096066,
    1.0,
)
GLL_WEIGHTS = (
    0.03571428571428571,
    0.21070422714350603,
    0.3411226924835044,
    0.4124587946587038,
    0.4124587946587038,
    0.3411226924835044,
    0.21070422714350603,
    0.03571428571428571,
)
HIGHEST = lax.Precision.HIGHEST
TIME_STEP = 0.02
PSEUDO_STEP = 0.004
INTERFACE_WIDTH = 0.5
GAS_DENSITY = 0.1
SOURCE_SCALE = 20.0
F32 = jnp.float32
BF16 = jnp.bfloat16


def node_tables():
    points = np.array(GLL_POINTS)
    amount = points.shape[0]
    barycentric = np.ones(amount)
    for target in range(amount):
        for partner in range(amount):
            if partner != target:
                barycentric[target] = barycentric[target] / (points[target] - points[partner])
    derivative = np.zeros((amount, amount))
    for target in range(amount):
        for partner in range(amount):
            if partner != target:
                derivative[target, partner] = (
                    barycentric[partner] / barycentric[target] / (points[target] - points[partner])
                )
        derivative[target, target] = -np.sum(derivative[target])
    return derivative


DERIV = node_tables()
TRANS = DERIV.T.copy()
SQUARE = (DERIV * DERIV).T.copy()
WEIGHTS = np.array(GLL_WEIGHTS)

BX, BY, BZ = 16, 16, 128
ROWS = BX * BY


def split_bf16(matrix):
    full = matrix.astype(np.float32)
    high = full.astype(ml_dtypes.bfloat16)
    low = (full - high.astype(np.float32)).astype(ml_dtypes.bfloat16)
    return high, low


def const_tables():
    parts = []
    for matrix in (DERIV, TRANS, SQUARE):
        for shift in range(NP):
            column = np.array([matrix[s, (s - shift) % NP] for s in range(NP)])
            parts.append(np.repeat(column[:, None], BZ, axis=1))
    wy = np.tile(WEIGHTS, BY // NP)
    wz = np.tile(WEIGHTS, BZ // NP)
    parts.append(wy[:, None] * wz[None, :])
    parts.append(1.0 / (wy[:, None] * wz[None, :]))
    return np.concatenate(parts, axis=0).astype(np.float32)


def z_tables():
    out = []
    for matrix in (DERIV, TRANS, SQUARE):
        high, low = split_bf16(np.kron(np.eye(BZ // NP), matrix.T))
        out += [high, low]
    return np.concatenate(out, axis=0)


KIND = {"d": 0, "t": 1, "s": 2}
MATS = {"d": DERIV, "t": TRANS, "s": SQUARE}


def along_x(v, kind):
    matrix = MATS[kind]
    sign = 1.0 if abs(matrix[7, 7] - matrix[0, 0]) < abs(matrix[7, 7] + matrix[0, 0]) else -1.0
    out = [None] * BX
    for e in range(BX // NP):
        part = [v[(e * NP + i) * BY : (e * NP + i + 1) * BY] for i in range(NP)]
        even = [part[j] + part[7 - j] for j in range(4)]
        odd = [part[j] - part[7 - j] for j in range(4)]
        for i in range(4):
            a = b = None
            for j in range(4):
                ca = float(0.5 * (matrix[i, j] + matrix[i, 7 - j]))
                cb = float(0.5 * (matrix[i, j] - matrix[i, 7 - j]))
                a = ca * even[j] if a is None else a + ca * even[j]
                b = cb * odd[j] if b is None else b + cb * odd[j]
            out[e * NP + i] = a + b
            out[e * NP + 7 - i] = a - b if sign > 0 else b - a
    return jnp.concatenate(out, axis=0)


def along_y(v, kind, tab):
    v3 = v.reshape(ROWS // NP, NP, BZ)
    base = KIND[kind] * NP * NP
    total = None
    for shift in range(NP):
        coef = tab[base + shift * NP : base + (shift + 1) * NP, :][None]
        rolled = v3 if shift == 0 else pltpu.roll(v3, shift, 1)
        total = coef * rolled if total is None else total + coef * rolled
    return total.reshape(ROWS, BZ)


def along_z(v, kind, zt):
    base = KIND[kind] * 2 * BZ
    high = zt[base : base + BZ, :]
    low = zt[base + BZ : base + 2 * BZ, :]
    vh = v.astype(BF16)
    vl = (v - vh.astype(F32)).astype(BF16)

    def dot(a, b):
        return jnp.dot(a, b, preferred_element_type=F32)

    return dot(vh, high) + (dot(vl, high) + dot(vh, low))


def bmass_of(tab):
    base = 3 * NP * NP
    yz = tab[base : base + BY, :]
    return jnp.concatenate([yz * float(WEIGHTS[x % NP]) for x in range(BX)], axis=0)


def local_sum(v):
    parts = [v[x * BY : (x + 1) * BY] for x in range(BX)]
    for x in range(NP, BX, NP):
        both = parts[x - 1] + parts[x]
        parts[x - 1] = both
        parts[x] = both
    sub = lax.broadcasted_iota(jnp.int32, (NP, BZ), 0)
    out = []
    for x in range(BX):
        a, b = parts[x][:NP], parts[x][NP:]
        out.append(jnp.where(sub == NP - 1, a + pltpu.roll(b, NP - 1, 0), a))
        out.append(jnp.where(sub == 0, b + pltpu.roll(a, 1, 0), b))
    v = jnp.concatenate(out, axis=0)
    lane = lax.broadcasted_iota(jnp.int32, (NP, BZ), 1)
    last = (lane % NP == NP - 1) & (lane < BZ - 1)
    first = (lane % NP == 0) & (lane > 0)
    v3 = v.reshape(ROWS // NP, NP, BZ)
    up = pltpu.roll(v3, BZ - 1, 2)
    down = pltpu.roll(v3, 1, 2)
    v3 = v3 + jnp.where(last[None], up, jnp.where(first[None], down, 0.0))
    return v3.reshape(ROWS, BZ)


class Geometry:
    def __init__(self, sizes):
        self.sizes = sizes
        self.at = [lax.axis_index(a) for a in AXES]
        self.low = [g > 0 for g in self.at]
        self.high = [g < n - 1 for g, n in zip(self.at, sizes)]
        self.me = (self.at[0] * sizes[1] + self.at[1]) * sizes[2] + self.at[2]

    def neighbour(self, *step):
        ok = None
        number = self.me
        strides = (self.sizes[1] * self.sizes[2], self.sizes[2], 1)
        for a in range(3):
            if step[a]:
                there = self.high[a] if step[a] > 0 else self.low[a]
                ok = there if ok is None else jnp.logical_and(ok, there)
                number = number + step[a] * strides[a]
        return jnp.where(ok, number, self.me)

    def half(self, flag):
        return jnp.where(flag, 0.5, 1.0).astype(F32)

    def x_share(self, x):
        if x == 0:
            return self.half(self.low[0])
        if x == BX - 1:
            return self.half(self.high[0])
        return None

    def y_share(self):
        row = lax.broadcasted_iota(jnp.int32, (BY, BZ), 0)
        one = jnp.where(row == 0, self.half(self.low[1]), 1.0)
        return jnp.where(row == BY - 1, self.half(self.high[1]), one)

    def z_share(self, shape, dim):
        lane = lax.broadcasted_iota(jnp.int32, shape, dim)
        one = jnp.where(lane == 0, self.half(self.low[2]), 1.0)
        return jnp.where(lane == BZ - 1, self.half(self.high[2]), one)

    def yz_weight(self):
        row = lax.broadcasted_iota(jnp.int32, (BY, BZ), 0)
        lane = lax.broadcasted_iota(jnp.int32, (BY, BZ), 1)
        inside_y = ((row % NP == 0) & (row > 0)) | ((row % NP == NP - 1) & (row < BY - 1))
        inside_z = ((lane % NP == 0) & (lane > 0)) | ((lane % NP == NP - 1) & (lane < BZ - 1))
        wy = jnp.where(inside_y, 0.5, self.y_share())
        wz = jnp.where(inside_z, 0.5, self.z_share((BY, BZ), 1))
        return wy * wz

    def x_weight(self, x):
        if x in (0, BX - 1):
            return self.x_share(x)
        return 0.5 if x % NP in (0, NP - 1) else 1.0


def inverse_mass(geo, tab):
    base = 3 * NP * NP + BY
    yz = tab[base : base + BY, :] * geo.yz_weight()
    return jnp.concatenate(
        [yz * (geo.x_weight(x) * float(1.0 / WEIGHTS[x % NP])) for x in range(BX)], axis=0
    )


def face_steps(n):
    return ("swap",) if n == 2 else ("up", "down")


class Layout:
    def __init__(self, sizes):
        self.sizes = sizes
        self.devices = sizes[0] * sizes[1] * sizes[2]
        self.lanes = -(-(self.devices + 3) // 128) * 128
        self.scalar_rows = self.lanes // 128

    def slot_rows(self, fields):
        need = self.scalar_rows + 2 * fields
        if fields == 2:
            need += self.scalar_rows
        return 4 if need <= 4 else -(-need // 8) * 8


def pick_faces(geo, axis, n, low, high):
    if n == 2:
        return [jnp.where(geo.at[axis] == 0, high, low)]
    return [high, low]


def send_fields(geo, lay, f_refs, scalars, send_ref, xs, ys, fields, extra=None):
    rows = lay.slot_rows(fields)
    base = [scalars[:, i * 128 : (i + 1) * 128] for i in range(lay.scalar_rows)]
    used = lay.scalar_rows
    if extra is not None:
        base.append(jnp.zeros((2 * fields, 128), F32))
        base += [extra[:, i * 128 : (i + 1) * 128] for i in range(lay.scalar_rows)]
        used += 2 * fields + lay.scalar_rows
    base.append(jnp.zeros((rows - used, 128), F32))
    base = jnp.concatenate([b for b in base if b.shape[0]], axis=0)
    send_ref[...] = jnp.broadcast_to(base[None], (lay.devices, rows, 128))
    picker = lax.broadcasted_iota(jnp.int32, (8, BZ), 0)
    lane = lax.broadcasted_iota(jnp.int32, (8, BZ), 1)
    picker = jnp.where(
        ((picker == 0) & (lane == 0)) | ((picker == 1) & (lane == BZ - 1)), 1.0, 0.0
    ).astype(F32)
    for k, f_ref in enumerate(f_refs):
        at = lay.scalar_rows + 2 * k
        halves = [
            lax.dot_general(
                picker,
                f_ref[h * 128 : (h + 1) * 128, :],
                (((1,), (1,)), ((), ())),
                precision=HIGHEST,
                preferred_element_type=F32,
            )
            for h in range(2)
        ]
        for dz in (-1, 1):
            side = 0 if dz < 0 else 1
            pair = jnp.concatenate([halves[0][side : side + 1], halves[1][side : side + 1]], axis=0)
            for dx in (-1, 0, 1):
                for dy in (-1, 0, 1):
                    send_ref[geo.neighbour(dx, dy, dz), at : at + 2, :] = pair
        for dx in (-1, 1):
            for dy in (-1, 1):
                row = (BX - 1 if dx > 0 else 0) * BY + (BY - 1 if dy > 0 else 0)
                send_ref[geo.neighbour(dx, dy, 0), at : at + 1, :] = f_ref[row : row + 1, :]
        lowx, highx = f_ref[0:BY, :], f_ref[ROWS - BY : ROWS, :]
        for ref, face in zip(xs, pick_faces(geo, 0, lay.sizes[0], lowx, highx)):
            ref[k * BY : (k + 1) * BY, :] = face
        lowy = f_ref[pl.ds(0, BX, stride=BY), :]
        highy = f_ref[pl.ds(BY - 1, BX, stride=BY), :]
        for ref, face in zip(ys, pick_faces(geo, 1, lay.sizes[1], lowy, highy)):
            ref[k * BX : (k + 1) * BX, :] = face
    send_ref[geo.me] = base


def came_from(geo, axis, n, refs, k, size):
    if n == 2:
        face = refs[0][k * size : (k + 1) * size, :]
        return (
            jnp.where(geo.low[axis], face, 0.0),
            jnp.where(geo.high[axis], face, 0.0),
        )
    up = refs[0][k * size : (k + 1) * size, :]
    down = refs[1][k * size : (k + 1) * size, :]
    return jnp.where(geo.low[axis], up, 0.0), jnp.where(geo.high[axis], down, 0.0)


def received(geo, lay, f, recv_ref, xs, ys, w_ref, k):
    at = lay.scalar_rows + 2 * k
    lane = lax.broadcasted_iota(jnp.int32, (2, 128), 1)
    row = lax.broadcasted_iota(jnp.int32, (2, 128), 0)
    sides = []
    for dz in (-1, 1):
        total = None
        for dx in (-1, 0, 1):
            for dy in (-1, 0, 1):
                pair = recv_ref[geo.neighbour(dx, dy, dz), at : at + 2, :]
                shift = 0
                keep = None
                if dx:
                    pair = jnp.concatenate([pair[1:2], pair[0:1]], axis=0)
                    shift += 112 * dx
                    want = (lane >= 112) & (row == 1) if dx > 0 else (lane < 16) & (row == 0)
                    keep = want
                if dy:
                    shift += 15 * dy
                    want = lane % 16 == (15 if dy > 0 else 0)
                    keep = want if keep is None else keep & want
                if shift % 128:
                    pair = pltpu.roll(pair, shift % 128, 1)
                if keep is not None:
                    pair = jnp.where(keep, pair, 0.0)
                total = pair if total is None else total + pair
        sides.append(total)
    placer_row = lax.broadcasted_iota(jnp.int32, (8, BZ), 0)
    placer_lane = lax.broadcasted_iota(jnp.int32, (8, BZ), 1)
    placer = jnp.where(
        ((placer_row == 0) & (placer_lane == 0)) | ((placer_row == 1) & (placer_lane == BZ - 1)),
        1.0,
        0.0,
    ).astype(F32)
    halves = []
    for h in range(2):
        stack = jnp.concatenate(
            [sides[0][h : h + 1], sides[1][h : h + 1], jnp.zeros((6, 128), F32)], axis=0
        )
        halves.append(
            lax.dot_general(
                stack,
                placer,
                (((0,), (0,)), ((), ())),
                precision=HIGHEST,
                preferred_element_type=F32,
            )
        )
    w_ref[...] = f + jnp.concatenate(halves, axis=0)
    lowx, highx = came_from(geo, 0, lay.sizes[0], xs, k, BY)
    w_ref[0:BY, :] += lowx
    w_ref[ROWS - BY : ROWS, :] += highx
    lowy, highy = came_from(geo, 1, lay.sizes[1], ys, k, BX)
    w_ref[pl.ds(0, BX, stride=BY), :] += lowy
    w_ref[pl.ds(BY - 1, BX, stride=BY), :] += highy
    for dx in (-1, 1):
        for dy in (-1, 1):
            row = (BX - 1 if dx > 0 else 0) * BY + (BY - 1 if dy > 0 else 0)
            w_ref[row : row + 1, :] += recv_ref[geo.neighbour(dx, dy, 0), at : at + 1, :]


def received_scalars(lay, recv_ref):
    total = jnp.sum(recv_ref[...], axis=0)
    return jnp.concatenate([total[i : i + 1] for i in range(lay.scalar_rows)], axis=1)


def coarse_tables(geo, lay, places):
    steps = [places[a : a + 1, :] - geo.at[a].astype(F32) for a in range(3)]
    z = lax.broadcasted_iota(jnp.int32, (BZ, lay.lanes), 0)
    lane = lax.broadcasted_iota(jnp.int32, (1, lay.lanes), 1)
    dz = jnp.broadcast_to(steps[2], (BZ, lay.lanes))
    zmat = jnp.where(dz == 0.0, geo.z_share((BZ, lay.lanes), 0), 0.0)
    zmat = jnp.where((dz == 1.0) & (z == BZ - 1), 0.5, zmat)
    zmat = jnp.where((dz == -1.0) & (z == 0), 0.5, zmat)
    zmat = jnp.where(jnp.broadcast_to(lane, (BZ, lay.lanes)) >= lay.devices, 1.0, zmat)
    row = lax.broadcasted_iota(jnp.int32, (16, lay.lanes), 0)
    near = (jnp.abs(steps[0]) <= 1.0) & (jnp.abs(steps[1]) <= 1.0)
    own = (steps[0] + 1.0) * 3.0 + steps[1] + 1.0
    own = jnp.where(near & (lane < lay.devices), own, -1.0)
    own = jnp.where(
        (lane >= lay.devices) & (lane < lay.devices + 3),
        (lane - lay.devices + 9).astype(F32),
        own,
    )
    msel = jnp.where(row.astype(F32) == jnp.broadcast_to(own, (16, lay.lanes)), 1.0, 0.0)
    return zmat, msel.astype(F32)


def partial_sums(geo, v, sums, q_ref, zmat, msel):
    first, last = v[0:BY], v[ROWS - BY : ROWS]
    middle = first * geo.x_share(0) + last * geo.x_share(BX - 1)
    for x in range(1, BX - 1):
        middle = middle + v[x * BY : (x + 1) * BY]
    share = geo.y_share()
    for i, part in enumerate((0.5 * first, middle, 0.5 * last)):
        q_ref[3 * i : 3 * i + 1, :] = 0.5 * part[0:1]
        q_ref[3 * i + 1 : 3 * i + 2, :] = jnp.sum(part * share, axis=0, keepdims=True)
        q_ref[3 * i + 2 : 3 * i + 3, :] = 0.5 * part[BY - 1 : BY]
    q_ref[9:16, :] = jnp.zeros((7, BZ), F32)
    for i, total in enumerate(sums):
        q_ref[9 + i : 10 + i, :] = total
    rows = jnp.dot(q_ref[...], zmat, precision=HIGHEST, preferred_element_type=F32)
    return jnp.sum(rows * msel, axis=0, keepdims=True)


def spread(geo, values, zmat, msel):
    rows = lax.dot_general(
        msel * values,
        zmat,
        (((1,), (1,)), ((), ())),
        precision=HIGHEST,
        preferred_element_type=F32,
    )
    y = lax.broadcasted_iota(jnp.int32, (BY, BZ), 0)
    share = geo.y_share()
    planes = []
    for i in range(3):
        plane = share * rows[3 * i + 1 : 3 * i + 2]
        plane = plane + jnp.where(y == 0, 0.5 * rows[3 * i : 3 * i + 1], 0.0)
        planes.append(plane + jnp.where(y == BY - 1, 0.5 * rows[3 * i + 2 : 3 * i + 3], 0.0))
    out = [planes[1]] * BX
    out[0] = planes[1] * geo.x_share(0) + 0.5 * planes[0]
    out[BX - 1] = planes[1] * geo.x_share(BX - 1) + 0.5 * planes[2]
    return out


def all_rows(v):
    total = v[0:8]
    for i in range(1, ROWS // 8):
        total = total + v[8 * i : 8 * i + 8]
    return jnp.sum(total, axis=0, keepdims=True)


def weighted_rows(geo, v):
    yz = geo.yz_weight()
    total = None
    for x in range(BX):
        weight = geo.x_weight(x)
        part = v[x * BY : (x + 1) * BY]
        if not (isinstance(weight, float) and weight == 1.0):
            part = part * weight
        total = part if total is None else total + part
    return jnp.sum(total * yz, axis=0, keepdims=True)


def weak_form(level, tab, zt):
    gx, gy, gz = along_x(level, "d"), along_y(level, "d", tab), along_z(level, "d", zt)
    inv_norm = 1.0 / jnp.sqrt(1.0 + gx * gx + gy * gy + gz * gz)
    coef = bmass_of(tab) * (level * (1.0 - level) * inv_norm - INTERFACE_WIDTH)
    return (
        along_x(coef * gx, "t") + along_y(coef * gy, "t", tab) + along_z(coef * gz, "t", zt)
    )


def stiffness(v, scaled, tab, zt):
    out = bmass_of(tab) * v
    out = out + along_x(scaled * along_x(v, "d"), "t")
    out = out + along_y(scaled * along_y(v, "d", tab), "t", tab)
    return out + along_z(scaled * along_z(v, "d", zt), "t", zt)


def local_step(geo, lay, residual, dinv, scaled, state, p_old, refs):
    tab, zt, zmat, msel, gram, u_ref, f_ref, send_ref, xs, ys, q_ref, state_ref, final = refs
    s_row, ts_row, gamma, curvature = state
    values = jnp.dot(s_row, gram, precision=HIGHEST, preferred_element_type=F32)
    coarse = jnp.sum(s_row * values, axis=1, keepdims=True)
    jacobi = residual * dinv
    planes = spread(geo, values, zmat, msel)
    u = jnp.concatenate([jacobi[x * BY : (x + 1) * BY] + planes[x] for x in range(BX)], axis=0)
    u_ref[...] = u
    local = stiffness(u, scaled, tab, zt)
    sums = [weighted_rows(geo, residual * jacobi), all_rows(u * local)]
    sums.append(jnp.zeros((1, BZ), F32) if p_old is None else all_rows(p_old * local))
    scalars = partial_sums(geo, local, sums, q_ref, zmat, msel)
    ones = jnp.ones_like(s_row)
    state_ref[...] = jnp.concatenate(
        [s_row, ts_row, ones * gamma, ones * curvature, ones * coarse, jnp.zeros((3, lay.lanes), F32)],
        axis=0,
    )
    if final:
        rows = [scalars[:, i * 128 : (i + 1) * 128] for i in range(lay.scalar_rows)]
        rows = jnp.concatenate(rows, axis=0)
        send_ref[...] = jnp.broadcast_to(rows[None], send_ref.shape)
        return
    f_ref[...] = local_sum(local)
    send_fields(geo, lay, [f_ref], scalars, send_ref, xs, ys, 1)


def step_sizes(lay, recv_ref, state_ref, first):
    row = received_scalars(lay, recv_ref)
    lane = lax.broadcasted_iota(jnp.int32, row.shape, 1)

    def pick(which):
        return jnp.sum(jnp.where(lane == lay.devices + which, row, 0.0), axis=1, keepdims=True)

    gamma = pick(0) + state_ref[4:5, 0:1]
    if first:
        curvature = pick(1)
        beta = None
    else:
        beta = gamma / state_ref[2:3, 0:1]
        curvature = pick(1) + beta * (2.0 * pick(2) + beta * state_ref[3:4, 0:1])
    return row, gamma, curvature, beta, gamma / curvature


def build(mesh):
    sizes = tuple(int(mesh.shape[a]) for a in AXES)
    lay = Layout(sizes)
    steps = [face_steps(sizes[0]), face_steps(sizes[1])]
    nx, ny = len(steps[0]), len(steps[1])
    tab_np, zt_np = const_tables(), z_tables()
    number = np.arange(lay.lanes)
    places_np = np.full((8, lay.lanes), -9.0, np.float32)
    places_np[0, : lay.devices] = (number // (sizes[1] * sizes[2]))[: lay.devices]
    places_np[1, : lay.devices] = (number // sizes[2] % sizes[1])[: lay.devices]
    places_np[2, : lay.devices] = (number % sizes[2])[: lay.devices]
    block = jax.ShapeDtypeStruct((ROWS, BZ), F32)

    def like(*shape):
        return jax.ShapeDtypeStruct(shape, F32)

    def outgoing(fields):
        return (
            [like(lay.devices, lay.slot_rows(fields), 128)]
            + [like(BY * fields, BZ)] * nx
            + [like(BX * fields, BZ)] * ny
        )

    def call(kernel, ins, outs, scratch, name):
        spec = pl.BlockSpec(memory_space=pltpu.VMEM)
        return pl.pallas_call(
            kernel,
            out_shape=outs,
            in_specs=[spec] * len(ins),
            out_specs=[spec] * len(outs),
            scratch_shapes=scratch,
            compiler_params=pltpu.CompilerParams(vmem_limit_bytes=48 * 1024 * 1024),
            name=name,
        )(*ins)

    work = pltpu.VMEM((ROWS, BZ), F32)
    qrows = pltpu.VMEM((16, BZ), F32)

    def ring(v, axis, n, step):
        if step == "swap":
            pairs = [(0, 1), (1, 0)]
        else:
            d = 1 if step == "up" else n - 1
            pairs = [(i, (i + d) % n) for i in range(n)]
        return lax.ppermute(v, axis, pairs)

    def exchange(out):
        send, faces = out[0], out[1:]
        recv = lax.all_to_all(send, AXES, 0, 0, tiled=True)
        xs = [ring(faces[i], "gx", sizes[0], s) for i, s in enumerate(steps[0])]
        ys = [ring(faces[nx + i], "gy", sizes[1], s) for i, s in enumerate(steps[1])]
        return [recv, *xs, *ys]

    n_out = 1 + nx + ny

    def split(refs):
        return refs[0], refs[1 : 1 + nx], refs[1 + nx : 1 + nx + ny]

    def start_kernel(level_ref, vel_ref, source_ref, factor_ref, tab_ref, zt_ref, places_ref, *rest):
        send, xs, ys = split(rest[:n_out])
        fa_ref, fd_ref, zmat_ref, msel_ref, q_ref = rest[n_out:]
        geo = Geometry(sizes)
        level = level_ref[...]
        bm = bmass_of(tab_ref)
        advect = vel_ref[0] * along_x(level, "d")
        advect = advect + vel_ref[1] * along_y(level, "d", tab_ref)
        advect = advect + vel_ref[2] * along_z(level, "d", zt_ref)
        fa_ref[...] = local_sum(bm * advect)
        div = bm * source_ref[...] + along_x(bm * vel_ref[0], "t")
        div = div + along_y(bm * vel_ref[1], "t", tab_ref)
        div = div + along_z(bm * vel_ref[2], "t", zt_ref)
        fd_ref[...] = local_sum(div)
        zmat, msel = coarse_tables(geo, lay, places_ref)
        zmat_ref[...] = zmat
        msel_ref[...] = msel
        scalars = partial_sums(geo, div, [], q_ref, zmat, msel)
        send_fields(geo, lay, [fa_ref, fd_ref], scalars, send, xs, ys, 2, factor_ref[...])

    def first_kernel(recv, *rest):
        xs, ys = rest[:nx], rest[nx : nx + ny]
        level_ref, fa_ref, fd_ref, tab_ref, zt_ref = rest[nx + ny : nx + ny + 5]
        out = rest[nx + ny + 5 :]
        send, oxs, oys = split(out[:n_out])
        level_out, f_ref, r_ref, s_ref, gram_ref, w_ref = out[n_out:]
        geo = Geometry(sizes)
        at = lay.scalar_rows + 4
        factor = [recv[:, at + i, :] for i in range(lay.scalar_rows)]
        factor = jnp.concatenate(factor, axis=1)
        if lay.lanes > lay.devices:
            pad = jnp.zeros((lay.lanes - lay.devices, lay.lanes), F32)
            factor = jnp.concatenate([factor, pad], axis=0)
        gram_ref[...] = lax.dot_general(
            factor,
            factor,
            (((1,), (1,)), ((), ())),
            precision=HIGHEST,
            preferred_element_type=F32,
        )
        received(geo, lay, fd_ref[...], recv, xs, ys, w_ref, 1)
        r_ref[...] = SOURCE_SCALE * w_ref[...]
        row = received_scalars(lay, recv)
        s_ref[...] = jnp.broadcast_to(SOURCE_SCALE * row, s_ref.shape)
        received(geo, lay, fa_ref[...], recv, xs, ys, w_ref, 0)
        level = level_ref[...] - TIME_STEP * w_ref[...] * inverse_mass(geo, tab_ref)
        level_out[...] = level
        f_ref[...] = local_sum(weak_form(level, tab_ref, zt_ref))
        send_fields(geo, lay, [f_ref], jnp.zeros((1, lay.lanes), F32), send, oxs, oys, 1)

    def new_level(geo, recv, xs, ys, level_ref, f_ref, tab_ref, w_ref):
        received(geo, lay, f_ref[...], recv, xs, ys, w_ref, 0)
        return level_ref[...] + PSEUDO_STEP * w_ref[...] * inverse_mass(geo, tab_ref)

    def sweep_kernel(recv, *rest):
        xs, ys = rest[:nx], rest[nx : nx + ny]
        level_ref, fin_ref, tab_ref, zt_ref = rest[nx + ny : nx + ny + 4]
        out = rest[nx + ny + 4 :]
        send, oxs, oys = split(out[:n_out])
        level_out, f_ref, w_ref = out[n_out:]
        geo = Geometry(sizes)
        level = new_level(geo, recv, xs, ys, level_ref, fin_ref, tab_ref, w_ref)
        level_out[...] = level
        f_ref[...] = local_sum(weak_form(level, tab_ref, zt_ref))
        send_fields(geo, lay, [f_ref], jnp.zeros((1, lay.lanes), F32), send, oxs, oys, 1)

    def diagonal_kernel(recv, *rest):
        xs, ys = rest[:nx], rest[nx : nx + ny]
        level_ref, fin_ref, tab_ref, zt_ref = rest[nx + ny : nx + ny + 4]
        out = rest[nx + ny + 4 :]
        send, oxs, oys = split(out[:n_out])
        level_out, f_ref, scaled_ref, w_ref = out[n_out:]
        geo = Geometry(sizes)
        level = new_level(geo, recv, xs, ys, level_ref, fin_ref, tab_ref, w_ref)
        level_out[...] = level
        bm = bmass_of(tab_ref)
        scaled = bm / (GAS_DENSITY + (1.0 - GAS_DENSITY) * jnp.clip(level, 0.0, 1.0))
        scaled_ref[...] = scaled
        diag = bm + along_x(scaled, "s") + along_y(scaled, "s", tab_ref) + along_z(scaled, "s", zt_ref)
        f_ref[...] = local_sum(diag)
        send_fields(geo, lay, [f_ref], jnp.zeros((1, lay.lanes), F32), send, oxs, oys, 1)

    def solve_kernel(recv, *rest):
        xs, ys = rest[:nx], rest[nx : nx + ny]
        fin_ref, r_ref, scaled_ref, s_ref, tab_ref, zt_ref, zmat_ref, msel_ref, gram_ref = rest[
            nx + ny : nx + ny + 9
        ]
        out = rest[nx + ny + 9 :]
        send, oxs, oys = split(out[:n_out])
        dinv_ref, u_ref, f_ref, state_ref, w_ref, q_ref = out[n_out:]
        geo = Geometry(sizes)
        received(geo, lay, fin_ref[...], recv, xs, ys, w_ref, 0)
        dinv = 1.0 / w_ref[...]
        dinv_ref[...] = dinv
        zero = jnp.zeros((1, 1), F32)
        s_row = s_ref[0:1, :]
        state = (s_row, jnp.zeros_like(s_row), zero, zero)
        refs = (tab_ref, zt_ref, zmat_ref[...], msel_ref[...], gram_ref[...], u_ref, f_ref, send, oxs, oys)
        local_step(
            geo, lay, r_ref[...], dinv, scaled_ref[...], state, None, (*refs, q_ref, state_ref, False)
        )

    def make_iterate(first, final):
        def iterate_kernel(recv, *rest):
            xs, ys = rest[:nx], rest[nx : nx + ny]
            n_in = 10 + (0 if first else 3)
            ins = rest[nx + ny : nx + ny + n_in]
            fin_ref, r_ref, u_in, dinv_ref, scaled_ref, state_in = ins[:6]
            tab_ref, zt_ref, zmat_ref, msel_ref = ins[6:10]
            gram_ref = rest[nx + ny + n_in]
            p_in, si_in, x_in = (None, None, None) if first else ins[10:13]
            out = rest[nx + ny + n_in + 1 :]
            if final:
                send, oxs, oys = out[0], (), ()
                out = out[1:]
                u_ref, state_ref, p_ref, x_ref, w_ref, q_ref = out
                f_ref = r_out = si_ref = None
            else:
                send, oxs, oys = split(out[:n_out])
                u_ref, state_ref, p_ref, x_ref, r_out, si_ref, f_ref, w_ref, q_ref = out[n_out:]
            geo = Geometry(sizes)
            row, gamma, curvature, beta, alpha = step_sizes(lay, recv, state_in, first)
            received(geo, lay, fin_ref[...], recv, xs, ys, w_ref, 0)
            image = w_ref[...]
            p = u_in[...]
            s_row, ts_row = state_in[0:1, :], row
            if not first:
                p = p + beta * p_in[...]
                image = image + beta * si_in[...]
                ts_row = ts_row + beta * state_in[1:2, :]
            p_ref[...] = p
            x_ref[...] = alpha * p if first else x_in[...] + alpha * p
            residual = r_ref[...] - alpha * image
            if not final:
                si_ref[...] = image
                r_out[...] = residual
            lane = lax.broadcasted_iota(jnp.int32, row.shape, 1)
            ts_row = jnp.where(lane < lay.devices, ts_row, 0.0)
            state = (s_row - alpha * ts_row, ts_row, gamma, curvature)
            refs = (tab_ref, zt_ref, zmat_ref[...], msel_ref[...], gram_ref[...], u_ref, f_ref, send)
            local_step(
                geo,
                lay,
                residual,
                dinv_ref[...],
                scaled_ref[...],
                state,
                p,
                (*refs, oxs, oys, q_ref, state_ref, final),
            )

        return iterate_kernel

    def last_kernel(recv, state_in, u_in, p_in, x_in, out_ref):
        _, _, _, beta, alpha = step_sizes(lay, recv, state_in, False)
        out_ref[...] = x_in[...] + alpha * (u_in[...] + beta * p_in[...])

    def body(level_set, velocity, source, coarse_factor):
        level = level_set.reshape(ROWS, BZ)
        vel = velocity.reshape(3, ROWS, BZ)
        src = source.reshape(ROWS, BZ)
        tab, zt, places = jnp.asarray(tab_np), jnp.asarray(zt_np), jnp.asarray(places_np)
        factor = jnp.pad(coarse_factor, ((0, 0), (0, lay.lanes - lay.devices)))

        out = call(
            start_kernel,
            [level, vel, src, factor, tab, zt, places],
            outgoing(2) + [block, block, like(BZ, lay.lanes), like(16, lay.lanes)],
            [qrows],
            "advect",
        )
        fa, fd, zmat, msel = out[n_out:]
        got = exchange(out[:n_out])
        out = call(
            first_kernel,
            [*got, level, fa, fd, tab, zt],
            outgoing(1) + [block, block, block, like(8, lay.lanes), like(lay.lanes, lay.lanes)],
            [work],
            "sweep_first",
        )
        level, f, residual, s_rows, gram = out[n_out:]
        for _ in range(RSWEEPS - 1):
            got = exchange(out[:n_out])
            out = call(
                sweep_kernel, [*got, level, f, tab, zt], outgoing(1) + [block, block], [work], "sweep"
            )
            level, f = out[n_out:]
        got = exchange(out[:n_out])
        out = call(
            diagonal_kernel,
            [*got, level, f, tab, zt],
            outgoing(1) + [block, block, block],
            [work],
            "diagonal",
        )
        level, f, scaled = out[n_out:]
        got = exchange(out[:n_out])
        out = call(
            solve_kernel,
            [*got, f, residual, scaled, s_rows, tab, zt, zmat, msel, gram],
            outgoing(1) + [block, block, block, like(8, lay.lanes)],
            [work, qrows],
            "solve_start",
        )
        dinv, u, f, state = out[n_out:]
        p = image = x = None
        for step in range(ITERS - 1):
            first, final = step == 0, step == ITERS - 2
            got = exchange(out[:n_out])
            ins = [*got, f, residual, u, dinv, scaled, state, tab, zt, zmat, msel]
            if not first:
                ins += [p, image, x]
            ins.append(gram)
            fields = [block, like(8, lay.lanes), block, block]
            if final:
                outs = [like(lay.devices, lay.scalar_rows, 128)] + fields
            else:
                outs = outgoing(1) + fields + [block, block, block]
            out = call(make_iterate(first, final), ins, outs, [work, qrows], "iterate")
            if final:
                u, state, p, x = out[1:]
            else:
                u, state, p, x, residual, image, f = out[n_out:]
        recv = lax.all_to_all(out[0], AXES, 0, 0, tiled=True)
        (x,) = call(last_kernel, [recv, state, u, p, x], [block], [], "pressure")
        return level.reshape(BX, BY, BZ), x.reshape(BX, BY, BZ)

    return body


def solution(mesh):
    in_specs = (
        P("gx", "gy", "gz"),
        P(None, "gx", "gy", "gz"),
        P("gx", "gy", "gz"),
        P(("gx", "gy", "gz"), None),
    )
    out_specs = (P("gx", "gy", "gz"), P("gx", "gy", "gz"))
    return jax.shard_map(
        build(mesh), mesh=mesh, in_specs=in_specs, out_specs=out_specs, check_vma=False
    )
```

```python
import jax
import jax.numpy as jnp
import ml_dtypes
import numpy as np
from jax import lax
from jax.experimental import pallas as pl
from jax.experimental.pallas import tpu as pltpu
from jax.sharding import PartitionSpec as P

NP = 8
RSWEEPS = 2
ITERS = 6
AXES = ("gx", "gy", "gz")

GLL_POINTS = (
    -1.0,
    -0.8717401485096066,
    -0.5917001814331423,
    -0.2092992179024789,
    0.2092992179024789,
    0.5917001814331423,
    0.8717401485096066,
    1.0,
)
GLL_WEIGHTS = (
    0.03571428571428571,
    0.21070422714350603,
    0.3411226924835044,
    0.4124587946587038,
    0.4124587946587038,
    0.3411226924835044,
    0.21070422714350603,
    0.03571428571428571,
)
HIGHEST = lax.Precision.HIGHEST
TIME_STEP = 0.02
PSEUDO_STEP = 0.004
INTERFACE_WIDTH = 0.5
GAS_DENSITY = 0.1
SOURCE_SCALE = 20.0
F32 = jnp.float32
BF16 = jnp.bfloat16


def node_tables():
    points = np.array(GLL_POINTS)
    amount = points.shape[0]
    barycentric = np.ones(amount)
    for target in range(amount):
        for partner in range(amount):
            if partner != target:
                barycentric[target] = barycentric[target] / (points[target] - points[partner])
    derivative = np.zeros((amount, amount))
    for target in range(amount):
        for partner in range(amount):
            if partner != target:
                derivative[target, partner] = (
                    barycentric[partner] / barycentric[target] / (points[target] - points[partner])
                )
        derivative[target, target] = -np.sum(derivative[target])
    return derivative


DERIV = node_tables()
TRANS = DERIV.T.copy()
SQUARE = (DERIV * DERIV).T.copy()
WEIGHTS = np.array(GLL_WEIGHTS)

BX, BY, BZ = 16, 16, 128
ROWS = BX * BY


def split_bf16(matrix):
    full = matrix.astype(np.float32)
    high = full.astype(ml_dtypes.bfloat16)
    low = (full - high.astype(np.float32)).astype(ml_dtypes.bfloat16)
    return high, low


def const_tables():
    parts = []
    for matrix in (DERIV, TRANS, SQUARE):
        for column in matrix.T:
            parts.append(np.repeat(column[:, None], BZ, axis=1))
    wy = np.tile(WEIGHTS, BY // NP)
    wz = np.tile(WEIGHTS, BZ // NP)
    parts.append(wy[:, None] * wz[None, :])
    parts.append(1.0 / (wy[:, None] * wz[None, :]))
    return np.concatenate(parts, axis=0).astype(np.float32)


def z_tables():
    out = []
    for matrix in (DERIV, TRANS, SQUARE):
        high, low = split_bf16(np.kron(np.eye(BZ // NP), matrix.T))
        top = np.concatenate([high, low], axis=1)
        out += [top, np.concatenate([high, np.zeros_like(low)], axis=1)]
    return np.concatenate(out, axis=0)


KIND = {"d": 0, "t": 1, "s": 2}
MATS = {"d": DERIV, "t": TRANS, "s": SQUARE}


def along_x(v, kind):
    matrix = MATS[kind]
    sign = 1.0 if abs(matrix[7, 7] - matrix[0, 0]) < abs(matrix[7, 7] + matrix[0, 0]) else -1.0
    out = [None] * BX
    for e in range(BX // NP):
        part = [v[(e * NP + i) * BY : (e * NP + i + 1) * BY] for i in range(NP)]
        even = [part[j] + part[7 - j] for j in range(4)]
        odd = [part[j] - part[7 - j] for j in range(4)]
        for i in range(4):
            a = b = None
            for j in range(4):
                ca = float(0.5 * (matrix[i, j] + matrix[i, 7 - j]))
                cb = float(0.5 * (matrix[i, j] - matrix[i, 7 - j]))
                a = ca * even[j] if a is None else a + ca * even[j]
                b = cb * odd[j] if b is None else b + cb * odd[j]
            out[e * NP + i] = a + b
            out[e * NP + 7 - i] = a - b if sign > 0 else b - a
    return jnp.concatenate(out, axis=0)


def along_y(v, kind, tab, work):
    work[...] = v
    base = KIND[kind] * NP * NP
    columns = [tab[base + s * NP : base + (s + 1) * NP, :] for s in range(NP)]
    out = []
    for q in range(ROWS // NP):
        total = None
        for s in range(NP):
            part = columns[s] * work[NP * q + s : NP * q + s + 1, :]
            total = part if total is None else total + part
        out.append(total)
    return jnp.concatenate(out, axis=0)


def along_z(v, kind, zt):
    base = KIND[kind] * 2 * BZ
    vh = v.astype(BF16)
    vl = (v - vh.astype(F32)).astype(BF16)
    both = jnp.dot(
        jnp.concatenate([vh, vl], axis=1), zt[base : base + 2 * BZ, :], preferred_element_type=F32
    )
    return both[:, :BZ] + both[:, BZ:]


def bmass_of(tab):
    base = 3 * NP * NP
    yz = tab[base : base + BY, :]
    return jnp.concatenate([yz * float(WEIGHTS[x % NP]) for x in range(BX)], axis=0)


def local_sum_xy(v):
    parts = [v[x * BY : (x + 1) * BY] for x in range(BX)]
    for x in range(NP, BX, NP):
        both = parts[x - 1] + parts[x]
        parts[x - 1] = both
        parts[x] = both
    sub = lax.broadcasted_iota(jnp.int32, (NP, BZ), 0)
    out = []
    for x in range(BX):
        a, b = parts[x][:NP], parts[x][NP:]
        out.append(jnp.where(sub == NP - 1, a + pltpu.roll(b, NP - 1, 0), a))
        out.append(jnp.where(sub == 0, b + pltpu.roll(a, 1, 0), b))
    return jnp.concatenate(out, axis=0)


def local_sum_z(v):
    lane = lax.broadcasted_iota(jnp.int32, (NP, BZ), 1)
    last = (lane % NP == NP - 1) & (lane < BZ - 1)
    first = (lane % NP == 0) & (lane > 0)
    v3 = v.reshape(ROWS // NP, NP, BZ)
    up = pltpu.roll(v3, BZ - 1, 2)
    down = pltpu.roll(v3, 1, 2)
    v3 = v3 + jnp.where(last[None], up, jnp.where(first[None], down, 0.0))
    return v3.reshape(ROWS, BZ)


class Geometry:
    def __init__(self, sizes):
        self.sizes = sizes
        self.at = [lax.axis_index(a) for a in AXES]
        self.low = [g > 0 for g in self.at]
        self.high = [g < n - 1 for g, n in zip(self.at, sizes)]
        self.me = (self.at[0] * sizes[1] + self.at[1]) * sizes[2] + self.at[2]

    def neighbour(self, *step):
        ok = None
        number = self.me
        strides = (self.sizes[1] * self.sizes[2], self.sizes[2], 1)
        for a in range(3):
            if step[a]:
                there = self.high[a] if step[a] > 0 else self.low[a]
                ok = there if ok is None else jnp.logical_and(ok, there)
                number = number + step[a] * strides[a]
        return jnp.where(ok, number, self.me)

    def half(self, flag):
        return jnp.where(flag, 0.5, 1.0).astype(F32)

    def x_share(self, x):
        if x == 0:
            return self.half(self.low[0])
        if x == BX - 1:
            return self.half(self.high[0])
        return None

    def y_share(self):
        row = lax.broadcasted_iota(jnp.int32, (BY, BZ), 0)
        one = jnp.where(row == 0, self.half(self.low[1]), 1.0)
        return jnp.where(row == BY - 1, self.half(self.high[1]), one)

    def z_share(self, shape, dim):
        lane = lax.broadcasted_iota(jnp.int32, shape, dim)
        one = jnp.where(lane == 0, self.half(self.low[2]), 1.0)
        return jnp.where(lane == BZ - 1, self.half(self.high[2]), one)

    def yz_weight(self):
        row = lax.broadcasted_iota(jnp.int32, (BY, BZ), 0)
        lane = lax.broadcasted_iota(jnp.int32, (BY, BZ), 1)
        inside_y = ((row % NP == 0) & (row > 0)) | ((row % NP == NP - 1) & (row < BY - 1))
        inside_z = ((lane % NP == 0) & (lane > 0)) | ((lane % NP == NP - 1) & (lane < BZ - 1))
        wy = jnp.where(inside_y, 0.5, self.y_share())
        wz = jnp.where(inside_z, 0.5, self.z_share((BY, BZ), 1))
        return wy * wz

    def x_weight(self, x):
        if x in (0, BX - 1):
            return self.x_share(x)
        return 0.5 if x % NP in (0, NP - 1) else 1.0


def inverse_mass(geo, tab):
    base = 3 * NP * NP + BY
    yz = tab[base : base + BY, :] * geo.yz_weight()
    return jnp.concatenate(
        [yz * (geo.x_weight(x) * float(1.0 / WEIGHTS[x % NP])) for x in range(BX)], axis=0
    )


def face_steps(n):
    return ("swap",) if n == 2 else ("up", "down")


class Layout:
    def __init__(self, sizes):
        self.sizes = sizes
        self.devices = sizes[0] * sizes[1] * sizes[2]
        self.plain = self.devices
        self.offset = self.devices + 8
        self.lanes = -(-(self.offset + self.devices) // 128) * 128
        self.scalar_rows = self.lanes // 128

    def slot_rows(self, fields):
        need = self.scalar_rows + 2 * fields
        if fields == 2:
            need += self.scalar_rows
        return 4 if need <= 4 else -(-need // 8) * 8


def pick_faces(geo, axis, n, low, high):
    if n == 2:
        return [jnp.where(geo.at[axis] == 0, high, low)]
    return [high, low]


def tile_iota():
    return lax.broadcasted_iota(jnp.int32, (8, BZ), 0), lax.broadcasted_iota(jnp.int32, (8, BZ), 1)


def pack_z_faces(v, work):
    sub, lane = tile_iota()
    tile = None
    for q in range(ROWS // 8):
        part = pltpu.roll(v[8 * q : 8 * q + 8], (2 * q + 1) % BZ, 1)
        if tile is None:
            tile = part
        else:
            tile = jnp.where(lane >= 2 * q, part, tile)
    turns = (-1, 0, 1, 63, 64, 65)
    for i, a in enumerate(turns):
        work[8 * i : 8 * i + 8, :] = tile if a == 0 else pltpu.roll(tile, a % BZ, 1)
    line = lane[0:1]
    out = []
    for side in (1, 0):
        pair = []
        for r in range(2):
            total = None
            for g in range(4):
                e, h = g % 2, g // 2
                at = 8 * turns.index(e - side + 64 * h) + 4 * r + g
                part = work[at : at + 1, :]
                keep = (line % 2 == e) & (line // 64 == h)
                total = part if total is None else jnp.where(keep, part, total)
            pair.append(total)
        out.append(pair)
    return out


def unpack_z_faces(sides):
    sub, lane = tile_iota()
    low, high = [
        jnp.where(sub < 4, jnp.broadcast_to(s[0], (8, BZ)), jnp.broadcast_to(s[1], (8, BZ)))
        for s in sides
    ]
    tile = None
    for g in range(4):
        shift = g % 2 + 64 * (g // 2)
        a = high if shift == 0 else pltpu.roll(high, -shift % BZ, 1)
        b = low if shift == 1 else pltpu.roll(low, (1 - shift) % BZ, 1)
        part = jnp.where(lane % 2 == 0, a, b)
        tile = part if tile is None else jnp.where(sub % 4 == g, part, tile)
    return tile


def send_fields(geo, lay, f_refs, zs, work, scalars, send_ref, xs, ys, fields, extra=None):
    rows = lay.slot_rows(fields)
    base = [scalars[:, i * 128 : (i + 1) * 128] for i in range(lay.scalar_rows)]
    used = lay.scalar_rows
    if extra is not None:
        base.append(jnp.zeros((2 * fields, 128), F32))
        base += [extra[:, i * 128 : (i + 1) * 128] for i in range(lay.scalar_rows)]
        used += 2 * fields + lay.scalar_rows
    base.append(jnp.zeros((rows - used, 128), F32))
    base = jnp.concatenate([b for b in base if b.shape[0]], axis=0)
    send_ref[...] = jnp.broadcast_to(base[None], (lay.devices, rows, 128))
    for k, f_ref in enumerate(f_refs):
        at = lay.scalar_rows + 2 * k
        pairs = pack_z_faces(zs[k], work)
        for dz in (-1, 1):
            pair = pairs[0 if dz < 0 else 1]
            for dx in (-1, 0, 1):
                for dy in (-1, 0, 1):
                    there = geo.neighbour(dx, dy, dz)
                    send_ref[there, at : at + 1, :] = pair[0]
                    send_ref[there, at + 1 : at + 2, :] = pair[1]
        for dx in (-1, 1):
            for dy in (-1, 1):
                row = (BX - 1 if dx > 0 else 0) * BY + (BY - 1 if dy > 0 else 0)
                send_ref[geo.neighbour(dx, dy, 0), at : at + 1, :] = f_ref[row : row + 1, :]
        lowx, highx = f_ref[0:BY, :], f_ref[ROWS - BY : ROWS, :]
        for ref, face in zip(xs, pick_faces(geo, 0, lay.sizes[0], lowx, highx)):
            ref[k * BY : (k + 1) * BY, :] = face
        lowy = f_ref[pl.ds(0, BX, stride=BY), :]
        highy = f_ref[pl.ds(BY - 1, BX, stride=BY), :]
        for ref, face in zip(ys, pick_faces(geo, 1, lay.sizes[1], lowy, highy)):
            ref[k * BX : (k + 1) * BX, :] = face
    send_ref[geo.me] = base


def came_from(geo, axis, n, refs, k, size):
    if n == 2:
        face = refs[0][k * size : (k + 1) * size, :]
        return (
            jnp.where(geo.low[axis], face, 0.0),
            jnp.where(geo.high[axis], face, 0.0),
        )
    up = refs[0][k * size : (k + 1) * size, :]
    down = refs[1][k * size : (k + 1) * size, :]
    return jnp.where(geo.low[axis], up, 0.0), jnp.where(geo.high[axis], down, 0.0)


def received(geo, lay, f, recv_ref, xs, ys, w_ref, k):
    at = lay.scalar_rows + 2 * k
    line = lax.broadcasted_iota(jnp.int32, (1, BZ), 1)
    sides = []
    for dz in (-1, 1):
        pair = []
        for r in range(2):
            total = None
            for dy in (0, 1 if r else -1):
                for dx in (0, -1, 1):
                    source = 1 - r if dy else r
                    part = recv_ref[geo.neighbour(dx, dy, dz), at + source : at + source + 1, :]
                    keep = None
                    if dx:
                        keep = line % 64 >= 60 if dx > 0 else line % 64 < 4
                    if dy > 0:
                        want = (line >= 64) & (line % 4 == 3)
                        keep = want if keep is None else keep & want
                    if dy < 0:
                        want = (line < 64) & (line % 4 == 0)
                        keep = want if keep is None else keep & want
                    if keep is not None:
                        part = jnp.where(keep, pltpu.roll(part, (60 * dx + 67 * dy) % BZ, 1), 0.0)
                    total = part if total is None else total + part
            pair.append(total)
        sides.append(pair)
    tile = unpack_z_faces(sides)
    _, lane = tile_iota()
    ends = (lane == 0) | (lane == BZ - 1)
    parts = []
    for q in range(ROWS // 8):
        part = pltpu.roll(tile, (BZ - 1 - 2 * q) % BZ, 1)
        parts.append(f[8 * q : 8 * q + 8] + jnp.where(ends, part, 0.0))
    w_ref[...] = jnp.concatenate(parts, axis=0)
    lowx, highx = came_from(geo, 0, lay.sizes[0], xs, k, BY)
    w_ref[0:BY, :] += lowx
    w_ref[ROWS - BY : ROWS, :] += highx
    lowy, highy = came_from(geo, 1, lay.sizes[1], ys, k, BX)
    w_ref[pl.ds(0, BX, stride=BY), :] += lowy
    w_ref[pl.ds(BY - 1, BX, stride=BY), :] += highy
    for dx in (-1, 1):
        for dy in (-1, 1):
            row = (BX - 1 if dx > 0 else 0) * BY + (BY - 1 if dy > 0 else 0)
            w_ref[row : row + 1, :] += recv_ref[geo.neighbour(dx, dy, 0), at : at + 1, :]


def received_scalars(lay, recv_ref):
    total = jnp.sum(recv_ref[...], axis=0)
    return jnp.concatenate([total[i : i + 1] for i in range(lay.scalar_rows)], axis=1)


def coarse_tables(geo, lay, places):
    out = []
    for half in range(2):
        size = 32 if half else 16
        row = lax.broadcasted_iota(jnp.int32, (size, lay.lanes), 0)
        steps = [
            jnp.broadcast_to(places[3 * half + a : 3 * half + a + 1, :], row.shape)
            - geo.at[a].astype(F32)
            for a in range(3)
        ]
        if half:
            row_dx = jnp.where(row < 24, row // 8 - 1, (row - 24) // 2 - 1)
            row_dy = jnp.where(row < 24, 0, row % 2 * 2 - 1)
            row_dx = jnp.where(row < 30, row_dx, 1000)
        else:
            row_dx, row_dy = row // 3 - 1, row % 3 - 1
            row_dx = jnp.where(row < 9, row_dx, 1000)
        near = (steps[0] == row_dx.astype(F32)) & (steps[1] == row_dy.astype(F32))
        for dz in (-1.0, 0.0, 1.0):
            out.append(jnp.where(near & (steps[2] == dz), 1.0, 0.0))
    row = lax.broadcasted_iota(jnp.int32, (24, lay.lanes), 0)
    lane = lax.broadcasted_iota(jnp.int32, (24, lay.lanes), 1)
    out.append(jnp.where(lane == lay.plain + row // 8, 1.0, 0.0))
    return jnp.concatenate(out, axis=0)


HOT_ROWS = 48 + 96 + 24


def partial_sums(geo, v, sums, q_ref, hot_ref):
    first, last = v[0:BY], v[ROWS - BY : ROWS]
    middle = first * geo.x_share(0) + last * geo.x_share(BX - 1)
    for x in range(1, BX - 1):
        middle = middle + v[x * BY : (x + 1) * BY]
    share = geo.y_share()
    for i, part in enumerate((0.5 * first, middle, 0.5 * last)):
        shared = part * share
        q_ref[8 * i : 8 * i + 8, :] = shared[0:8] + shared[8:16]
        q_ref[24 + 2 * i : 25 + 2 * i, :] = 0.5 * part[0:1]
        q_ref[25 + 2 * i : 26 + 2 * i, :] = 0.5 * part[BY - 1 : BY]
    q_ref[30:32, :] = jnp.zeros((2, BZ), F32)
    q = q_ref[...]
    own = jnp.sum(q * geo.z_share(q.shape, 1), axis=1, keepdims=True)
    below, above = 0.5 * q[:, 0:1], 0.5 * q[:, BZ - 1 : BZ]
    rows = hot_ref[48:80, :] * below + hot_ref[80:112, :] * own + hot_ref[112:144, :] * above
    rows = rows[0:8] + rows[8:16] + rows[16:24] + rows[24:32]
    for i, total in enumerate(sums):
        at = 144 + 8 * i
        rows = rows + hot_ref[at : at + 8, :] * jnp.sum(total, axis=1, keepdims=True)
    return jnp.sum(rows, axis=0, keepdims=True)


def spread(geo, values, hot_ref):
    below, own, above = [
        jnp.sum(hot_ref[16 * i : 16 * i + 16, :] * values, axis=1, keepdims=True) for i in range(3)
    ]
    lane = lax.broadcasted_iota(jnp.int32, (16, BZ), 1)
    rows = own * geo.z_share((16, BZ), 1)
    rows = rows + jnp.where(lane == 0, 0.5 * below, 0.0)
    rows = rows + jnp.where(lane == BZ - 1, 0.5 * above, 0.0)
    y = lax.broadcasted_iota(jnp.int32, (BY, BZ), 0)
    share = geo.y_share()
    planes = []
    for i in range(3):
        plane = share * rows[3 * i + 1 : 3 * i + 2]
        plane = plane + jnp.where(y == 0, 0.5 * rows[3 * i : 3 * i + 1], 0.0)
        planes.append(plane + jnp.where(y == BY - 1, 0.5 * rows[3 * i + 2 : 3 * i + 3], 0.0))
    out = [planes[1]] * BX
    out[0] = planes[1] * geo.x_share(0) + 0.5 * planes[0]
    out[BX - 1] = planes[1] * geo.x_share(BX - 1) + 0.5 * planes[2]
    return out


def with_coarse(lay, row, gram_ref):
    return row + jnp.dot(row, gram_ref[...], precision=HIGHEST, preferred_element_type=F32)


def coarse_inner(lay, row):
    lane = lax.broadcasted_iota(jnp.int32, row.shape, 1)
    both = row * pltpu.roll(row, lay.offset, 1)
    return jnp.sum(jnp.where(lane >= lay.offset, both, 0.0), axis=1, keepdims=True)


def all_rows(v):
    total = v[0:8]
    for i in range(1, ROWS // 8):
        total = total + v[8 * i : 8 * i + 8]
    return total


def weighted_rows(geo, v):
    yz = geo.yz_weight()
    total = None
    for x in range(BX):
        weight = geo.x_weight(x)
        part = v[x * BY : (x + 1) * BY]
        if not (isinstance(weight, float) and weight == 1.0):
            part = part * weight
        total = part if total is None else total + part
    total = total * yz
    return total[0:8] + total[8:16]


def weak_form(level, tab, zt, work):
    gx, gy, gz = along_x(level, "d"), along_y(level, "d", tab, work.at[0]), along_z(level, "d", zt)
    inv_norm = lax.rsqrt(1.0 + gx * gx + gy * gy + gz * gz)
    coef = bmass_of(tab) * (level * (1.0 - level) * inv_norm - INTERFACE_WIDTH)
    out = along_x(coef * gx, "t") + along_y(coef * gy, "t", tab, work.at[1])
    return out + along_z(coef * gz, "t", zt)


def stiffness(v, scaled, tab, zt, work):
    out = bmass_of(tab) * v
    out = out + along_x(scaled * along_x(v, "d"), "t")
    out = out + along_y(scaled * along_y(v, "d", tab, work.at[0]), "t", tab, work.at[1])
    return out + along_z(scaled * along_z(v, "d", zt), "t", zt)


def local_step(geo, lay, residual, dinv, scaled, state, p_old, refs):
    tab, zt, hot, u_ref, f_ref, send_ref, xs, ys, q_ref, state_ref, work, zwork, final = refs
    s_row, ts_row, gamma, curvature = state
    jacobi = residual * dinv
    planes = spread(geo, s_row, hot)
    u = jnp.concatenate([jacobi[x * BY : (x + 1) * BY] + planes[x] for x in range(BX)], axis=0)
    u_ref[...] = u
    local = stiffness(u, scaled, tab, zt, work)
    sums = [weighted_rows(geo, residual * jacobi), all_rows(u * local)]
    if p_old is not None:
        sums.append(all_rows(p_old * local))
    scalars = partial_sums(geo, local, sums, q_ref, hot)
    ones = jnp.ones_like(s_row)
    coarse = coarse_inner(lay, s_row)
    state_ref[...] = jnp.concatenate(
        [s_row, ts_row, ones * gamma, ones * curvature, ones * coarse, jnp.zeros((3, lay.lanes), F32)],
        axis=0,
    )
    if final:
        rows = [scalars[:, i * 128 : (i + 1) * 128] for i in range(lay.scalar_rows)]
        rows = jnp.concatenate(rows, axis=0)
        send_ref[...] = jnp.broadcast_to(rows[None], send_ref.shape)
        return
    local = local_sum_xy(local)
    f_ref[...] = local_sum_z(local)
    send_fields(geo, lay, [f_ref], [local], zwork, scalars, send_ref, xs, ys, 1)


def step_sizes(lay, recv_ref, state_ref, first):
    row = received_scalars(lay, recv_ref)
    lane = lax.broadcasted_iota(jnp.int32, row.shape, 1)

    def pick(which):
        return jnp.sum(jnp.where(lane == lay.plain + which, row, 0.0), axis=1, keepdims=True)

    gamma = pick(0) + state_ref[4:5, 0:1]
    if first:
        curvature = pick(1)
        beta = None
    else:
        beta = gamma / state_ref[2:3, 0:1]
        curvature = pick(1) + beta * (2.0 * pick(2) + beta * state_ref[3:4, 0:1])
    return row, gamma, curvature, beta, gamma / curvature


def build(mesh):
    sizes = tuple(int(mesh.shape[a]) for a in AXES)
    lay = Layout(sizes)
    steps = [face_steps(sizes[0]), face_steps(sizes[1])]
    nx, ny = len(steps[0]), len(steps[1])
    tab_np, zt_np = const_tables(), z_tables()
    number = np.arange(lay.lanes)
    places_np = np.full((8, lay.lanes), -9.0, np.float32)
    for half in range(2):
        lanes = slice(half * lay.offset, half * lay.offset + lay.devices)
        for a, place in enumerate(np.unravel_index(np.arange(lay.devices), sizes)):
            places_np[3 * half + a, lanes] = place
    block = jax.ShapeDtypeStruct((ROWS, BZ), F32)

    def like(*shape):
        return jax.ShapeDtypeStruct(shape, F32)

    def outgoing(fields):
        return (
            [like(lay.devices, lay.slot_rows(fields), 128)]
            + [like(BY * fields, BZ)] * nx
            + [like(BX * fields, BZ)] * ny
        )

    def call(kernel, ins, outs, scratch, name, space=pltpu.VMEM, limit=48):
        spec = pl.BlockSpec(memory_space=pltpu.VMEM)
        if space == pltpu.HBM:
            ins = [pltpu.with_memory_space_constraint(v, pltpu.HBM) for v in ins]
        return pl.pallas_call(
            kernel,
            out_shape=outs,
            in_specs=[pl.BlockSpec(memory_space=space)] * len(ins),
            out_specs=[spec] * len(outs),
            scratch_shapes=scratch,
            compiler_params=pltpu.CompilerParams(vmem_limit_bytes=limit * 1024 * 1024),
            name=name,
        )(*ins)

    work = pltpu.VMEM((ROWS, BZ), F32)
    qrows = pltpu.VMEM((32, BZ), F32)
    pair = pltpu.VMEM((2, ROWS, BZ), F32)
    tiles = pltpu.VMEM((48, BZ), F32)

    def ring(v, axis, n, step):
        if step == "swap":
            pairs = [(0, 1), (1, 0)]
        else:
            d = 1 if step == "up" else n - 1
            pairs = [(i, (i + d) % n) for i in range(n)]
        return lax.ppermute(v, axis, pairs)

    def exchange(out):
        send, faces = out[0], out[1:]
        recv = lax.all_to_all(send, AXES, 0, 0, tiled=True)
        xs = [ring(faces[i], "gx", sizes[0], s) for i, s in enumerate(steps[0])]
        ys = [ring(faces[nx + i], "gy", sizes[1], s) for i, s in enumerate(steps[1])]
        return [recv, *xs, *ys]

    n_out = 1 + nx + ny

    def split(refs):
        return refs[0], refs[1 : 1 + nx], refs[1 + nx : 1 + nx + ny]

    def start_kernel(level_any, vel_any, source_any, factor_any, tab_any, zt_any, places_any, *rest):
        send, xs, ys = split(rest[:n_out])
        fa_ref, fd_ref, hot_ref, q_ref, work, zwork = rest[n_out : n_out + 6]
        buffers, sems = rest[n_out + 6 : -1], rest[-1]
        sources = (level_any, zt_any, tab_any, vel_any, source_any, places_any, factor_any)
        copies = [
            pltpu.make_async_copy(source, target, sems.at[i])
            for i, (source, target) in enumerate(zip(sources, buffers))
        ]
        for copy in copies:
            copy.start()
        for copy in copies:
            copy.wait()
        level_ref, zt_ref, tab_ref, vel_ref, source_ref, places_ref, factor_ref = buffers
        geo = Geometry(sizes)
        level = level_ref[...]
        bm = bmass_of(tab_ref)
        advect = vel_ref[0] * along_x(level, "d")
        advect = advect + vel_ref[1] * along_y(level, "d", tab_ref, work.at[0])
        advect = advect + vel_ref[2] * along_z(level, "d", zt_ref)
        advect = local_sum_xy(bm * advect)
        fa_ref[...] = local_sum_z(advect)
        div = bm * source_ref[...] + along_x(bm * vel_ref[0], "t")
        div = div + along_y(bm * vel_ref[1], "t", tab_ref, work.at[1])
        div = div + along_z(bm * vel_ref[2], "t", zt_ref)
        hot_ref[...] = coarse_tables(geo, lay, places_ref)
        scalars = partial_sums(geo, div, [], q_ref, hot_ref)
        div = local_sum_xy(div)
        fd_ref[...] = local_sum_z(div)
        factor = factor_ref[...]
        if lay.lanes > lay.devices:
            pad = jnp.zeros((1, lay.lanes - lay.devices), F32)
            factor = jnp.concatenate([factor, pad], axis=1)
        send_fields(
            geo, lay, [fa_ref, fd_ref], [advect, div], zwork, scalars, send, xs, ys, 2, factor
        )

    def finish(geo, v, f_ref, zwork, send, xs, ys):
        v = local_sum_xy(v)
        f_ref[...] = local_sum_z(v)
        nothing = jnp.zeros((1, lay.lanes), F32)
        send_fields(geo, lay, [f_ref], [v], zwork, nothing, send, xs, ys, 1)

    def first_kernel(recv, *rest):
        xs, ys = rest[:nx], rest[nx : nx + ny]
        level_ref, fa_ref, fd_ref, tab_ref, zt_ref, hot_ref = rest[nx + ny : nx + ny + 6]
        out = rest[nx + ny + 6 :]
        send, oxs, oys = split(out[:n_out])
        level_out, f_ref, r_ref, s_ref, hot_out, w_ref, work, zwork, gram_ref = out[n_out:]
        geo = Geometry(sizes)
        at = lay.scalar_rows + 4
        factor = [recv[:, at + i, :] for i in range(lay.scalar_rows)]
        factor = jnp.concatenate(factor, axis=1)
        after = lay.lanes - lay.offset - lay.devices
        shifted = [jnp.zeros((lay.offset, lay.lanes), F32), factor]
        if after:
            shifted.append(jnp.zeros((after, lay.lanes), F32))
        plain = [factor, jnp.zeros((lay.lanes - lay.devices, lay.lanes), F32)]
        gram_ref[...] = lax.dot_general(
            jnp.concatenate(shifted, axis=0),
            jnp.concatenate(plain, axis=0),
            (((1,), (1,)), ((), ())),
            precision=HIGHEST,
            preferred_element_type=F32,
        )
        received(geo, lay, fd_ref[...], recv, xs, ys, w_ref, 1)
        r_ref[...] = SOURCE_SCALE * w_ref[...]
        row = received_scalars(lay, recv)
        row = with_coarse(lay, SOURCE_SCALE * row, gram_ref)
        s_ref[...] = jnp.broadcast_to(row, s_ref.shape)
        hot_out[...] = hot_ref[...]
        hot_out[48:144, :] = with_coarse(lay, hot_ref[48:144, :], gram_ref)
        received(geo, lay, fa_ref[...], recv, xs, ys, w_ref, 0)
        level = level_ref[...] - TIME_STEP * w_ref[...] * inverse_mass(geo, tab_ref)
        level_out[...] = level
        finish(geo, weak_form(level, tab_ref, zt_ref, work), f_ref, zwork, send, oxs, oys)

    def new_level(geo, recv, xs, ys, level_ref, f_ref, tab_ref, w_ref):
        received(geo, lay, f_ref[...], recv, xs, ys, w_ref, 0)
        return level_ref[...] + PSEUDO_STEP * w_ref[...] * inverse_mass(geo, tab_ref)

    def sweep_kernel(recv, *rest):
        xs, ys = rest[:nx], rest[nx : nx + ny]
        level_ref, fin_ref, tab_ref, zt_ref = rest[nx + ny : nx + ny + 4]
        out = rest[nx + ny + 4 :]
        send, oxs, oys = split(out[:n_out])
        level_out, f_ref, w_ref, work, zwork = out[n_out:]
        geo = Geometry(sizes)
        level = new_level(geo, recv, xs, ys, level_ref, fin_ref, tab_ref, w_ref)
        level_out[...] = level
        finish(geo, weak_form(level, tab_ref, zt_ref, work), f_ref, zwork, send, oxs, oys)

    def diagonal_kernel(recv, *rest):
        xs, ys = rest[:nx], rest[nx : nx + ny]
        level_ref, fin_ref, tab_ref, zt_ref = rest[nx + ny : nx + ny + 4]
        out = rest[nx + ny + 4 :]
        send, oxs, oys = split(out[:n_out])
        level_out, f_ref, scaled_ref, w_ref, work, zwork = out[n_out:]
        geo = Geometry(sizes)
        level = new_level(geo, recv, xs, ys, level_ref, fin_ref, tab_ref, w_ref)
        level_out[...] = level
        bm = bmass_of(tab_ref)
        scaled = bm / (GAS_DENSITY + (1.0 - GAS_DENSITY) * jnp.clip(level, 0.0, 1.0))
        scaled_ref[...] = scaled
        diag = bm + along_x(scaled, "s") + along_y(scaled, "s", tab_ref, work.at[0])
        diag = diag + along_z(scaled, "s", zt_ref)
        finish(geo, diag, f_ref, zwork, send, oxs, oys)

    def solve_kernel(recv, *rest):
        xs, ys = rest[:nx], rest[nx : nx + ny]
        fin_ref, r_ref, scaled_ref, s_ref, tab_ref, zt_ref, hot_ref = rest[nx + ny : nx + ny + 7]
        out = rest[nx + ny + 7 :]
        send, oxs, oys = split(out[:n_out])
        dinv_ref, u_ref, f_ref, state_ref, w_ref, work, zwork, q_ref = out[n_out:]
        geo = Geometry(sizes)
        received(geo, lay, fin_ref[...], recv, xs, ys, w_ref, 0)
        dinv = 1.0 / w_ref[...]
        dinv_ref[...] = dinv
        zero = jnp.zeros((1, 1), F32)
        s_row = s_ref[0:1, :]
        state = (s_row, jnp.zeros_like(s_row), zero, zero)
        refs = (tab_ref, zt_ref, hot_ref, u_ref, f_ref, send, oxs, oys)
        local_step(
            geo, lay, r_ref[...], dinv, scaled_ref[...], state, None, (*refs, q_ref, state_ref, work, zwork, False)
        )

    def make_iterate(first, final):
        def iterate_kernel(recv, *rest):
            xs, ys = rest[:nx], rest[nx : nx + ny]
            n_in = 9 + (0 if first else 3)
            ins = rest[nx + ny : nx + ny + n_in]
            fin_ref, r_ref, u_in, dinv_ref, scaled_ref, state_in = ins[:6]
            tab_ref, zt_ref, hot_ref = ins[6:9]
            p_in, si_in, x_in = (None, None, None) if first else ins[9:12]
            out = rest[nx + ny + n_in :]
            if final:
                send, oxs, oys = out[0], (), ()
                out = out[1:]
                u_ref, state_ref, p_ref, x_ref, w_ref, work, zwork, q_ref = out
                f_ref = r_out = si_ref = None
            else:
                send, oxs, oys = split(out[:n_out])
                u_ref, state_ref, p_ref, x_ref, r_out, si_ref, f_ref, w_ref, work, zwork, q_ref = out[
                    n_out:
                ]
            geo = Geometry(sizes)
            row, gamma, curvature, beta, alpha = step_sizes(lay, recv, state_in, first)
            received(geo, lay, fin_ref[...], recv, xs, ys, w_ref, 0)
            image = w_ref[...]
            p = u_in[...]
            s_row, ts_row = state_in[0:1, :], row
            if not first:
                p = p + beta * p_in[...]
                image = image + beta * si_in[...]
                ts_row = ts_row + beta * state_in[1:2, :]
            p_ref[...] = p
            x_ref[...] = alpha * p if first else x_in[...] + alpha * p
            residual = r_ref[...] - alpha * image
            if not final:
                si_ref[...] = image
                r_out[...] = residual
            lane = lax.broadcasted_iota(jnp.int32, row.shape, 1)
            ts_row = jnp.where((lane < lay.devices) | (lane >= lay.offset), ts_row, 0.0)
            state = (s_row - alpha * ts_row, ts_row, gamma, curvature)
            refs = (tab_ref, zt_ref, hot_ref, u_ref, f_ref, send)
            local_step(
                geo,
                lay,
                residual,
                dinv_ref[...],
                scaled_ref[...],
                state,
                p,
                (*refs, oxs, oys, q_ref, state_ref, work, zwork, final),
            )

        return iterate_kernel

    def last_kernel(recv, state_in, u_in, p_in, x_in, out_ref):
        _, _, _, beta, alpha = step_sizes(lay, recv, state_in, False)
        out_ref[...] = x_in[...] + alpha * (u_in[...] + beta * p_in[...])

    def body(level_set, velocity, source, coarse_factor):
        level = level_set.reshape(ROWS, BZ)
        vel = velocity.reshape(3, ROWS, BZ)
        src = source.reshape(ROWS, BZ)
        tab, zt, places = jnp.asarray(tab_np), jnp.asarray(zt_np), jnp.asarray(places_np)
        out = call(
            start_kernel,
            [level, vel, src, coarse_factor, tab, zt, places],
            outgoing(2) + [block, block, like(HOT_ROWS, lay.lanes)],
            [qrows, pair, tiles]
            + [pltpu.VMEM(a.shape, a.dtype) for a in (level, zt, tab, vel, src, places, coarse_factor)]
            + [pltpu.SemaphoreType.DMA((7,))],
            "advect",
            pltpu.HBM,
        )
        fa, fd, hot = out[n_out:]
        got = exchange(out[:n_out])
        out = call(
            first_kernel,
            [*got, level, fa, fd, tab, zt, hot],
            outgoing(1) + [block, block, block, like(8, lay.lanes), like(HOT_ROWS, lay.lanes)],
            [work, pair, tiles, pltpu.VMEM((lay.lanes, lay.lanes), F32)],
            "sweep_first",
        )
        level, f, residual, s_rows, hot = out[n_out:]
        for _ in range(RSWEEPS - 1):
            got = exchange(out[:n_out])
            out = call(
                sweep_kernel, [*got, level, f, tab, zt], outgoing(1) + [block, block], [work, pair, tiles], "sweep"
            )
            level, f = out[n_out:]
        got = exchange(out[:n_out])
        out = call(
            diagonal_kernel,
            [*got, level, f, tab, zt],
            outgoing(1) + [block, block, block],
            [work, pair, tiles],
            "diagonal",
        )
        level, f, scaled = out[n_out:]
        got = exchange(out[:n_out])
        out = call(
            solve_kernel,
            [*got, f, residual, scaled, s_rows, tab, zt, hot],
            outgoing(1) + [block, block, block, like(8, lay.lanes)],
            [work, pair, tiles, qrows],
            "solve_start",
        )
        dinv, u, f, state = out[n_out:]
        p = image = x = None
        for step in range(ITERS - 1):
            first, final = step == 0, step == ITERS - 2
            got = exchange(out[:n_out])
            ins = [*got, f, residual, u, dinv, scaled, state, tab, zt, hot]
            if not first:
                ins += [p, image, x]
            fields = [block, like(8, lay.lanes), block, block]
            if final:
                outs = [like(lay.devices, lay.scalar_rows, 128)] + fields
            else:
                outs = outgoing(1) + fields + [block, block, block]
            out = call(make_iterate(first, final), ins, outs, [work, pair, tiles, qrows], "iterate")
            if final:
                u, state, p, x = out[1:]
            else:
                u, state, p, x, residual, image, f = out[n_out:]
        recv = lax.all_to_all(out[0], AXES, 0, 0, tiled=True)
        (x,) = call(last_kernel, [recv, state, u, p, x], [block], [], "pressure")
        return level.reshape(BX, BY, BZ), x.reshape(BX, BY, BZ)

    return body


def solution(mesh):
    in_specs = (
        P("gx", "gy", "gz"),
        P(None, "gx", "gy", "gz"),
        P("gx", "gy", "gz"),
        P(("gx", "gy", "gz"), None),
    )
    out_specs = (P("gx", "gy", "gz"), P("gx", "gy", "gz"))
    return jax.shard_map(
        build(mesh), mesh=mesh, in_specs=in_specs, out_specs=out_specs, check_vma=False
    )
```

```python
import jax
import jax.numpy as jnp
import ml_dtypes
import numpy as np
from jax import lax
from jax.experimental import pallas as pl
from jax.experimental.pallas import tpu as pltpu
from jax.sharding import PartitionSpec as P

NP = 8
RSWEEPS = 2
ITERS = 6
AXES = ("gx", "gy", "gz")

GLL_POINTS = (
    -1.0,
    -0.8717401485096066,
    -0.5917001814331423,
    -0.2092992179024789,
    0.2092992179024789,
    0.5917001814331423,
    0.8717401485096066,
    1.0,
)
GLL_WEIGHTS = (
    0.03571428571428571,
    0.21070422714350603,
    0.3411226924835044,
    0.4124587946587038,
    0.4124587946587038,
    0.3411226924835044,
    0.21070422714350603,
    0.03571428571428571,
)
HIGHEST = lax.Precision.HIGHEST
TIME_STEP = 0.02
PSEUDO_STEP = 0.004
INTERFACE_WIDTH = 0.5
GAS_DENSITY = 0.1
SOURCE_SCALE = 20.0
F32 = jnp.float32
BF16 = jnp.bfloat16


def node_tables():
    points = np.array(GLL_POINTS)
    amount = points.shape[0]
    barycentric = np.ones(amount)
    for target in range(amount):
        for partner in range(amount):
            if partner != target:
                barycentric[target] = barycentric[target] / (points[target] - points[partner])
    derivative = np.zeros((amount, amount))
    for target in range(amount):
        for partner in range(amount):
            if partner != target:
                derivative[target, partner] = (
                    barycentric[partner] / barycentric[target] / (points[target] - points[partner])
                )
        derivative[target, target] = -np.sum(derivative[target])
    return derivative


DERIV = node_tables()
TRANS = DERIV.T.copy()
SQUARE = (DERIV * DERIV).T.copy()
WEIGHTS = np.array(GLL_WEIGHTS)

BX, BY, BZ = 16, 16, 128
ROWS = BX * BY


def split_bf16(matrix):
    full = matrix.astype(np.float32)
    high = full.astype(ml_dtypes.bfloat16)
    low = (full - high.astype(np.float32)).astype(ml_dtypes.bfloat16)
    return high, low


def const_tables():
    parts = []
    for matrix in (DERIV, TRANS, SQUARE):
        for column in matrix.T:
            parts.append(np.repeat(column[:, None], BZ, axis=1))
    wy = np.tile(WEIGHTS, BY // NP)
    wz = np.tile(WEIGHTS, BZ // NP)
    parts.append(wy[:, None] * wz[None, :])
    parts.append(1.0 / (wy[:, None] * wz[None, :]))
    return np.concatenate(parts, axis=0).astype(np.float32)


def z_tables():
    out = []
    for matrix in (DERIV, TRANS, SQUARE):
        high, low = split_bf16(np.kron(np.eye(BZ // NP), matrix.T))
        top = np.concatenate([high, low], axis=1)
        out += [top, np.concatenate([high, np.zeros_like(low)], axis=1)]
    return np.concatenate(out, axis=0)


KIND = {"d": 0, "t": 1, "s": 2}
MATS = {"d": DERIV, "t": TRANS, "s": SQUARE}


def along_x(v, kind):
    matrix = MATS[kind]
    sign = 1.0 if abs(matrix[7, 7] - matrix[0, 0]) < abs(matrix[7, 7] + matrix[0, 0]) else -1.0
    out = [None] * BX
    for e in range(BX // NP):
        part = [v[(e * NP + i) * BY : (e * NP + i + 1) * BY] for i in range(NP)]
        even = [part[j] + part[7 - j] for j in range(4)]
        odd = [part[j] - part[7 - j] for j in range(4)]
        for i in range(4):
            a = b = None
            for j in range(4):
                ca = float(0.5 * (matrix[i, j] + matrix[i, 7 - j]))
                cb = float(0.5 * (matrix[i, j] - matrix[i, 7 - j]))
                a = ca * even[j] if a is None else a + ca * even[j]
                b = cb * odd[j] if b is None else b + cb * odd[j]
            out[e * NP + i] = a + b
            out[e * NP + 7 - i] = a - b if sign > 0 else b - a
    return jnp.concatenate(out, axis=0)


def along_y(v, kind, tab, work):
    work[...] = v
    base = KIND[kind] * NP * NP
    columns = [tab[base + s * NP : base + (s + 1) * NP, :] for s in range(NP)]
    out = []
    for q in range(ROWS // NP):
        total = None
        for s in range(NP):
            part = columns[s] * work[NP * q + s : NP * q + s + 1, :]
            total = part if total is None else total + part
        out.append(total)
    return jnp.concatenate(out, axis=0)


def along_z(v, kind, zt):
    base = KIND[kind] * 2 * BZ
    vh = v.astype(BF16)
    vl = (v - vh.astype(F32)).astype(BF16)
    both = jnp.dot(
        jnp.concatenate([vh, vl], axis=1), zt[base : base + 2 * BZ, :], preferred_element_type=F32
    )
    return both[:, :BZ] + both[:, BZ:]


def bmass_of(tab):
    base = 3 * NP * NP
    yz = tab[base : base + BY, :]
    return jnp.concatenate([yz * float(WEIGHTS[x % NP]) for x in range(BX)], axis=0)


def local_sum_xy(v):
    parts = [v[x * BY : (x + 1) * BY] for x in range(BX)]
    for x in range(NP, BX, NP):
        both = parts[x - 1] + parts[x]
        parts[x - 1] = both
        parts[x] = both
    sub = lax.broadcasted_iota(jnp.int32, (NP, BZ), 0)
    out = []
    for x in range(BX):
        a, b = parts[x][:NP], parts[x][NP:]
        out.append(jnp.where(sub == NP - 1, a + pltpu.roll(b, NP - 1, 0), a))
        out.append(jnp.where(sub == 0, b + pltpu.roll(a, 1, 0), b))
    return jnp.concatenate(out, axis=0)


def local_sum_z(v):
    lane = lax.broadcasted_iota(jnp.int32, (NP, BZ), 1)
    last = (lane % NP == NP - 1) & (lane < BZ - 1)
    first = (lane % NP == 0) & (lane > 0)
    swap = jnp.where(last, lane + 1, jnp.where(first, lane - 1, lane))
    out = []
    for q in range(v.shape[0] // NP):
        part = v[NP * q : NP * q + NP]
        other = jnp.take_along_axis(part, swap, axis=1, mode="promise_in_bounds")
        out.append(part + jnp.where(last | first, other, 0.0))
    return jnp.concatenate(out, axis=0)


def tree(parts):
    while len(parts) > 1:
        rest = parts[len(parts) // 2 * 2 :]
        parts = [a + b for a, b in zip(parts[0::2], parts[1::2])] + rest
    return parts[0]


class Geometry:
    def __init__(self, sizes):
        self.sizes = sizes
        self.at = [lax.axis_index(a) for a in AXES]
        self.low = [g > 0 for g in self.at]
        self.high = [g < n - 1 for g, n in zip(self.at, sizes)]
        self.me = (self.at[0] * sizes[1] + self.at[1]) * sizes[2] + self.at[2]

    def neighbour(self, *step):
        ok = None
        number = self.me
        strides = (self.sizes[1] * self.sizes[2], self.sizes[2], 1)
        for a in range(3):
            if step[a]:
                there = self.high[a] if step[a] > 0 else self.low[a]
                ok = there if ok is None else jnp.logical_and(ok, there)
                number = number + step[a] * strides[a]
        return jnp.where(ok, number, self.me)

    def half(self, flag):
        return jnp.where(flag, 0.5, 1.0).astype(F32)

    def x_share(self, x):
        if x == 0:
            return self.half(self.low[0])
        if x == BX - 1:
            return self.half(self.high[0])
        return None

    def y_share(self):
        row = lax.broadcasted_iota(jnp.int32, (BY, BZ), 0)
        one = jnp.where(row == 0, self.half(self.low[1]), 1.0)
        return jnp.where(row == BY - 1, self.half(self.high[1]), one)

    def z_share(self, shape, dim):
        lane = lax.broadcasted_iota(jnp.int32, shape, dim)
        one = jnp.where(lane == 0, self.half(self.low[2]), 1.0)
        return jnp.where(lane == BZ - 1, self.half(self.high[2]), one)

    def yz_weight(self):
        row = lax.broadcasted_iota(jnp.int32, (BY, BZ), 0)
        lane = lax.broadcasted_iota(jnp.int32, (BY, BZ), 1)
        inside_y = ((row % NP == 0) & (row > 0)) | ((row % NP == NP - 1) & (row < BY - 1))
        inside_z = ((lane % NP == 0) & (lane > 0)) | ((lane % NP == NP - 1) & (lane < BZ - 1))
        wy = jnp.where(inside_y, 0.5, self.y_share())
        wz = jnp.where(inside_z, 0.5, self.z_share((BY, BZ), 1))
        return wy * wz

    def x_weight(self, x):
        if x in (0, BX - 1):
            return self.x_share(x)
        return 0.5 if x % NP in (0, NP - 1) else 1.0


def inverse_mass(geo, tab):
    base = 3 * NP * NP + BY
    yz = tab[base : base + BY, :] * geo.yz_weight()
    return jnp.concatenate(
        [yz * (geo.x_weight(x) * float(1.0 / WEIGHTS[x % NP])) for x in range(BX)], axis=0
    )


def face_steps(n):
    return ("swap",) if n == 2 else ("up", "down")


class Layout:
    def __init__(self, sizes):
        self.sizes = sizes
        self.devices = sizes[0] * sizes[1] * sizes[2]
        self.plain = self.devices
        self.offset = self.devices + 8
        self.lanes = -(-(self.offset + self.devices) // 128) * 128
        self.scalar_rows = self.lanes // 128

    def slot_rows(self, fields):
        need = self.scalar_rows + 2 * fields
        if fields == 2:
            need += self.scalar_rows
        return 4 if need <= 4 else -(-need // 8) * 8


def pick_faces(geo, axis, n, low, high):
    if n == 2:
        return [jnp.where(geo.at[axis] == 0, high, low)]
    return [high, low]


def tile_iota():
    return lax.broadcasted_iota(jnp.int32, (8, BZ), 0), lax.broadcasted_iota(jnp.int32, (8, BZ), 1)


def pack_z_faces(v, work):
    sub, lane = tile_iota()
    parts = [pltpu.roll(v[8 * q : 8 * q + 8], (2 * q + 1) % BZ, 1) for q in range(ROWS // 8)]
    width = 2
    while len(parts) > 1:
        pairs = zip(parts[0::2], parts[1::2])
        parts = [jnp.where(lane & width == 0, a, b) for a, b in pairs]
        width *= 2
    tile = parts[0]
    turns = (-1, 0, 1, 63, 64, 65)
    for i, a in enumerate(turns):
        work[8 * i : 8 * i + 8, :] = tile if a == 0 else pltpu.roll(tile, a % BZ, 1)
    line = lane[0:1]
    out = []
    for side in (1, 0):
        pair = []
        for r in range(2):
            total = None
            for g in range(4):
                e, h = g % 2, g // 2
                at = 8 * turns.index(e - side + 64 * h) + 4 * r + g
                part = work[at : at + 1, :]
                keep = (line % 2 == e) & (line // 64 == h)
                total = part if total is None else jnp.where(keep, part, total)
            pair.append(total)
        out.append(pair)
    return out


def unpack_z_faces(sides):
    sub, lane = tile_iota()
    low, high = [
        jnp.where(sub < 4, jnp.broadcast_to(s[0], (8, BZ)), jnp.broadcast_to(s[1], (8, BZ)))
        for s in sides
    ]
    tile = None
    for g in range(4):
        shift = g % 2 + 64 * (g // 2)
        a = high if shift == 0 else pltpu.roll(high, -shift % BZ, 1)
        b = low if shift == 1 else pltpu.roll(low, (1 - shift) % BZ, 1)
        part = jnp.where(lane % 2 == 0, a, b)
        tile = part if tile is None else jnp.where(sub % 4 == g, part, tile)
    return tile


def send_fields(geo, lay, f_ref, z, work, scalars, send_ref, xs, ys, fields=1, extra=None):
    rows = lay.slot_rows(fields)
    base = [scalars[:, i * 128 : (i + 1) * 128] for i in range(lay.scalar_rows)]
    used = lay.scalar_rows
    if extra is not None:
        base.append(jnp.zeros((2 * fields, 128), F32))
        base += [extra[:, i * 128 : (i + 1) * 128] for i in range(lay.scalar_rows)]
        used += 2 * fields + lay.scalar_rows
    base.append(jnp.zeros((rows - used, 128), F32))
    base = jnp.concatenate([b for b in base if b.shape[0]], axis=0)
    send_ref[...] = jnp.broadcast_to(base[None], (lay.devices, rows, 128))
    fill_field(geo, lay, f_ref, z, work, send_ref, fields - 1)
    fill_faces(geo, lay, f_ref, xs, ys)
    send_ref[geo.me] = base


def fill_field(geo, lay, f_ref, z, work, send_ref, k):
    at = lay.scalar_rows + 2 * k
    pairs = pack_z_faces(z, work)
    for dz in (-1, 1):
        pair = pairs[0 if dz < 0 else 1]
        for dx in (-1, 0, 1):
            for dy in (-1, 0, 1):
                there = geo.neighbour(dx, dy, dz)
                send_ref[there, at : at + 1, :] = pair[0]
                send_ref[there, at + 1 : at + 2, :] = pair[1]
    for dx in (-1, 1):
        for dy in (-1, 1):
            row = (BX - 1 if dx > 0 else 0) * BY + (BY - 1 if dy > 0 else 0)
            send_ref[geo.neighbour(dx, dy, 0), at : at + 1, :] = f_ref[row : row + 1, :]


def fill_faces(geo, lay, f_ref, xs, ys):
    lowx, highx = f_ref[0:BY, :], f_ref[ROWS - BY : ROWS, :]
    for ref, face in zip(xs, pick_faces(geo, 0, lay.sizes[0], lowx, highx)):
        ref[0:BY, :] = face
    lowy = f_ref[pl.ds(0, BX, stride=BY), :]
    highy = f_ref[pl.ds(BY - 1, BX, stride=BY), :]
    for ref, face in zip(ys, pick_faces(geo, 1, lay.sizes[1], lowy, highy)):
        ref[0:BX, :] = face


def came_from(geo, axis, n, refs, k, size):
    if n == 2:
        face = refs[0][k * size : (k + 1) * size, :]
        return (
            jnp.where(geo.low[axis], face, 0.0),
            jnp.where(geo.high[axis], face, 0.0),
        )
    up = refs[0][k * size : (k + 1) * size, :]
    down = refs[1][k * size : (k + 1) * size, :]
    return jnp.where(geo.low[axis], up, 0.0), jnp.where(geo.high[axis], down, 0.0)


def received(geo, lay, f, recv_ref, xs, ys, w_ref, k):
    at = lay.scalar_rows + 2 * k
    line = lax.broadcasted_iota(jnp.int32, (1, BZ), 1)
    sides = []
    for dz in (-1, 1):
        pair = []
        for r in range(2):
            total = None
            for dy in (0, 1 if r else -1):
                for dx in (0, -1, 1):
                    source = 1 - r if dy else r
                    part = recv_ref[geo.neighbour(dx, dy, dz), at + source : at + source + 1, :]
                    keep = None
                    if dx:
                        keep = line % 64 >= 60 if dx > 0 else line % 64 < 4
                    if dy > 0:
                        want = (line >= 64) & (line % 4 == 3)
                        keep = want if keep is None else keep & want
                    if dy < 0:
                        want = (line < 64) & (line % 4 == 0)
                        keep = want if keep is None else keep & want
                    if keep is not None:
                        part = jnp.where(keep, pltpu.roll(part, (60 * dx + 67 * dy) % BZ, 1), 0.0)
                    total = part if total is None else total + part
            pair.append(total)
        sides.append(pair)
    tile = unpack_z_faces(sides)
    _, lane = tile_iota()
    ends = (lane == 0) | (lane == BZ - 1)
    parts = []
    for q in range(ROWS // 8):
        part = pltpu.roll(tile, (BZ - 1 - 2 * q) % BZ, 1)
        parts.append(f[8 * q : 8 * q + 8] + jnp.where(ends, part, 0.0))
    w_ref[...] = jnp.concatenate(parts, axis=0)
    lowx, highx = came_from(geo, 0, lay.sizes[0], xs, k, BY)
    w_ref[0:BY, :] += lowx
    w_ref[ROWS - BY : ROWS, :] += highx
    lowy, highy = came_from(geo, 1, lay.sizes[1], ys, k, BX)
    w_ref[pl.ds(0, BX, stride=BY), :] += lowy
    w_ref[pl.ds(BY - 1, BX, stride=BY), :] += highy
    for dx in (-1, 1):
        for dy in (-1, 1):
            row = (BX - 1 if dx > 0 else 0) * BY + (BY - 1 if dy > 0 else 0)
            w_ref[row : row + 1, :] += recv_ref[geo.neighbour(dx, dy, 0), at : at + 1, :]


def received_scalars(lay, recv_ref):
    total = recv_ref[...]
    while total.shape[0] % 2 == 0:
        half = total.shape[0] // 2
        total = total[:half] + total[half:]
    total = jnp.sum(total, axis=0)
    return jnp.concatenate([total[i : i + 1] for i in range(lay.scalar_rows)], axis=1)


def coarse_tables(geo, lay, places):
    out = []
    for half in range(2):
        size = 32 if half else 16
        row = lax.broadcasted_iota(jnp.int32, (size, lay.lanes), 0)
        steps = [
            jnp.broadcast_to(places[3 * half + a : 3 * half + a + 1, :], row.shape)
            - geo.at[a].astype(F32)
            for a in range(3)
        ]
        if half:
            row_dx = jnp.where(row < 24, row // 8 - 1, (row - 24) // 2 - 1)
            row_dy = jnp.where(row < 24, 0, row % 2 * 2 - 1)
            row_dx = jnp.where(row < 30, row_dx, 1000)
        else:
            row_dx, row_dy = row // 3 - 1, row % 3 - 1
            row_dx = jnp.where(row < 9, row_dx, 1000)
        near = (steps[0] == row_dx.astype(F32)) & (steps[1] == row_dy.astype(F32))
        for dz in (-1.0, 0.0, 1.0):
            out.append(jnp.where(near & (steps[2] == dz), 1.0, 0.0))
    row = lax.broadcasted_iota(jnp.int32, (24, lay.lanes), 0)
    lane = lax.broadcasted_iota(jnp.int32, (24, lay.lanes), 1)
    out.append(jnp.where(lane == lay.plain + row // 8, 1.0, 0.0))
    return jnp.concatenate(out, axis=0)


HOT_ROWS = 48 + 96 + 24


def partial_sums(geo, v, sums, q_ref, hot_ref):
    first, last = v[0:BY], v[ROWS - BY : ROWS]
    inner = [v[x * BY : (x + 1) * BY] for x in range(1, BX - 1)]
    middle = tree([first * geo.x_share(0), last * geo.x_share(BX - 1), *inner])
    share = geo.y_share()
    for i, part in enumerate((0.5 * first, middle, 0.5 * last)):
        shared = part * share
        q_ref[8 * i : 8 * i + 8, :] = shared[0:8] + shared[8:16]
        q_ref[24 + 2 * i : 25 + 2 * i, :] = 0.5 * part[0:1]
        q_ref[25 + 2 * i : 26 + 2 * i, :] = 0.5 * part[BY - 1 : BY]
    q_ref[30:32, :] = jnp.zeros((2, BZ), F32)
    q = q_ref[...]
    own = jnp.sum(q * geo.z_share(q.shape, 1), axis=1, keepdims=True)
    below, above = 0.5 * q[:, 0:1], 0.5 * q[:, BZ - 1 : BZ]
    rows = hot_ref[48:80, :] * below + hot_ref[80:112, :] * own + hot_ref[112:144, :] * above
    rows = rows[0:8] + rows[8:16] + rows[16:24] + rows[24:32]
    if sums:
        rows = rows + plain_sums(sums, hot_ref)
    return jnp.sum(rows, axis=0, keepdims=True)


def plain_sums(sums, hot_ref):
    parts = []
    for i, total in enumerate(sums):
        at = 144 + 8 * i
        parts.append(hot_ref[at : at + 8, :] * jnp.sum(total, axis=1, keepdims=True))
    return tree(parts)


def spread(geo, values, hot_ref):
    below, own, above = [
        jnp.sum(hot_ref[16 * i : 16 * i + 16, :] * values, axis=1, keepdims=True) for i in range(3)
    ]
    lane = lax.broadcasted_iota(jnp.int32, (16, BZ), 1)
    rows = own * geo.z_share((16, BZ), 1)
    rows = rows + jnp.where(lane == 0, 0.5 * below, 0.0)
    rows = rows + jnp.where(lane == BZ - 1, 0.5 * above, 0.0)
    y = lax.broadcasted_iota(jnp.int32, (BY, BZ), 0)
    share = geo.y_share()
    planes = []
    for i in range(3):
        plane = share * rows[3 * i + 1 : 3 * i + 2]
        plane = plane + jnp.where(y == 0, 0.5 * rows[3 * i : 3 * i + 1], 0.0)
        planes.append(plane + jnp.where(y == BY - 1, 0.5 * rows[3 * i + 2 : 3 * i + 3], 0.0))
    out = [planes[1]] * BX
    out[0] = planes[1] * geo.x_share(0) + 0.5 * planes[0]
    out[BX - 1] = planes[1] * geo.x_share(BX - 1) + 0.5 * planes[2]
    return out


def with_coarse(lay, row, gram_ref):
    return row + jnp.dot(row, gram_ref[...], precision=HIGHEST, preferred_element_type=F32)


def coarse_inner(lay, row):
    lane = lax.broadcasted_iota(jnp.int32, row.shape, 1)
    both = row * pltpu.roll(row, lay.offset, 1)
    return jnp.sum(jnp.where(lane >= lay.offset, both, 0.0), axis=1, keepdims=True)


def all_rows(v):
    return tree([v[8 * i : 8 * i + 8] for i in range(ROWS // 8)])


def weighted_rows(geo, v):
    yz = geo.yz_weight()
    parts = []
    for x in range(BX):
        weight = geo.x_weight(x)
        part = v[x * BY : (x + 1) * BY]
        if not (isinstance(weight, float) and weight == 1.0):
            part = part * weight
        parts.append(part)
    total = tree(parts)
    total = total * yz
    return total[0:8] + total[8:16]


def weak_form(level, tab, zt, work):
    gx, gy, gz = along_x(level, "d"), along_y(level, "d", tab, work.at[0]), along_z(level, "d", zt)
    inv_norm = lax.rsqrt(1.0 + gx * gx + gy * gy + gz * gz)
    coef = bmass_of(tab) * (level * (1.0 - level) * inv_norm - INTERFACE_WIDTH)
    out = along_x(coef * gx, "t") + along_y(coef * gy, "t", tab, work.at[1])
    return out + along_z(coef * gz, "t", zt)


def stiffness(v, scaled, tab, zt, work, final):
    bm = bmass_of(tab)
    gx, gy, gz = along_x(v, "d"), along_y(v, "d", tab, work.at[0]), along_z(v, "d", zt)
    tx, ty, tz = scaled * gx, scaled * gy, scaled * gz
    energy = all_rows(bm * v * v + (tx * gx + ty * gy + tz * gz))
    if final:
        return None, energy
    out = bm * v + along_x(tx, "t") + along_y(ty, "t", tab, work.at[1])
    return out + along_z(tz, "t", zt), energy


def local_step(geo, lay, residual, dinv, scaled, state, image, refs):
    tab, zt, hot, u_ref, f_ref, send_ref, xs, ys, q_ref, state_ref, work, zwork, final = refs
    s_row, ts_row, gamma, curvature = state
    jacobi = residual * dinv
    planes = spread(geo, s_row, hot)
    u = jnp.concatenate([jacobi[x * BY : (x + 1) * BY] + planes[x] for x in range(BX)], axis=0)
    u_ref[...] = u
    local, energy = stiffness(u, scaled, tab, zt, work, final)
    sums = [weighted_rows(geo, residual * jacobi), energy]
    if image is not None:
        sums.append(weighted_rows(geo, u * image))
    ones = jnp.ones_like(s_row)
    coarse = coarse_inner(lay, s_row)
    state_ref[...] = jnp.concatenate(
        [s_row, ts_row, ones * gamma, ones * curvature, ones * coarse, jnp.zeros((3, lay.lanes), F32)],
        axis=0,
    )
    if final:
        scalars = jnp.sum(plain_sums(sums, hot), axis=0, keepdims=True)
        rows = [scalars[:, i * 128 : (i + 1) * 128] for i in range(lay.scalar_rows)]
        rows = jnp.concatenate(rows, axis=0)
        send_ref[...] = jnp.broadcast_to(rows[None], send_ref.shape)
        return
    scalars = partial_sums(geo, local, sums, q_ref, hot)
    local = local_sum_xy(local)
    f_ref[...] = local_sum_z(local)
    send_fields(geo, lay, f_ref, local, zwork, scalars, send_ref, xs, ys)


def step_sizes(lay, recv_ref, state_ref, first):
    row = received_scalars(lay, recv_ref)
    lane = lax.broadcasted_iota(jnp.int32, row.shape, 1)

    def pick(which):
        return jnp.sum(jnp.where(lane == lay.plain + which, row, 0.0), axis=1, keepdims=True)

    gamma = pick(0) + state_ref[4:5, 0:1]
    if first:
        curvature = pick(1)
        beta = None
    else:
        beta = gamma / state_ref[2:3, 0:1]
        curvature = pick(1) + beta * (2.0 * pick(2) + beta * state_ref[3:4, 0:1])
    return row, gamma, curvature, beta, gamma / curvature


def build(mesh):
    sizes = tuple(int(mesh.shape[a]) for a in AXES)
    lay = Layout(sizes)
    steps = [face_steps(sizes[0]), face_steps(sizes[1])]
    nx, ny = len(steps[0]), len(steps[1])
    tab_np, zt_np = const_tables(), z_tables()
    number = np.arange(lay.lanes)
    places_np = np.full((8, lay.lanes), -9.0, np.float32)
    for half in range(2):
        lanes = slice(half * lay.offset, half * lay.offset + lay.devices)
        for a, place in enumerate(np.unravel_index(np.arange(lay.devices), sizes)):
            places_np[3 * half + a, lanes] = place
    block = jax.ShapeDtypeStruct((ROWS, BZ), F32)

    def like(*shape):
        return jax.ShapeDtypeStruct(shape, F32)

    def outgoing(fields):
        return (
            [like(lay.devices, lay.slot_rows(fields), 128)]
            + [like(BY * fields, BZ)] * nx
            + [like(BX * fields, BZ)] * ny
        )

    def call(kernel, ins, outs, scratch, name, from_hbm=()):
        spec = pl.BlockSpec(memory_space=pltpu.VMEM)
        hbm = pl.BlockSpec(memory_space=pltpu.HBM)
        ins = [pltpu.with_memory_space_constraint(v, pltpu.HBM) if i in from_hbm else v for i, v in enumerate(ins)]
        return pl.pallas_call(
            kernel,
            out_shape=outs,
            in_specs=[hbm if i in from_hbm else spec for i in range(len(ins))],
            out_specs=[spec] * len(outs),
            scratch_shapes=scratch,
            compiler_params=pltpu.CompilerParams(vmem_limit_bytes=48 * 1024 * 1024),
            cost_estimate=pl.CostEstimate(flops=4000000, bytes_accessed=1000000, transcendentals=0),
            name=name,
        )(*ins)

    work = pltpu.VMEM((ROWS, BZ), F32)
    qrows = pltpu.VMEM((32, BZ), F32)
    pair = pltpu.VMEM((2, ROWS, BZ), F32)
    tiles = pltpu.VMEM((48, BZ), F32)

    def ring(v, axis, n, step):
        if step == "swap":
            pairs = [(0, 1), (1, 0)]
        else:
            d = 1 if step == "up" else n - 1
            pairs = [(i, (i + d) % n) for i in range(n)]
        return lax.ppermute(v, axis, pairs)

    def exchange(out):
        send, faces = out[0], out[1:]
        recv = lax.all_to_all(send, AXES, 0, 0, tiled=True)
        xs = [ring(faces[i], "gx", sizes[0], s) for i, s in enumerate(steps[0])]
        ys = [ring(faces[nx + i], "gy", sizes[1], s) for i, s in enumerate(steps[1])]
        return [recv, *xs, *ys]

    n_out = 1 + nx + ny

    def split(refs):
        return refs[0], refs[1 : 1 + nx], refs[1 + nx : 1 + nx + ny]

    def start_kernel(level_any, vel_any, tab_any, zt_any, *rest):
        send, xs, ys = split(rest[:n_out])
        f_ref, work, zwork = rest[n_out : n_out + 3]
        level_ref, zt_ref, tab_ref, vel_ref, sems = rest[n_out + 3 :]
        sources = (level_any, zt_any.at[0 : 2 * BZ], tab_any, vel_any)
        copies = [
            pltpu.make_async_copy(source, target, sems.at[i])
            for i, (source, target) in enumerate(zip(sources, (level_ref, zt_ref, tab_ref, vel_ref)))
        ]
        for copy in copies:
            copy.start()
        for copy in copies[:3]:
            copy.wait()
        geo = Geometry(sizes)
        level = level_ref[...]
        gx, gy, gz = along_x(level, "d"), along_y(level, "d", tab_ref, work.at[0]), along_z(level, "d", zt_ref)
        copies[3].wait()
        advect = bmass_of(tab_ref) * (vel_ref[0] * gx + vel_ref[1] * gy + vel_ref[2] * gz)
        finish(geo, advect, f_ref, zwork, send, xs, ys)

    def finish(geo, v, f_ref, zwork, send, xs, ys):
        v = local_sum_xy(v)
        f_ref[...] = local_sum_z(v)
        nothing = jnp.zeros((1, lay.lanes), F32)
        send_fields(geo, lay, f_ref, v, zwork, nothing, send, xs, ys)

    def source_kernel(vel_ref, source_ref, factor_ref, tab_ref, zt_ref, places_ref, _, *rest):
        slots, xs, ys = split(rest[:n_out])
        f_ref, hot_ref, q_ref, work, zwork = rest[n_out:]
        geo = Geometry(sizes)
        bm = bmass_of(tab_ref)
        div = bm * source_ref[...] + along_x(bm * vel_ref[0], "t")
        div = div + along_y(bm * vel_ref[1], "t", tab_ref, work.at[1])
        div = div + along_z(bm * vel_ref[2], "t", zt_ref)
        hot_ref[...] = coarse_tables(geo, lay, places_ref)
        scalars = partial_sums(geo, div, [], q_ref, hot_ref)
        div = local_sum_xy(div)
        f_ref[...] = local_sum_z(div)
        factor = factor_ref[...]
        if lay.lanes > lay.devices:
            pad = jnp.zeros((1, lay.lanes - lay.devices), F32)
            factor = jnp.concatenate([factor, pad], axis=1)
        send_fields(geo, lay, f_ref, div, zwork, scalars, slots, xs, ys, 2, factor)

    def first_kernel(recv, *rest):
        xs, ys = rest[:nx], rest[nx : nx + ny]
        level_ref, fa_ref, tab_ref, zt_ref = rest[nx + ny : nx + ny + 4]
        slots, sxs, sys = split(rest[nx + ny + 4 : nx + ny + 4 + n_out])
        out = rest[nx + ny + 4 + n_out :]
        send, oxs, oys = split(out[:n_out])
        level_out, f_ref, w_ref, work, zwork = out[n_out:]
        geo = Geometry(sizes)
        received(geo, lay, fa_ref[...], recv, xs, ys, w_ref, 0)
        level = level_ref[...] - TIME_STEP * w_ref[...] * inverse_mass(geo, tab_ref)
        level_out[...] = level
        v = local_sum_xy(weak_form(level, tab_ref, zt_ref, work))
        f_ref[...] = local_sum_z(v)
        send[...] = slots[...]
        fill_field(geo, lay, f_ref, v, zwork, send, 0)
        send[geo.me] = slots[geo.me]
        fill_faces(geo, lay, f_ref, oxs, oys)
        for to, part in zip((*oxs, *oys), (*sxs, *sys)):
            to[BY : 2 * BY, :] = part[...]

    def rhs_kernel(recv, *rest):
        xs, ys = rest[:nx], rest[nx : nx + ny]
        fd_ref, hot_ref, r_ref, s_ref, hot_out, w_ref, gram_ref = rest[nx + ny :]
        geo = Geometry(sizes)
        at = lay.scalar_rows + 4
        factor = [recv[:, at + i, :] for i in range(lay.scalar_rows)]
        factor = jnp.concatenate(factor, axis=1)
        after = lay.lanes - lay.offset - lay.devices
        shifted = [jnp.zeros((lay.offset, lay.lanes), F32), factor]
        if after:
            shifted.append(jnp.zeros((after, lay.lanes), F32))
        plain = [factor, jnp.zeros((lay.lanes - lay.devices, lay.lanes), F32)]
        gram_ref[...] = lax.dot_general(
            jnp.concatenate(shifted, axis=0),
            jnp.concatenate(plain, axis=0),
            (((1,), (1,)), ((), ())),
            precision=HIGHEST,
            preferred_element_type=F32,
        )
        received(geo, lay, fd_ref[...], recv, xs, ys, w_ref, 1)
        r_ref[...] = SOURCE_SCALE * w_ref[...]
        row = with_coarse(lay, SOURCE_SCALE * received_scalars(lay, recv), gram_ref)
        s_ref[...] = jnp.broadcast_to(row, s_ref.shape)
        hot_out[...] = hot_ref[...]
        hot_out[48:144, :] = with_coarse(lay, hot_ref[48:144, :], gram_ref)

    def new_level(geo, recv, xs, ys, level_ref, f_ref, tab_ref, w_ref):
        received(geo, lay, f_ref[...], recv, xs, ys, w_ref, 0)
        return level_ref[...] + PSEUDO_STEP * w_ref[...] * inverse_mass(geo, tab_ref)

    def sweep_kernel(recv, *rest):
        xs, ys = rest[:nx], rest[nx : nx + ny]
        level_ref, fin_ref, tab_ref, zt_ref = rest[nx + ny : nx + ny + 4]
        out = rest[nx + ny + 4 :]
        send, oxs, oys = split(out[:n_out])
        level_out, f_ref, w_ref, work, zwork = out[n_out:]
        geo = Geometry(sizes)
        level = new_level(geo, recv, xs, ys, level_ref, fin_ref, tab_ref, w_ref)
        level_out[...] = level
        finish(geo, weak_form(level, tab_ref, zt_ref, work), f_ref, zwork, send, oxs, oys)

    def diagonal_kernel(recv, *rest):
        xs, ys = rest[:nx], rest[nx : nx + ny]
        level_ref, fin_ref, tab_ref, zt_ref = rest[nx + ny : nx + ny + 4]
        out = rest[nx + ny + 4 :]
        send, oxs, oys = split(out[:n_out])
        level_out, f_ref, scaled_ref, w_ref, work, zwork = out[n_out:]
        geo = Geometry(sizes)
        level = new_level(geo, recv, xs, ys, level_ref, fin_ref, tab_ref, w_ref)
        level_out[...] = level
        bm = bmass_of(tab_ref)
        scaled = bm / (GAS_DENSITY + (1.0 - GAS_DENSITY) * jnp.clip(level, 0.0, 1.0))
        scaled_ref[...] = scaled
        diag = bm + along_x(scaled, "s") + along_y(scaled, "s", tab_ref, work.at[0])
        diag = diag + along_z(scaled, "s", zt_ref)
        finish(geo, diag, f_ref, zwork, send, oxs, oys)

    def solve_kernel(recv, *rest):
        xs, ys = rest[:nx], rest[nx : nx + ny]
        fin_ref, r_ref, scaled_ref, s_ref, tab_ref, zt_ref, hot_ref = rest[nx + ny : nx + ny + 7]
        out = rest[nx + ny + 7 :]
        send, oxs, oys = split(out[:n_out])
        dinv_ref, u_ref, f_ref, state_ref, w_ref, work, zwork, q_ref = out[n_out:]
        geo = Geometry(sizes)
        received(geo, lay, fin_ref[...], recv, xs, ys, w_ref, 0)
        dinv = 1.0 / w_ref[...]
        dinv_ref[...] = dinv
        zero = jnp.zeros((1, 1), F32)
        s_row = s_ref[0:1, :]
        state = (s_row, jnp.zeros_like(s_row), zero, zero)
        refs = (tab_ref, zt_ref, hot_ref, u_ref, f_ref, send, oxs, oys)
        local_step(
            geo, lay, r_ref[...], dinv, scaled_ref[...], state, None, (*refs, q_ref, state_ref, work, zwork, False)
        )

    def make_iterate(first, final):
        def iterate_kernel(recv, *rest):
            xs, ys = rest[:nx], rest[nx : nx + ny]
            n_in = 9 + (0 if first else 3)
            ins = rest[nx + ny : nx + ny + n_in]
            fin_ref, r_ref, u_in, dinv_ref, scaled_ref, state_in = ins[:6]
            tab_ref, zt_ref, hot_ref = ins[6:9]
            p_in, si_in, x_in = (None, None, None) if first else ins[9:12]
            out = rest[nx + ny + n_in :]
            if final:
                send, oxs, oys = out[0], (), ()
                out = out[1:]
                u_ref, state_ref, p_ref, x_ref, w_ref, work, zwork, q_ref = out
                f_ref = r_out = si_ref = None
            else:
                send, oxs, oys = split(out[:n_out])
                u_ref, state_ref, p_ref, x_ref, r_out, si_ref, f_ref, w_ref, work, zwork, q_ref = out[
                    n_out:
                ]
            geo = Geometry(sizes)
            row, gamma, curvature, beta, alpha = step_sizes(lay, recv, state_in, first)
            received(geo, lay, fin_ref[...], recv, xs, ys, w_ref, 0)
            image = w_ref[...]
            p = u_in[...]
            s_row, ts_row = state_in[0:1, :], row
            if not first:
                p = p + beta * p_in[...]
                image = image + beta * si_in[...]
                ts_row = ts_row + beta * state_in[1:2, :]
            p_ref[...] = p
            x_ref[...] = alpha * p if first else x_in[...] + alpha * p
            residual = r_ref[...] - alpha * image
            if not final:
                si_ref[...] = image
                r_out[...] = residual
            lane = lax.broadcasted_iota(jnp.int32, row.shape, 1)
            ts_row = jnp.where((lane < lay.devices) | (lane >= lay.offset), ts_row, 0.0)
            state = (s_row - alpha * ts_row, ts_row, gamma, curvature)
            refs = (tab_ref, zt_ref, hot_ref, u_ref, f_ref, send)
            local_step(
                geo,
                lay,
                residual,
                dinv_ref[...],
                scaled_ref[...],
                state,
                image,
                (*refs, oxs, oys, q_ref, state_ref, work, zwork, final),
            )

        return iterate_kernel

    def last_kernel(recv, state_in, u_in, p_in, x_in, out_ref):
        _, _, _, beta, alpha = step_sizes(lay, recv, state_in, False)
        out_ref[...] = x_in[...] + alpha * (u_in[...] + beta * p_in[...])

    def body(level_set, velocity, source, coarse_factor):
        level = level_set.reshape(ROWS, BZ)
        vel = velocity.reshape(3, ROWS, BZ)
        src = source.reshape(ROWS, BZ)
        tab, zt, places = jnp.asarray(tab_np), jnp.asarray(zt_np), jnp.asarray(places_np)
        out = call(
            start_kernel,
            [level, vel, tab, zt],
            outgoing(1) + [block],
            [pair, tiles]
            + [pltpu.VMEM(a, d) for a, d in ((level.shape, F32), ((2 * BZ, 2 * BZ), BF16), (tab.shape, F32), (vel.shape, F32))]
            + [pltpu.SemaphoreType.DMA((4,))],
            "advect",
            range(4),
        )
        fa = out[n_out]
        got = exchange(out[:n_out])
        side = call(
            source_kernel,
            [vel, src, coarse_factor, tab, zt, places, fa],
            [like(lay.devices, lay.slot_rows(2), 128), *outgoing(1)[1:], block, like(HOT_ROWS, lay.lanes)],
            [qrows, pair, tiles],
            "source",
        )
        fd, hot = side[n_out:]
        out = call(
            first_kernel,
            [*got, level, fa, tab, zt, *side[:n_out]],
            outgoing(2) + [block, block],
            [work, pair, tiles],
            "sweep_first",
        )
        level, f = out[n_out:]
        got = exchange(out[:n_out])
        residual, s_rows, hot = call(
            rhs_kernel,
            [*got, fd, hot],
            [block, like(8, lay.lanes), like(HOT_ROWS, lay.lanes)],
            [work, pltpu.VMEM((lay.lanes, lay.lanes), F32)],
            "rhs",
        )
        for _ in range(RSWEEPS - 1):
            out = call(
                sweep_kernel, [*got, level, f, tab, zt], outgoing(1) + [block, block], [work, pair, tiles], "sweep"
            )
            level, f = out[n_out:]
            got = exchange(out[:n_out])
        out = call(
            diagonal_kernel,
            [*got, level, f, tab, zt],
            outgoing(1) + [block, block, block],
            [work, pair, tiles],
            "diagonal",
        )
        level, f, scaled = out[n_out:]
        got = exchange(out[:n_out])
        out = call(
            solve_kernel,
            [*got, f, residual, scaled, s_rows, tab, zt, hot],
            outgoing(1) + [block, block, block, like(8, lay.lanes)],
            [work, pair, tiles, qrows],
            "solve_start",
        )
        dinv, u, f, state = out[n_out:]
        p = image = x = None
        for step in range(ITERS - 1):
            first, final = step == 0, step == ITERS - 2
            got = exchange(out[:n_out])
            ins = [*got, f, residual, u, dinv, scaled, state, tab, zt, hot]
            if not first:
                ins += [p, image, x]
            fields = [block, like(8, lay.lanes), block, block]
            if final:
                outs = [like(lay.devices, lay.scalar_rows, 128)] + fields
            else:
                outs = outgoing(1) + fields + [block, block, block]
            out = call(make_iterate(first, final), ins, outs, [work, pair, tiles, qrows], "iterate")
            if final:
                u, state, p, x = out[1:]
            else:
                u, state, p, x, residual, image, f = out[n_out:]
        recv = lax.all_to_all(out[0], AXES, 0, 0, tiled=True)
        (x,) = call(last_kernel, [recv, state, u, p, x], [block], [], "pressure")
        return level.reshape(BX, BY, BZ), x.reshape(BX, BY, BZ)

    return body


def solution(mesh):
    in_specs = (
        P("gx", "gy", "gz"),
        P(None, "gx", "gy", "gz"),
        P("gx", "gy", "gz"),
        P(("gx", "gy", "gz"), None),
    )
    out_specs = (P("gx", "gy", "gz"), P("gx", "gy", "gz"))
    return jax.shard_map(
        build(mesh), mesh=mesh, in_specs=in_specs, out_specs=out_specs, check_vma=False
    )
```

```python
import jax
import jax.numpy as jnp
import ml_dtypes
import numpy as np
from jax import lax
from jax.experimental import pallas as pl
from jax.experimental.pallas import tpu as pltpu
from jax.sharding import PartitionSpec as P

NP = 8
ITERS = 6
AXES = ("gx", "gy", "gz")

GLL_POINTS = (
    -1.0,
    -0.8717401485096066,
    -0.5917001814331423,
    -0.2092992179024789,
    0.2092992179024789,
    0.5917001814331423,
    0.8717401485096066,
    1.0,
)
GLL_WEIGHTS = (
    0.03571428571428571,
    0.21070422714350603,
    0.3411226924835044,
    0.4124587946587038,
    0.4124587946587038,
    0.3411226924835044,
    0.21070422714350603,
    0.03571428571428571,
)
HIGHEST = lax.Precision.HIGHEST
TIME_STEP = 0.02
PSEUDO_STEP = 0.004
INTERFACE_WIDTH = 0.5
GAS_DENSITY = 0.1
SOURCE_SCALE = 20.0
F32 = jnp.float32
BF16 = jnp.bfloat16


def node_tables():
    points = np.array(GLL_POINTS)
    amount = points.shape[0]
    barycentric = np.ones(amount)
    for target in range(amount):
        for partner in range(amount):
            if partner != target:
                barycentric[target] = barycentric[target] / (points[target] - points[partner])
    derivative = np.zeros((amount, amount))
    for target in range(amount):
        for partner in range(amount):
            if partner != target:
                derivative[target, partner] = (
                    barycentric[partner] / barycentric[target] / (points[target] - points[partner])
                )
        derivative[target, target] = -np.sum(derivative[target])
    return derivative


DERIV = node_tables()
TRANS = DERIV.T.copy()
SQUARE = (DERIV * DERIV).T.copy()
WEIGHTS = np.array(GLL_WEIGHTS)

BX, BY, BZ = 16, 16, 128
ROWS = BX * BY


def split_bf16(matrix):
    full = matrix.astype(np.float32)
    high = full.astype(ml_dtypes.bfloat16)
    low = (full - high.astype(np.float32)).astype(ml_dtypes.bfloat16)
    return high, low


def const_tables():
    parts = []
    for matrix in (DERIV, TRANS, SQUARE):
        for column in matrix.T:
            parts.append(np.repeat(column[:, None], BZ, axis=1))
    wy = np.tile(WEIGHTS, BY // NP)
    wz = np.tile(WEIGHTS, BZ // NP)
    parts.append(wy[:, None] * wz[None, :])
    parts.append(1.0 / (wy[:, None] * wz[None, :]))
    return np.concatenate(parts, axis=0).astype(np.float32)


def z_tables():
    out = []
    for matrix in (DERIV, TRANS, SQUARE):
        high, low = split_bf16(np.kron(np.eye(BZ // NP), matrix.T))
        top = np.concatenate([high, low], axis=1)
        out += [top, np.concatenate([high, np.zeros_like(low)], axis=1)]
    return np.concatenate(out, axis=0)


KIND = {"d": 0, "t": 1, "s": 2}
MATS = {"d": DERIV, "t": TRANS, "s": SQUARE}


def along_x(v, kind):
    matrix = MATS[kind]
    sign = 1.0 if abs(matrix[7, 7] - matrix[0, 0]) < abs(matrix[7, 7] + matrix[0, 0]) else -1.0
    out = [None] * BX
    for e in range(BX // NP):
        part = [v[(e * NP + i) * BY : (e * NP + i + 1) * BY] for i in range(NP)]
        even = [part[j] + part[7 - j] for j in range(4)]
        odd = [part[j] - part[7 - j] for j in range(4)]
        for i in range(4):
            a = b = None
            for j in range(4):
                ca = float(0.5 * (matrix[i, j] + matrix[i, 7 - j]))
                cb = float(0.5 * (matrix[i, j] - matrix[i, 7 - j]))
                a = ca * even[j] if a is None else a + ca * even[j]
                b = cb * odd[j] if b is None else b + cb * odd[j]
            out[e * NP + i] = a + b
            out[e * NP + 7 - i] = a - b if sign > 0 else b - a
    return jnp.concatenate(out, axis=0)


def along_y(v, kind, tab, work):
    work[...] = v
    base = KIND[kind] * NP * NP
    columns = [tab[base + s * NP : base + (s + 1) * NP, :] for s in range(NP)]
    out = []
    for q in range(ROWS // NP):
        total = None
        for s in range(NP):
            part = columns[s] * work[NP * q + s : NP * q + s + 1, :]
            total = part if total is None else total + part
        out.append(total)
    return jnp.concatenate(out, axis=0)


def along_z(v, kind, zt):
    base = KIND[kind] * 2 * BZ
    vh = v.astype(BF16)
    vl = (v - vh.astype(F32)).astype(BF16)
    both = jnp.dot(
        jnp.concatenate([vh, vl], axis=1), zt[base : base + 2 * BZ, :], preferred_element_type=F32
    )
    return both[:, :BZ] + both[:, BZ:]


def bmass_of(tab):
    base = 3 * NP * NP
    yz = tab[base : base + BY, :]
    return jnp.concatenate([yz * float(WEIGHTS[x % NP]) for x in range(BX)], axis=0)


def local_sum_xy(v):
    parts = [v[x * BY : (x + 1) * BY] for x in range(BX)]
    for x in range(NP, BX, NP):
        both = parts[x - 1] + parts[x]
        parts[x - 1] = both
        parts[x] = both
    sub = lax.broadcasted_iota(jnp.int32, (NP, BZ), 0)
    out = []
    for x in range(BX):
        a, b = parts[x][:NP], parts[x][NP:]
        out.append(jnp.where(sub == NP - 1, a + pltpu.roll(b, NP - 1, 0), a))
        out.append(jnp.where(sub == 0, b + pltpu.roll(a, 1, 0), b))
    return jnp.concatenate(out, axis=0)


def local_sum_z(v):
    lane = lax.broadcasted_iota(jnp.int32, (NP, BZ), 1)
    last = (lane % NP == NP - 1) & (lane < BZ - 1)
    first = (lane % NP == 0) & (lane > 0)
    swap = jnp.where(last, lane + 1, jnp.where(first, lane - 1, lane))
    out = []
    for q in range(v.shape[0] // NP):
        part = v[NP * q : NP * q + NP]
        other = jnp.take_along_axis(part, swap, axis=1, mode="promise_in_bounds")
        out.append(part + jnp.where(last | first, other, 0.0))
    return jnp.concatenate(out, axis=0)


def tree(parts):
    while len(parts) > 1:
        rest = parts[len(parts) // 2 * 2 :]
        parts = [a + b for a, b in zip(parts[0::2], parts[1::2])] + rest
    return parts[0]


class Geometry:
    def __init__(self, sizes):
        self.sizes = sizes
        self.at = [lax.axis_index(a) for a in AXES]
        self.low = [g > 0 for g in self.at]
        self.high = [g < n - 1 for g, n in zip(self.at, sizes)]
        self.me = (self.at[0] * sizes[1] + self.at[1]) * sizes[2] + self.at[2]

    def neighbour(self, *step):
        ok = None
        number = self.me
        strides = (self.sizes[1] * self.sizes[2], self.sizes[2], 1)
        for a in range(3):
            if step[a]:
                there = self.high[a] if step[a] > 0 else self.low[a]
                ok = there if ok is None else jnp.logical_and(ok, there)
                number = number + step[a] * strides[a]
        return jnp.where(ok, number, self.me)

    def half(self, flag):
        return jnp.where(flag, 0.5, 1.0).astype(F32)

    def x_share(self, x):
        if x == 0:
            return self.half(self.low[0])
        if x == BX - 1:
            return self.half(self.high[0])
        return None

    def y_share(self):
        row = lax.broadcasted_iota(jnp.int32, (BY, BZ), 0)
        one = jnp.where(row == 0, self.half(self.low[1]), 1.0)
        return jnp.where(row == BY - 1, self.half(self.high[1]), one)

    def z_share(self, shape, dim):
        lane = lax.broadcasted_iota(jnp.int32, shape, dim)
        one = jnp.where(lane == 0, self.half(self.low[2]), 1.0)
        return jnp.where(lane == BZ - 1, self.half(self.high[2]), one)

    def yz_weight(self):
        row = lax.broadcasted_iota(jnp.int32, (BY, BZ), 0)
        lane = lax.broadcasted_iota(jnp.int32, (BY, BZ), 1)
        inside_y = ((row % NP == 0) & (row > 0)) | ((row % NP == NP - 1) & (row < BY - 1))
        inside_z = ((lane % NP == 0) & (lane > 0)) | ((lane % NP == NP - 1) & (lane < BZ - 1))
        wy = jnp.where(inside_y, 0.5, self.y_share())
        wz = jnp.where(inside_z, 0.5, self.z_share((BY, BZ), 1))
        return wy * wz

    def x_weight(self, x):
        if x in (0, BX - 1):
            return self.x_share(x)
        return 0.5 if x % NP in (0, NP - 1) else 1.0


def inverse_mass(geo, tab):
    base = 3 * NP * NP + BY
    yz = tab[base : base + BY, :] * geo.yz_weight()
    return jnp.concatenate(
        [yz * (geo.x_weight(x) * float(1.0 / WEIGHTS[x % NP])) for x in range(BX)], axis=0
    )


def face_steps(n):
    return ("swap",) if n == 2 else ("up", "down")


class Layout:
    def __init__(self, sizes):
        self.sizes = sizes
        self.devices = sizes[0] * sizes[1] * sizes[2]
        self.plain = self.devices
        self.offset = self.devices + 8
        self.lanes = -(-(self.offset + self.devices) // 128) * 128
        self.scalar_rows = self.lanes // 128

        need = 2 * self.scalar_rows + 2
        self.slot_rows = 4 if need <= 4 else -(-need // 8) * 8

    def field_rows(self, k):
        return (0, self.scalar_rows + 2) if k else (self.scalar_rows, self.scalar_rows + 1)


def pick_faces(geo, axis, n, low, high):
    if n == 2:
        return [jnp.where(geo.at[axis] == 0, high, low)]
    return [high, low]


def tile_iota():
    return lax.broadcasted_iota(jnp.int32, (8, BZ), 0), lax.broadcasted_iota(jnp.int32, (8, BZ), 1)


def pack_z_faces(v, work):
    sub, lane = tile_iota()
    parts = [pltpu.roll(v[8 * q : 8 * q + 8], (2 * q + 1) % BZ, 1) for q in range(ROWS // 8)]
    width = 2
    while len(parts) > 1:
        pairs = zip(parts[0::2], parts[1::2])
        parts = [jnp.where(lane & width == 0, a, b) for a, b in pairs]
        width *= 2
    tile = parts[0]
    turns = (-1, 0, 1, 63, 64, 65)
    for i, a in enumerate(turns):
        work[8 * i : 8 * i + 8, :] = tile if a == 0 else pltpu.roll(tile, a % BZ, 1)
    line = lane[0:1]
    out = []
    for side in (1, 0):
        pair = []
        for r in range(2):
            total = None
            for g in range(4):
                e, h = g % 2, g // 2
                at = 8 * turns.index(e - side + 64 * h) + 4 * r + g
                part = work[at : at + 1, :]
                keep = (line % 2 == e) & (line // 64 == h)
                total = part if total is None else jnp.where(keep, part, total)
            pair.append(total)
        out.append(pair)
    return out


def unpack_z_faces(sides):
    sub, lane = tile_iota()
    low, high = [
        jnp.where(sub < 4, jnp.broadcast_to(s[0], (8, BZ)), jnp.broadcast_to(s[1], (8, BZ)))
        for s in sides
    ]
    tile = None
    for g in range(4):
        shift = g % 2 + 64 * (g // 2)
        a = high if shift == 0 else pltpu.roll(high, -shift % BZ, 1)
        b = low if shift == 1 else pltpu.roll(low, (1 - shift) % BZ, 1)
        part = jnp.where(lane % 2 == 0, a, b)
        tile = part if tile is None else jnp.where(sub % 4 == g, part, tile)
    return tile


def send_field(geo, lay, f_ref, z, work, scalars, send_ref, xs, ys, extra=None):
    rows = lay.slot_rows
    base = [scalars[:, i * 128 : (i + 1) * 128] for i in range(lay.scalar_rows)]
    base.append(jnp.zeros((2, 128), F32))
    if extra is not None:
        base += [extra[:, i * 128 : (i + 1) * 128] for i in range(lay.scalar_rows)]
    used = sum(b.shape[0] for b in base)
    if used < rows:
        base.append(jnp.zeros((rows - used, 128), F32))
    base = jnp.concatenate(base, axis=0)
    send_ref[...] = jnp.broadcast_to(base[None], (lay.devices, rows, 128))
    fill_field(geo, lay, f_ref, z, work, send_ref, 0)
    fill_faces(geo, lay, f_ref, xs, ys)
    send_ref[geo.me] = base


def fill_field(geo, lay, f_ref, z, work, send_ref, k):
    row0, row1 = lay.field_rows(k)
    pairs = pack_z_faces(z, work)
    for dz in (-1, 1):
        pair = pairs[0 if dz < 0 else 1]
        for dx in (-1, 0, 1):
            for dy in (-1, 0, 1):
                there = geo.neighbour(dx, dy, dz)
                send_ref[there, row0 : row0 + 1, :] = pair[0]
                send_ref[there, row1 : row1 + 1, :] = pair[1]
    for dx in (-1, 1):
        for dy in (-1, 1):
            row = (BX - 1 if dx > 0 else 0) * BY + (BY - 1 if dy > 0 else 0)
            send_ref[geo.neighbour(dx, dy, 0), row0 : row0 + 1, :] = f_ref[row : row + 1, :]


def fill_faces(geo, lay, f_ref, xs, ys):
    lowx, highx = f_ref[0:BY, :], f_ref[ROWS - BY : ROWS, :]
    for ref, face in zip(xs, pick_faces(geo, 0, lay.sizes[0], lowx, highx)):
        ref[0:BY, :] = face
    lowy = f_ref[pl.ds(0, BX, stride=BY), :]
    highy = f_ref[pl.ds(BY - 1, BX, stride=BY), :]
    for ref, face in zip(ys, pick_faces(geo, 1, lay.sizes[1], lowy, highy)):
        ref[0:BX, :] = face


def came_from(geo, axis, n, refs, k, size):
    if n == 2:
        face = refs[0][k * size : (k + 1) * size, :]
        return (
            jnp.where(geo.low[axis], face, 0.0),
            jnp.where(geo.high[axis], face, 0.0),
        )
    up = refs[0][k * size : (k + 1) * size, :]
    down = refs[1][k * size : (k + 1) * size, :]
    return jnp.where(geo.low[axis], up, 0.0), jnp.where(geo.high[axis], down, 0.0)


def received(geo, lay, f, recv_ref, xs, ys, w_ref, k):
    at = lay.field_rows(k)
    line = lax.broadcasted_iota(jnp.int32, (1, BZ), 1)
    sides = []
    for dz in (-1, 1):
        pair = []
        for r in range(2):
            total = None
            for dy in (0, 1 if r else -1):
                for dx in (0, -1, 1):
                    source = 1 - r if dy else r
                    part = recv_ref[geo.neighbour(dx, dy, dz), at[source] : at[source] + 1, :]
                    keep = None
                    if dx:
                        keep = line % 64 >= 60 if dx > 0 else line % 64 < 4
                    if dy > 0:
                        want = (line >= 64) & (line % 4 == 3)
                        keep = want if keep is None else keep & want
                    if dy < 0:
                        want = (line < 64) & (line % 4 == 0)
                        keep = want if keep is None else keep & want
                    if keep is not None:
                        part = jnp.where(keep, pltpu.roll(part, (60 * dx + 67 * dy) % BZ, 1), 0.0)
                    total = part if total is None else total + part
            pair.append(total)
        sides.append(pair)
    tile = unpack_z_faces(sides)
    _, lane = tile_iota()
    ends = (lane == 0) | (lane == BZ - 1)
    parts = []
    for q in range(ROWS // 8):
        part = pltpu.roll(tile, (BZ - 1 - 2 * q) % BZ, 1)
        parts.append(f[8 * q : 8 * q + 8] + jnp.where(ends, part, 0.0))
    w_ref[...] = jnp.concatenate(parts, axis=0)
    lowx, highx = came_from(geo, 0, lay.sizes[0], xs, k, BY)
    w_ref[0:BY, :] += lowx
    w_ref[ROWS - BY : ROWS, :] += highx
    lowy, highy = came_from(geo, 1, lay.sizes[1], ys, k, BX)
    w_ref[pl.ds(0, BX, stride=BY), :] += lowy
    w_ref[pl.ds(BY - 1, BX, stride=BY), :] += highy
    for dx in (-1, 1):
        for dy in (-1, 1):
            row = (BX - 1 if dx > 0 else 0) * BY + (BY - 1 if dy > 0 else 0)
            w_ref[row : row + 1, :] += recv_ref[geo.neighbour(dx, dy, 0), at[0] : at[0] + 1, :]


def received_scalars(lay, recv_ref):
    total = recv_ref[...]
    while total.shape[0] % 2 == 0:
        half = total.shape[0] // 2
        total = total[:half] + total[half:]
    total = jnp.sum(total, axis=0)
    return jnp.concatenate([total[i : i + 1] for i in range(lay.scalar_rows)], axis=1)


def coarse_tables(geo, lay, places):
    out = []
    for half in range(2):
        size = 32 if half else 16
        row = lax.broadcasted_iota(jnp.int32, (size, lay.lanes), 0)
        steps = [
            jnp.broadcast_to(places[3 * half + a : 3 * half + a + 1, :], row.shape)
            - geo.at[a].astype(F32)
            for a in range(3)
        ]
        if half:
            row_dx = jnp.where(row < 24, row // 8 - 1, (row - 24) // 2 - 1)
            row_dy = jnp.where(row < 24, 0, row % 2 * 2 - 1)
            row_dx = jnp.where(row < 30, row_dx, 1000)
        else:
            row_dx, row_dy = row // 3 - 1, row % 3 - 1
            row_dx = jnp.where(row < 9, row_dx, 1000)
        near = (steps[0] == row_dx.astype(F32)) & (steps[1] == row_dy.astype(F32))
        for dz in (-1.0, 0.0, 1.0):
            out.append(jnp.where(near & (steps[2] == dz), 1.0, 0.0))
    row = lax.broadcasted_iota(jnp.int32, (24, lay.lanes), 0)
    lane = lax.broadcasted_iota(jnp.int32, (24, lay.lanes), 1)
    out.append(jnp.where(lane == lay.plain + row // 8, 1.0, 0.0))
    return jnp.concatenate(out, axis=0)


HOT_ROWS = 48 + 96 + 24


def partial_sums(geo, v, sums, q_ref, hot_ref):
    first, last = v[0:BY], v[ROWS - BY : ROWS]
    inner = [v[x * BY : (x + 1) * BY] for x in range(1, BX - 1)]
    middle = tree([first * geo.x_share(0), last * geo.x_share(BX - 1), *inner])
    share = geo.y_share()
    for i, part in enumerate((0.5 * first, middle, 0.5 * last)):
        shared = part * share
        q_ref[8 * i : 8 * i + 8, :] = shared[0:8] + shared[8:16]
        q_ref[24 + 2 * i : 25 + 2 * i, :] = 0.5 * part[0:1]
        q_ref[25 + 2 * i : 26 + 2 * i, :] = 0.5 * part[BY - 1 : BY]
    q_ref[30:32, :] = jnp.zeros((2, BZ), F32)
    q = q_ref[...]
    own = jnp.sum(q * geo.z_share(q.shape, 1), axis=1, keepdims=True)
    below, above = 0.5 * q[:, 0:1], 0.5 * q[:, BZ - 1 : BZ]
    rows = hot_ref[48:80, :] * below + hot_ref[80:112, :] * own + hot_ref[112:144, :] * above
    rows = rows[0:8] + rows[8:16] + rows[16:24] + rows[24:32]
    if sums:
        rows = rows + plain_sums(sums, hot_ref)
    return jnp.sum(rows, axis=0, keepdims=True)


def plain_sums(sums, hot_ref):
    parts = []
    for i, total in enumerate(sums):
        at = 144 + 8 * i
        parts.append(hot_ref[at : at + 8, :] * jnp.sum(total, axis=1, keepdims=True))
    return tree(parts)


def spread(geo, values, hot_ref):
    below, own, above = [
        jnp.sum(hot_ref[16 * i : 16 * i + 16, :] * values, axis=1, keepdims=True) for i in range(3)
    ]
    lane = lax.broadcasted_iota(jnp.int32, (16, BZ), 1)
    rows = own * geo.z_share((16, BZ), 1)
    rows = rows + jnp.where(lane == 0, 0.5 * below, 0.0)
    rows = rows + jnp.where(lane == BZ - 1, 0.5 * above, 0.0)
    y = lax.broadcasted_iota(jnp.int32, (BY, BZ), 0)
    share = geo.y_share()
    planes = []
    for i in range(3):
        plane = share * rows[3 * i + 1 : 3 * i + 2]
        plane = plane + jnp.where(y == 0, 0.5 * rows[3 * i : 3 * i + 1], 0.0)
        planes.append(plane + jnp.where(y == BY - 1, 0.5 * rows[3 * i + 2 : 3 * i + 3], 0.0))
    out = [planes[1]] * BX
    out[0] = planes[1] * geo.x_share(0) + 0.5 * planes[0]
    out[BX - 1] = planes[1] * geo.x_share(BX - 1) + 0.5 * planes[2]
    return out


def with_coarse(lay, row, gram_ref):
    return row + jnp.dot(row, gram_ref[...], precision=HIGHEST, preferred_element_type=F32)


def coarse_inner(lay, row):
    lane = lax.broadcasted_iota(jnp.int32, row.shape, 1)
    both = row * pltpu.roll(row, lay.offset, 1)
    return jnp.sum(jnp.where(lane >= lay.offset, both, 0.0), axis=1, keepdims=True)


def all_rows(v):
    return tree([v[8 * i : 8 * i + 8] for i in range(ROWS // 8)])


def weighted_rows(geo, v):
    yz = geo.yz_weight()
    parts = []
    for x in range(BX):
        weight = geo.x_weight(x)
        part = v[x * BY : (x + 1) * BY]
        if not (isinstance(weight, float) and weight == 1.0):
            part = part * weight
        parts.append(part)
    total = tree(parts)
    total = total * yz
    return total[0:8] + total[8:16]


def weak_form(level, tab, zt, work):
    gx, gy, gz = along_x(level, "d"), along_y(level, "d", tab, work.at[0]), along_z(level, "d", zt)
    inv_norm = lax.rsqrt(1.0 + gx * gx + gy * gy + gz * gz)
    coef = bmass_of(tab) * (level * (1.0 - level) * inv_norm - INTERFACE_WIDTH)
    out = along_x(coef * gx, "t") + along_y(coef * gy, "t", tab, work.at[1])
    return out + along_z(coef * gz, "t", zt)


def stiffness(v, scaled, tab, zt, work, final):
    bm = bmass_of(tab)
    gx, gy, gz = along_x(v, "d"), along_y(v, "d", tab, work.at[0]), along_z(v, "d", zt)
    tx, ty, tz = scaled * gx, scaled * gy, scaled * gz
    energy = all_rows(bm * v * v + (tx * gx + ty * gy + tz * gz))
    if final:
        return None, energy
    out = bm * v + along_x(tx, "t") + along_y(ty, "t", tab, work.at[1])
    return out + along_z(tz, "t", zt), energy


def local_step(geo, lay, residual, dinv, scaled, state, image, refs):
    tab, zt, hot, u_ref, f_ref, send_ref, xs, ys, q_ref, state_ref, work, zwork, final = refs
    s_row, ts_row, gamma, curvature = state
    jacobi = residual * dinv
    planes = spread(geo, s_row, hot)
    u = jnp.concatenate([jacobi[x * BY : (x + 1) * BY] + planes[x] for x in range(BX)], axis=0)
    u_ref[...] = u
    local, energy = stiffness(u, scaled, tab, zt, work, final)
    sums = [weighted_rows(geo, residual * jacobi), energy]
    if image is not None:
        sums.append(weighted_rows(geo, u * image))
    ones = jnp.ones_like(s_row)
    coarse = coarse_inner(lay, s_row)
    state_ref[...] = jnp.concatenate(
        [s_row, ts_row, ones * gamma, ones * curvature, ones * coarse, jnp.zeros((3, lay.lanes), F32)],
        axis=0,
    )
    if final:
        scalars = jnp.sum(plain_sums(sums, hot), axis=0, keepdims=True)
        rows = [scalars[:, i * 128 : (i + 1) * 128] for i in range(lay.scalar_rows)]
        rows = jnp.concatenate(rows, axis=0)
        send_ref[...] = jnp.broadcast_to(rows[None], send_ref.shape)
        return
    scalars = partial_sums(geo, local, sums, q_ref, hot)
    local = local_sum_xy(local)
    f_ref[...] = local_sum_z(local)
    send_field(geo, lay, f_ref, local, zwork, scalars, send_ref, xs, ys)


def step_sizes(lay, recv_ref, state_ref, first):
    row = received_scalars(lay, recv_ref)
    lane = lax.broadcasted_iota(jnp.int32, row.shape, 1)

    def pick(which):
        return jnp.sum(jnp.where(lane == lay.plain + which, row, 0.0), axis=1, keepdims=True)

    gamma = pick(0) + state_ref[4:5, 0:1]
    if first:
        curvature = pick(1)
        beta = None
    else:
        beta = gamma / state_ref[2:3, 0:1]
        curvature = pick(1) + beta * (2.0 * pick(2) + beta * state_ref[3:4, 0:1])
    return row, gamma, curvature, beta, gamma / curvature


def build(mesh):
    sizes = tuple(int(mesh.shape[a]) for a in AXES)
    lay = Layout(sizes)
    steps = [face_steps(sizes[0]), face_steps(sizes[1])]
    nx, ny = len(steps[0]), len(steps[1])
    tab_np, zt_np = const_tables(), z_tables()
    number = np.arange(lay.lanes)
    places_np = np.full((8, lay.lanes), -9.0, np.float32)
    for half in range(2):
        lanes = slice(half * lay.offset, half * lay.offset + lay.devices)
        for a, place in enumerate(np.unravel_index(np.arange(lay.devices), sizes)):
            places_np[3 * half + a, lanes] = place
    block = jax.ShapeDtypeStruct((ROWS, BZ), F32)

    def like(*shape):
        return jax.ShapeDtypeStruct(shape, F32)

    def outgoing(fields):
        return (
            [like(lay.devices, lay.slot_rows, 128)]
            + [like(BY * fields, BZ)] * nx
            + [like(BX * fields, BZ)] * ny
        )

    def call(kernel, ins, outs, scratch, name, from_hbm=()):
        spec = pl.BlockSpec(memory_space=pltpu.VMEM)
        hbm = pl.BlockSpec(memory_space=pltpu.HBM)
        ins = [pltpu.with_memory_space_constraint(v, pltpu.HBM) if i in from_hbm else v for i, v in enumerate(ins)]
        return pl.pallas_call(
            kernel,
            out_shape=outs,
            in_specs=[hbm if i in from_hbm else spec for i in range(len(ins))],
            out_specs=[spec] * len(outs),
            scratch_shapes=scratch,
            compiler_params=pltpu.CompilerParams(vmem_limit_bytes=48 * 1024 * 1024),
            cost_estimate=pl.CostEstimate(flops=4000000, bytes_accessed=1000000, transcendentals=0),
            name=name,
        )(*ins)

    work = pltpu.VMEM((ROWS, BZ), F32)
    qrows = pltpu.VMEM((32, BZ), F32)
    pair = pltpu.VMEM((2, ROWS, BZ), F32)
    tiles = pltpu.VMEM((48, BZ), F32)

    def ring(v, axis, n, step):
        if step == "swap":
            pairs = [(0, 1), (1, 0)]
        else:
            d = 1 if step == "up" else n - 1
            pairs = [(i, (i + d) % n) for i in range(n)]
        return lax.ppermute(v, axis, pairs)

    def exchange(out):
        send, faces = out[0], out[1:]
        recv = lax.all_to_all(send, AXES, 0, 0, tiled=True)
        xs = [ring(faces[i], "gx", sizes[0], s) for i, s in enumerate(steps[0])]
        ys = [ring(faces[nx + i], "gy", sizes[1], s) for i, s in enumerate(steps[1])]
        return [recv, *xs, *ys]

    n_out = 1 + nx + ny

    def split(refs):
        return refs[0], refs[1 : 1 + nx], refs[1 + nx : 1 + nx + ny]

    def start_kernel(level_any, vel_any, tab_any, zt_any, *rest):
        send, xs, ys = split(rest[:n_out])
        f_ref, work, zwork = rest[n_out : n_out + 3]
        level_ref, zt_ref, tab_ref, vel_ref, sems = rest[n_out + 3 :]
        sources = (level_any, zt_any.at[0 : 2 * BZ], tab_any, vel_any)
        copies = [
            pltpu.make_async_copy(source, target, sems.at[i])
            for i, (source, target) in enumerate(zip(sources, (level_ref, zt_ref, tab_ref, vel_ref)))
        ]
        for copy in copies:
            copy.start()
        for copy in copies[:3]:
            copy.wait()
        geo = Geometry(sizes)
        level = level_ref[...]
        gx, gy, gz = along_x(level, "d"), along_y(level, "d", tab_ref, work.at[0]), along_z(level, "d", zt_ref)
        copies[3].wait()
        advect = bmass_of(tab_ref) * (vel_ref[0] * gx + vel_ref[1] * gy + vel_ref[2] * gz)
        finish(geo, advect, f_ref, zwork, send, xs, ys)

    def finish(geo, v, f_ref, zwork, send, xs, ys, scalars=None, extra=None):
        v = local_sum_xy(v)
        f_ref[...] = local_sum_z(v)
        if scalars is None:
            scalars = jnp.zeros((1, lay.lanes), F32)
        send_field(geo, lay, f_ref, v, zwork, scalars, send, xs, ys, extra)

    def source_kernel(vel_ref, source_ref, factor_ref, tab_ref, zt_ref, places_ref, _, *rest):
        slots, xs, ys = split(rest[:n_out])
        f_ref, hot_ref, row_ref, q_ref, work, zwork = rest[n_out:]
        geo = Geometry(sizes)
        bm = bmass_of(tab_ref)
        div = bm * source_ref[...] + along_x(bm * vel_ref[0], "t")
        div = div + along_y(bm * vel_ref[1], "t", tab_ref, work.at[1])
        div = div + along_z(bm * vel_ref[2], "t", zt_ref)
        hot_ref[...] = coarse_tables(geo, lay, places_ref)
        row_ref[0:1, :] = partial_sums(geo, div, [], q_ref, hot_ref)
        factor = factor_ref[...]
        if lay.lanes > lay.devices:
            pad = jnp.zeros((1, lay.lanes - lay.devices), F32)
            factor = jnp.concatenate([factor, pad], axis=1)
        row_ref[1:2, :] = factor
        row_ref[2:8, :] = jnp.zeros((6, lay.lanes), F32)
        div = local_sum_xy(div)
        f_ref[...] = local_sum_z(div)
        slots[...] = jnp.zeros(slots.shape, F32)
        fill_field(geo, lay, f_ref, div, zwork, slots, 1)
        slots[geo.me] = jnp.zeros(slots.shape[1:], F32)
        fill_faces(geo, lay, f_ref, xs, ys)

    def first_kernel(recv, *rest):
        xs, ys = rest[:nx], rest[nx : nx + ny]
        level_ref, fa_ref, tab_ref, zt_ref, row_ref = rest[nx + ny : nx + ny + 5]
        out = rest[nx + ny + 5 :]
        send, oxs, oys = split(out[:n_out])
        level_out, f_ref, w_ref, work, zwork = out[n_out:]
        geo = Geometry(sizes)
        received(geo, lay, fa_ref[...], recv, xs, ys, w_ref, 0)
        level = level_ref[...] - TIME_STEP * w_ref[...] * inverse_mass(geo, tab_ref)
        level_out[...] = level
        weak = weak_form(level, tab_ref, zt_ref, work)
        finish(geo, weak, f_ref, zwork, send, oxs, oys, row_ref[0:1, :], row_ref[1:2, :])

    def rhs_kernel(recv, *rest):
        xs, ys = rest[:nx], rest[nx : nx + ny]
        rows_ref, fd_ref, hot_ref, r_ref, s_ref, hot_out, w_ref, gram_ref = rest[nx + ny :]
        geo = Geometry(sizes)
        at = lay.scalar_rows + 2
        factor = [rows_ref[:, at + i, :] for i in range(lay.scalar_rows)]
        factor = jnp.concatenate(factor, axis=1)
        after = lay.lanes - lay.offset - lay.devices
        shifted = [jnp.zeros((lay.offset, lay.lanes), F32), factor]
        if after:
            shifted.append(jnp.zeros((after, lay.lanes), F32))
        plain = [factor, jnp.zeros((lay.lanes - lay.devices, lay.lanes), F32)]
        gram_ref[...] = lax.dot_general(
            jnp.concatenate(shifted, axis=0),
            jnp.concatenate(plain, axis=0),
            (((1,), (1,)), ((), ())),
            precision=HIGHEST,
            preferred_element_type=F32,
        )
        received(geo, lay, fd_ref[...], recv, xs, ys, w_ref, 1)
        r_ref[...] = SOURCE_SCALE * w_ref[...]
        row = with_coarse(lay, SOURCE_SCALE * received_scalars(lay, rows_ref), gram_ref)
        s_ref[...] = jnp.broadcast_to(row, s_ref.shape)
        hot_out[...] = hot_ref[...]
        hot_out[48:144, :] = with_coarse(lay, hot_ref[48:144, :], gram_ref)

    def new_level(geo, recv, xs, ys, level_ref, f_ref, tab_ref, w_ref):
        received(geo, lay, f_ref[...], recv, xs, ys, w_ref, 0)
        return level_ref[...] + PSEUDO_STEP * w_ref[...] * inverse_mass(geo, tab_ref)

    def sweep_kernel(recv, *rest):
        xs, ys = rest[:nx], rest[nx : nx + ny]
        level_ref, fin_ref, tab_ref, zt_ref = rest[nx + ny : nx + ny + 4]
        slots, sxs, sys = split(rest[nx + ny + 4 : nx + ny + 4 + n_out])
        out = rest[nx + ny + 4 + n_out :]
        send, oxs, oys = split(out[:n_out])
        level_out, f_ref, w_ref, work, zwork = out[n_out:]
        geo = Geometry(sizes)
        level = new_level(geo, recv, xs, ys, level_ref, fin_ref, tab_ref, w_ref)
        level_out[...] = level
        v = local_sum_xy(weak_form(level, tab_ref, zt_ref, work))
        f_ref[...] = local_sum_z(v)
        send[...] = slots[...]
        fill_field(geo, lay, f_ref, v, zwork, send, 0)
        send[geo.me] = slots[geo.me]
        fill_faces(geo, lay, f_ref, oxs, oys)
        for to, part in zip((*oxs, *oys), (*sxs, *sys)):
            to[BY : 2 * BY, :] = part[...]

    def diagonal_kernel(recv, *rest):
        xs, ys = rest[:nx], rest[nx : nx + ny]
        level_ref, fin_ref, tab_ref, zt_ref = rest[nx + ny : nx + ny + 4]
        out = rest[nx + ny + 4 :]
        send, oxs, oys = split(out[:n_out])
        level_out, f_ref, scaled_ref, w_ref, work, zwork = out[n_out:]
        geo = Geometry(sizes)
        level = new_level(geo, recv, xs, ys, level_ref, fin_ref, tab_ref, w_ref)
        level_out[...] = level
        bm = bmass_of(tab_ref)
        scaled = bm / (GAS_DENSITY + (1.0 - GAS_DENSITY) * jnp.clip(level, 0.0, 1.0))
        scaled_ref[...] = scaled
        diag = bm + along_x(scaled, "s") + along_y(scaled, "s", tab_ref, work.at[0])
        diag = diag + along_z(scaled, "s", zt_ref)
        finish(geo, diag, f_ref, zwork, send, oxs, oys)

    def solve_kernel(recv, *rest):
        xs, ys = rest[:nx], rest[nx : nx + ny]
        fin_ref, r_ref, scaled_ref, s_ref, tab_ref, zt_ref, hot_ref = rest[nx + ny : nx + ny + 7]
        out = rest[nx + ny + 7 :]
        send, oxs, oys = split(out[:n_out])
        dinv_ref, u_ref, f_ref, state_ref, w_ref, work, zwork, q_ref = out[n_out:]
        geo = Geometry(sizes)
        received(geo, lay, fin_ref[...], recv, xs, ys, w_ref, 0)
        dinv = 1.0 / w_ref[...]
        dinv_ref[...] = dinv
        zero = jnp.zeros((1, 1), F32)
        s_row = s_ref[0:1, :]
        state = (s_row, jnp.zeros_like(s_row), zero, zero)
        refs = (tab_ref, zt_ref, hot_ref, u_ref, f_ref, send, oxs, oys)
        local_step(
            geo, lay, r_ref[...], dinv, scaled_ref[...], state, None, (*refs, q_ref, state_ref, work, zwork, False)
        )

    def make_iterate(first, final):
        def iterate_kernel(recv, *rest):
            xs, ys = rest[:nx], rest[nx : nx + ny]
            n_in = 9 + (0 if first else 3)
            ins = rest[nx + ny : nx + ny + n_in]
            fin_ref, r_ref, u_in, dinv_ref, scaled_ref, state_in = ins[:6]
            tab_ref, zt_ref, hot_ref = ins[6:9]
            p_in, si_in, x_in = (None, None, None) if first else ins[9:12]
            out = rest[nx + ny + n_in :]
            if final:
                send, oxs, oys = out[0], (), ()
                out = out[1:]
                u_ref, state_ref, p_ref, x_ref, w_ref, work, zwork, q_ref = out
                f_ref = r_out = si_ref = None
            else:
                send, oxs, oys = split(out[:n_out])
                u_ref, state_ref, p_ref, x_ref, r_out, si_ref, f_ref, w_ref, work, zwork, q_ref = out[
                    n_out:
                ]
            geo = Geometry(sizes)
            row, gamma, curvature, beta, alpha = step_sizes(lay, recv, state_in, first)
            received(geo, lay, fin_ref[...], recv, xs, ys, w_ref, 0)
            image = w_ref[...]
            p = u_in[...]
            s_row, ts_row = state_in[0:1, :], row
            if not first:
                p = p + beta * p_in[...]
                image = image + beta * si_in[...]
                ts_row = ts_row + beta * state_in[1:2, :]
            p_ref[...] = p
            x_ref[...] = alpha * p if first else x_in[...] + alpha * p
            residual = r_ref[...] - alpha * image
            if not final:
                si_ref[...] = image
                r_out[...] = residual
            lane = lax.broadcasted_iota(jnp.int32, row.shape, 1)
            ts_row = jnp.where((lane < lay.devices) | (lane >= lay.offset), ts_row, 0.0)
            state = (s_row - alpha * ts_row, ts_row, gamma, curvature)
            refs = (tab_ref, zt_ref, hot_ref, u_ref, f_ref, send)
            local_step(
                geo,
                lay,
                residual,
                dinv_ref[...],
                scaled_ref[...],
                state,
                image,
                (*refs, oxs, oys, q_ref, state_ref, work, zwork, final),
            )

        return iterate_kernel

    def last_kernel(recv, state_in, u_in, p_in, x_in, out_ref):
        _, _, _, beta, alpha = step_sizes(lay, recv, state_in, False)
        out_ref[...] = x_in[...] + alpha * (u_in[...] + beta * p_in[...])

    def body(level_set, velocity, source, coarse_factor):
        level = level_set.reshape(ROWS, BZ)
        vel = velocity.reshape(3, ROWS, BZ)
        src = source.reshape(ROWS, BZ)
        tab, zt, places = jnp.asarray(tab_np), jnp.asarray(zt_np), jnp.asarray(places_np)
        out = call(
            start_kernel,
            [level, vel, tab, zt],
            outgoing(1) + [block],
            [pair, tiles]
            + [pltpu.VMEM(a, d) for a, d in ((level.shape, F32), ((2 * BZ, 2 * BZ), BF16), (tab.shape, F32), (vel.shape, F32))]
            + [pltpu.SemaphoreType.DMA((4,))],
            "advect",
            range(4),
        )
        fa = out[n_out]
        got = exchange(out[:n_out])
        side = call(
            source_kernel,
            [vel, src, coarse_factor, tab, zt, places, fa],
            outgoing(1) + [block, like(HOT_ROWS, lay.lanes), like(8, lay.lanes)],
            [qrows, pair, tiles],
            "source",
        )
        fd, hot, row = side[n_out:]
        out = call(
            first_kernel,
            [*got, level, fa, tab, zt, row],
            outgoing(1) + [block, block],
            [work, pair, tiles],
            "sweep_first",
        )
        level, f = out[n_out:]
        got = rows = exchange(out[:n_out])
        out = call(
            sweep_kernel,
            [*got, level, f, tab, zt, *side[:n_out]],
            outgoing(2) + [block, block],
            [work, pair, tiles],
            "sweep",
        )
        level, f = out[n_out:]
        got = exchange(out[:n_out])
        residual, s_rows, hot = call(
            rhs_kernel,
            [*got, rows[0], fd, hot],
            [block, like(8, lay.lanes), like(HOT_ROWS, lay.lanes)],
            [work, pltpu.VMEM((lay.lanes, lay.lanes), F32)],
            "rhs",
        )
        out = call(
            diagonal_kernel,
            [*got, level, f, tab, zt],
            outgoing(1) + [block, block, block],
            [work, pair, tiles],
            "diagonal",
        )
        level, f, scaled = out[n_out:]
        got = exchange(out[:n_out])
        out = call(
            solve_kernel,
            [*got, f, residual, scaled, s_rows, tab, zt, hot],
            outgoing(1) + [block, block, block, like(8, lay.lanes)],
            [work, pair, tiles, qrows],
            "solve_start",
        )
        dinv, u, f, state = out[n_out:]
        p = image = x = None
        for step in range(ITERS - 1):
            first, final = step == 0, step == ITERS - 2
            got = exchange(out[:n_out])
            ins = [*got, f, residual, u, dinv, scaled, state, tab, zt, hot]
            if not first:
                ins += [p, image, x]
            fields = [block, like(8, lay.lanes), block, block]
            if final:
                outs = [like(lay.devices, lay.scalar_rows, 128)] + fields
            else:
                outs = outgoing(1) + fields + [block, block, block]
            out = call(make_iterate(first, final), ins, outs, [work, pair, tiles, qrows], "iterate")
            if final:
                u, state, p, x = out[1:]
            else:
                u, state, p, x, residual, image, f = out[n_out:]
        recv = lax.all_to_all(out[0], AXES, 0, 0, tiled=True)
        (x,) = call(last_kernel, [recv, state, u, p, x], [block], [], "pressure")
        return level.reshape(BX, BY, BZ), x.reshape(BX, BY, BZ)

    return body


def solution(mesh):
    in_specs = (
        P("gx", "gy", "gz"),
        P(None, "gx", "gy", "gz"),
        P("gx", "gy", "gz"),
        P(("gx", "gy", "gz"), None),
    )
    out_specs = (P("gx", "gy", "gz"), P("gx", "gy", "gz"))
    return jax.shard_map(
        build(mesh), mesh=mesh, in_specs=in_specs, out_specs=out_specs, check_vma=False
    )
```

```python
import jax
import jax.numpy as jnp
import ml_dtypes
import numpy as np
from jax import lax
from jax.experimental import pallas as pl
from jax.experimental.pallas import tpu as pltpu
from jax.sharding import PartitionSpec as P

NP = 8
ITERS = 6
AXES = ("gx", "gy", "gz")

GLL_POINTS = (
    -1.0,
    -0.8717401485096066,
    -0.5917001814331423,
    -0.2092992179024789,
    0.2092992179024789,
    0.5917001814331423,
    0.8717401485096066,
    1.0,
)
GLL_WEIGHTS = (
    0.03571428571428571,
    0.21070422714350603,
    0.3411226924835044,
    0.4124587946587038,
    0.4124587946587038,
    0.3411226924835044,
    0.21070422714350603,
    0.03571428571428571,
)
HIGHEST = lax.Precision.HIGHEST
TIME_STEP = 0.02
PSEUDO_STEP = 0.004
INTERFACE_WIDTH = 0.5
GAS_DENSITY = 0.1
SOURCE_SCALE = 20.0
F32 = jnp.float32
BF16 = jnp.bfloat16


def node_tables():
    points = np.array(GLL_POINTS)
    amount = points.shape[0]
    barycentric = np.ones(amount)
    for target in range(amount):
        for partner in range(amount):
            if partner != target:
                barycentric[target] = barycentric[target] / (points[target] - points[partner])
    derivative = np.zeros((amount, amount))
    for target in range(amount):
        for partner in range(amount):
            if partner != target:
                derivative[target, partner] = (
                    barycentric[partner] / barycentric[target] / (points[target] - points[partner])
                )
        derivative[target, target] = -np.sum(derivative[target])
    return derivative


DERIV = node_tables()
TRANS = DERIV.T.copy()
SQUARE = (DERIV * DERIV).T.copy()
WEIGHTS = np.array(GLL_WEIGHTS)

BX, BY, BZ = 16, 16, 128
ROWS = BX * BY


def split_bf16(matrix):
    full = matrix.astype(np.float32)
    high = full.astype(ml_dtypes.bfloat16)
    low = (full - high.astype(np.float32)).astype(ml_dtypes.bfloat16)
    return high, low


def const_tables():
    parts = []
    for matrix in (DERIV, TRANS, SQUARE):
        for column in matrix.T:
            parts.append(np.repeat(column[:, None], BZ, axis=1))
    wy = np.tile(WEIGHTS, BY // NP)
    wz = np.tile(WEIGHTS, BZ // NP)
    parts.append(wy[:, None] * wz[None, :])
    parts.append(1.0 / (wy[:, None] * wz[None, :]))
    return np.concatenate(parts, axis=0).astype(np.float32)


def z_tables():
    out = []
    for matrix in (DERIV, TRANS, SQUARE):
        high, low = split_bf16(np.kron(np.eye(BZ // NP), matrix.T))
        top = np.concatenate([high, low], axis=1)
        out += [top, np.concatenate([high, np.zeros_like(low)], axis=1)]
    return np.concatenate(out, axis=0)


KIND = {"d": 0, "t": 1, "s": 2}
MATS = {"d": DERIV, "t": TRANS, "s": SQUARE}


def along_x(v, kind):
    matrix = MATS[kind]
    sign = 1.0 if abs(matrix[7, 7] - matrix[0, 0]) < abs(matrix[7, 7] + matrix[0, 0]) else -1.0
    out = [None] * BX
    for e in range(BX // NP):
        part = [v[(e * NP + i) * BY : (e * NP + i + 1) * BY] for i in range(NP)]
        even = [part[j] + part[7 - j] for j in range(4)]
        odd = [part[j] - part[7 - j] for j in range(4)]
        for i in range(4):
            a = b = None
            for j in range(4):
                ca = float(0.5 * (matrix[i, j] + matrix[i, 7 - j]))
                cb = float(0.5 * (matrix[i, j] - matrix[i, 7 - j]))
                a = ca * even[j] if a is None else a + ca * even[j]
                b = cb * odd[j] if b is None else b + cb * odd[j]
            out[e * NP + i] = a + b
            out[e * NP + 7 - i] = a - b if sign > 0 else b - a
    return jnp.concatenate(out, axis=0)


def along_y(v, kind, tab, work):
    work[...] = v
    base = KIND[kind] * NP * NP
    columns = [tab[base + s * NP : base + (s + 1) * NP, :] for s in range(NP)]
    out = []
    for q in range(ROWS // NP):
        total = None
        for s in range(NP):
            part = columns[s] * work[NP * q + s : NP * q + s + 1, :]
            total = part if total is None else total + part
        out.append(total)
    return jnp.concatenate(out, axis=0)


def along_z(v, kind, zt):
    base = KIND[kind] * 2 * BZ
    vh = v.astype(BF16)
    vl = (v - vh.astype(F32)).astype(BF16)
    both = jnp.dot(
        jnp.concatenate([vh, vl], axis=1), zt[base : base + 2 * BZ, :], preferred_element_type=F32
    )
    return both[:, :BZ] + both[:, BZ:]


def bmass_of(tab):
    base = 3 * NP * NP
    yz = tab[base : base + BY, :]
    return jnp.concatenate([yz * float(WEIGHTS[x % NP]) for x in range(BX)], axis=0)


def local_sum_xy(v):
    parts = [v[x * BY : (x + 1) * BY] for x in range(BX)]
    for x in range(NP, BX, NP):
        both = parts[x - 1] + parts[x]
        parts[x - 1] = both
        parts[x] = both
    sub = lax.broadcasted_iota(jnp.int32, (NP, BZ), 0)
    out = []
    for x in range(BX):
        a, b = parts[x][:NP], parts[x][NP:]
        out.append(jnp.where(sub == NP - 1, a + pltpu.roll(b, NP - 1, 0), a))
        out.append(jnp.where(sub == 0, b + pltpu.roll(a, 1, 0), b))
    return jnp.concatenate(out, axis=0)


def local_sum_z(v):
    lane = lax.broadcasted_iota(jnp.int32, (NP, BZ), 1)
    last = (lane % NP == NP - 1) & (lane < BZ - 1)
    first = (lane % NP == 0) & (lane > 0)
    swap = jnp.where(last, lane + 1, jnp.where(first, lane - 1, lane))
    out = []
    for q in range(v.shape[0] // NP):
        part = v[NP * q : NP * q + NP]
        other = jnp.take_along_axis(part, swap, axis=1, mode="promise_in_bounds")
        out.append(part + jnp.where(last | first, other, 0.0))
    return jnp.concatenate(out, axis=0)


def tree(parts):
    while len(parts) > 1:
        rest = parts[len(parts) // 2 * 2 :]
        parts = [a + b for a, b in zip(parts[0::2], parts[1::2])] + rest
    return parts[0]


class Geometry:
    def __init__(self, sizes):
        self.sizes = sizes
        self.at = [lax.axis_index(a) for a in AXES]
        self.low = [g > 0 for g in self.at]
        self.high = [g < n - 1 for g, n in zip(self.at, sizes)]
        self.me = (self.at[0] * sizes[1] + self.at[1]) * sizes[2] + self.at[2]

    def neighbour(self, *step):
        ok = None
        number = self.me
        strides = (self.sizes[1] * self.sizes[2], self.sizes[2], 1)
        for a in range(3):
            if step[a]:
                there = self.high[a] if step[a] > 0 else self.low[a]
                ok = there if ok is None else jnp.logical_and(ok, there)
                number = number + step[a] * strides[a]
        return jnp.where(ok, number, self.me)

    def across(self, dy, dz):
        plane = self.sizes[1] * self.sizes[2]
        there = self.neighbour(0, dy, dz)
        other = jnp.where(self.at[0] == 0, there + plane, there - plane)
        return other if dy == 0 and dz == 0 else jnp.where(there == self.me, self.me, other)

    def x_sides(self):
        return (2,) if self.sizes[0] == 2 else (-1, 1)

    def beside(self, dx, dy, dz):
        return self.across(dy, dz) if dx == 2 else self.neighbour(dx, dy, dz)

    def half(self, flag):
        return jnp.where(flag, 0.5, 1.0).astype(F32)

    def x_share(self, x):
        if x == 0:
            return self.half(self.low[0])
        if x == BX - 1:
            return self.half(self.high[0])
        return None

    def y_share(self):
        row = lax.broadcasted_iota(jnp.int32, (BY, BZ), 0)
        one = jnp.where(row == 0, self.half(self.low[1]), 1.0)
        return jnp.where(row == BY - 1, self.half(self.high[1]), one)

    def z_share(self, shape, dim):
        lane = lax.broadcasted_iota(jnp.int32, shape, dim)
        one = jnp.where(lane == 0, self.half(self.low[2]), 1.0)
        return jnp.where(lane == BZ - 1, self.half(self.high[2]), one)

    def yz_weight(self):
        row = lax.broadcasted_iota(jnp.int32, (BY, BZ), 0)
        lane = lax.broadcasted_iota(jnp.int32, (BY, BZ), 1)
        inside_y = ((row % NP == 0) & (row > 0)) | ((row % NP == NP - 1) & (row < BY - 1))
        inside_z = ((lane % NP == 0) & (lane > 0)) | ((lane % NP == NP - 1) & (lane < BZ - 1))
        wy = jnp.where(inside_y, 0.5, self.y_share())
        wz = jnp.where(inside_z, 0.5, self.z_share((BY, BZ), 1))
        return wy * wz

    def x_weight(self, x):
        if x in (0, BX - 1):
            return self.x_share(x)
        return 0.5 if x % NP in (0, NP - 1) else 1.0


def inverse_mass(geo, tab):
    base = 3 * NP * NP + BY
    yz = tab[base : base + BY, :] * geo.yz_weight()
    return jnp.concatenate(
        [yz * (geo.x_weight(x) * float(1.0 / WEIGHTS[x % NP])) for x in range(BX)], axis=0
    )


def face_steps(n):
    return ("swap",) if n == 2 else ("up", "down")


class Layout:
    def __init__(self, sizes):
        self.sizes = sizes
        self.devices = sizes[0] * sizes[1] * sizes[2]
        self.plain = self.devices
        self.offset = self.devices + 8
        self.lanes = -(-(self.offset + self.devices) // 128) * 128
        self.scalar_rows = self.lanes // 128

        need = 2 * self.scalar_rows + 2
        self.slot_rows = 4 if need <= 4 else -(-need // 8) * 8

    def field_rows(self, k):
        return (0, self.scalar_rows + 2) if k else (self.scalar_rows, self.scalar_rows + 1)


def pick_faces(geo, axis, n, low, high):
    if n == 2:
        return [jnp.where(geo.at[axis] == 0, high, low)]
    return [high, low]


def tile_iota():
    return lax.broadcasted_iota(jnp.int32, (8, BZ), 0), lax.broadcasted_iota(jnp.int32, (8, BZ), 1)


def pack_z_faces(v, work):
    sub, lane = tile_iota()
    parts = [pltpu.roll(v[8 * q : 8 * q + 8], (2 * q + 1) % BZ, 1) for q in range(ROWS // 8)]
    width = 2
    while len(parts) > 1:
        pairs = zip(parts[0::2], parts[1::2])
        parts = [jnp.where(lane & width == 0, a, b) for a, b in pairs]
        width *= 2
    tile = parts[0]
    turns = (-1, 0, 1, 63, 64, 65)
    for i, a in enumerate(turns):
        work[8 * i : 8 * i + 8, :] = tile if a == 0 else pltpu.roll(tile, a % BZ, 1)
    line = lane[0:1]
    out = []
    for side in (1, 0):
        pair = []
        for r in range(2):
            total = None
            for g in range(4):
                e, h = g % 2, g // 2
                at = 8 * turns.index(e - side + 64 * h) + 4 * r + g
                part = work[at : at + 1, :]
                keep = (line % 2 == e) & (line // 64 == h)
                total = part if total is None else jnp.where(keep, part, total)
            pair.append(total)
        out.append(pair)
    return out


def unpack_z_faces(sides):
    sub, lane = tile_iota()
    low, high = [
        jnp.where(sub < 4, jnp.broadcast_to(s[0], (8, BZ)), jnp.broadcast_to(s[1], (8, BZ)))
        for s in sides
    ]
    tile = None
    for g in range(4):
        shift = g % 2 + 64 * (g // 2)
        a = high if shift == 0 else pltpu.roll(high, -shift % BZ, 1)
        b = low if shift == 1 else pltpu.roll(low, (1 - shift) % BZ, 1)
        part = jnp.where(lane % 2 == 0, a, b)
        tile = part if tile is None else jnp.where(sub % 4 == g, part, tile)
    return tile


def send_field(geo, lay, f_ref, z, work, scalars, send_ref, xs, ys, extra=None):
    rows = lay.slot_rows
    base = [scalars[:, i * 128 : (i + 1) * 128] for i in range(lay.scalar_rows)]
    base.append(jnp.zeros((2, 128), F32))
    if extra is not None:
        base += [extra[:, i * 128 : (i + 1) * 128] for i in range(lay.scalar_rows)]
    used = sum(b.shape[0] for b in base)
    if used < rows:
        base.append(jnp.zeros((rows - used, 128), F32))
    base = jnp.concatenate(base, axis=0)
    send_ref[...] = jnp.broadcast_to(base[None], (lay.devices, rows, 128))
    fill_field(geo, lay, f_ref, z, work, send_ref, 0)
    fill_faces(geo, lay, f_ref, xs, ys)
    send_ref[geo.me] = base


def fill_field(geo, lay, f_ref, z, work, send_ref, k):
    row0, row1 = lay.field_rows(k)
    pairs = pack_z_faces(z, work)
    for dz in (-1, 1):
        pair = pairs[0 if dz < 0 else 1]
        for dx in (0, *geo.x_sides()):
            for dy in (-1, 0, 1):
                there = geo.beside(dx, dy, dz)
                send_ref[there, row0 : row0 + 1, :] = pair[0]
                send_ref[there, row1 : row1 + 1, :] = pair[1]
    for dx in geo.x_sides():
        for dy in (-1, 1):
            low = BY - 1 if dy > 0 else 0
            high = low + (BX - 1) * BY
            if dx == 2:
                edge = jnp.where(geo.at[0] == 0, f_ref[high : high + 1, :], f_ref[low : low + 1, :])
            else:
                row = high if dx > 0 else low
                edge = f_ref[row : row + 1, :]
            send_ref[geo.beside(dx, dy, 0), row0 : row0 + 1, :] = edge


def fill_faces(geo, lay, f_ref, xs, ys):
    lowx, highx = f_ref[0:BY, :], f_ref[ROWS - BY : ROWS, :]
    for ref, face in zip(xs, pick_faces(geo, 0, lay.sizes[0], lowx, highx)):
        ref[0:BY, :] = face
    lowy = f_ref[pl.ds(0, BX, stride=BY), :]
    highy = f_ref[pl.ds(BY - 1, BX, stride=BY), :]
    for ref, face in zip(ys, pick_faces(geo, 1, lay.sizes[1], lowy, highy)):
        ref[0:BX, :] = face


def came_from(geo, axis, n, refs, k, size):
    if n == 2:
        face = refs[0][k * size : (k + 1) * size, :]
        return (
            jnp.where(geo.low[axis], face, 0.0),
            jnp.where(geo.high[axis], face, 0.0),
        )
    up = refs[0][k * size : (k + 1) * size, :]
    down = refs[1][k * size : (k + 1) * size, :]
    return jnp.where(geo.low[axis], up, 0.0), jnp.where(geo.high[axis], down, 0.0)


def received(geo, lay, f, recv_ref, xs, ys, w_ref, k):
    at = lay.field_rows(k)
    line = lax.broadcasted_iota(jnp.int32, (1, BZ), 1)
    sides = []
    for dz in (-1, 1):
        pair = []
        for r in range(2):
            total = None
            for dy in (0, 1 if r else -1):
                for dx in (0, *geo.x_sides()):
                    source = 1 - r if dy else r
                    part = recv_ref[geo.beside(dx, dy, dz), at[source] : at[source] + 1, :]
                    keep = None
                    shift = (60 * dx + 67 * dy) % BZ
                    if dx == 2:
                        first = jnp.where(geo.at[0] == 0, 60, 0)
                        keep = (line % 64 >= first) & (line % 64 < first + 4)
                        shift = jnp.where(geo.at[0] == 0, (60 + 67 * dy) % BZ, (67 * dy - 60) % BZ)
                    elif dx:
                        keep = line % 64 >= 60 if dx > 0 else line % 64 < 4
                    if dy > 0:
                        want = (line >= 64) & (line % 4 == 3)
                        keep = want if keep is None else keep & want
                    if dy < 0:
                        want = (line < 64) & (line % 4 == 0)
                        keep = want if keep is None else keep & want
                    if keep is not None:
                        part = jnp.where(keep, pltpu.roll(part, shift, 1), 0.0)
                    total = part if total is None else total + part
            pair.append(total)
        sides.append(pair)
    tile = unpack_z_faces(sides)
    _, lane = tile_iota()
    ends = (lane == 0) | (lane == BZ - 1)
    parts = []
    for q in range(ROWS // 8):
        part = pltpu.roll(tile, (BZ - 1 - 2 * q) % BZ, 1)
        parts.append(f[8 * q : 8 * q + 8] + jnp.where(ends, part, 0.0))
    w_ref[...] = jnp.concatenate(parts, axis=0)
    lowx, highx = came_from(geo, 0, lay.sizes[0], xs, k, BY)
    w_ref[0:BY, :] += lowx
    w_ref[ROWS - BY : ROWS, :] += highx
    lowy, highy = came_from(geo, 1, lay.sizes[1], ys, k, BX)
    w_ref[pl.ds(0, BX, stride=BY), :] += lowy
    w_ref[pl.ds(BY - 1, BX, stride=BY), :] += highy
    for dx in geo.x_sides():
        for dy in (-1, 1):
            edge = recv_ref[geo.beside(dx, dy, 0), at[0] : at[0] + 1, :]
            low = BY - 1 if dy > 0 else 0
            high = low + (BX - 1) * BY
            if dx == 2:
                w_ref[low : low + 1, :] += jnp.where(geo.at[0] == 0, 0.0, edge)
                w_ref[high : high + 1, :] += jnp.where(geo.at[0] == 0, edge, 0.0)
            else:
                row = high if dx > 0 else low
                w_ref[row : row + 1, :] += edge


def received_scalars(lay, recv_ref):
    total = recv_ref[...]
    while total.shape[0] % 2 == 0:
        half = total.shape[0] // 2
        total = total[:half] + total[half:]
    total = jnp.sum(total, axis=0)
    return jnp.concatenate([total[i : i + 1] for i in range(lay.scalar_rows)], axis=1)


def coarse_tables(geo, lay, places):
    out = []
    for half in range(2):
        size = 32 if half else 16
        row = lax.broadcasted_iota(jnp.int32, (size, lay.lanes), 0)
        steps = [
            jnp.broadcast_to(places[3 * half + a : 3 * half + a + 1, :], row.shape)
            - geo.at[a].astype(F32)
            for a in range(3)
        ]
        if half:
            row_dx = jnp.where(row < 24, row // 8 - 1, (row - 24) // 2 - 1)
            row_dy = jnp.where(row < 24, 0, row % 2 * 2 - 1)
            row_dx = jnp.where(row < 30, row_dx, 1000)
        else:
            row_dx, row_dy = row // 3 - 1, row % 3 - 1
            row_dx = jnp.where(row < 9, row_dx, 1000)
        near = (steps[0] == row_dx.astype(F32)) & (steps[1] == row_dy.astype(F32))
        for dz in (-1.0, 0.0, 1.0):
            out.append(jnp.where(near & (steps[2] == dz), 1.0, 0.0))
    row = lax.broadcasted_iota(jnp.int32, (24, lay.lanes), 0)
    lane = lax.broadcasted_iota(jnp.int32, (24, lay.lanes), 1)
    out.append(jnp.where(lane == lay.plain + row // 8, 1.0, 0.0))
    return jnp.concatenate(out, axis=0)


HOT_ROWS = 48 + 96 + 24


def partial_sums(geo, v, sums, q_ref, hot_ref):
    first, last = v[0:BY], v[ROWS - BY : ROWS]
    inner = [v[x * BY : (x + 1) * BY] for x in range(1, BX - 1)]
    middle = tree([first * geo.x_share(0), last * geo.x_share(BX - 1), *inner])
    share = geo.y_share()
    for i, part in enumerate((0.5 * first, middle, 0.5 * last)):
        shared = part * share
        q_ref[8 * i : 8 * i + 8, :] = shared[0:8] + shared[8:16]
        q_ref[24 + 2 * i : 25 + 2 * i, :] = 0.5 * part[0:1]
        q_ref[25 + 2 * i : 26 + 2 * i, :] = 0.5 * part[BY - 1 : BY]
    q_ref[30:32, :] = jnp.zeros((2, BZ), F32)
    q = q_ref[...]
    own = jnp.sum(q * geo.z_share(q.shape, 1), axis=1, keepdims=True)
    below, above = 0.5 * q[:, 0:1], 0.5 * q[:, BZ - 1 : BZ]
    rows = hot_ref[48:80, :] * below + hot_ref[80:112, :] * own + hot_ref[112:144, :] * above
    rows = rows[0:8] + rows[8:16] + rows[16:24] + rows[24:32]
    if sums:
        rows = rows + plain_sums(sums, hot_ref)
    return jnp.sum(rows, axis=0, keepdims=True)


def plain_sums(sums, hot_ref):
    parts = []
    for i, total in enumerate(sums):
        at = 144 + 8 * i
        parts.append(hot_ref[at : at + 8, :] * jnp.sum(total, axis=1, keepdims=True))
    return tree(parts)


def spread(geo, values, hot_ref):
    below, own, above = [
        jnp.sum(hot_ref[16 * i : 16 * i + 16, :] * values, axis=1, keepdims=True) for i in range(3)
    ]
    lane = lax.broadcasted_iota(jnp.int32, (16, BZ), 1)
    rows = own * geo.z_share((16, BZ), 1)
    rows = rows + jnp.where(lane == 0, 0.5 * below, 0.0)
    rows = rows + jnp.where(lane == BZ - 1, 0.5 * above, 0.0)
    y = lax.broadcasted_iota(jnp.int32, (BY, BZ), 0)
    share = geo.y_share()
    planes = []
    for i in range(3):
        plane = share * rows[3 * i + 1 : 3 * i + 2]
        plane = plane + jnp.where(y == 0, 0.5 * rows[3 * i : 3 * i + 1], 0.0)
        planes.append(plane + jnp.where(y == BY - 1, 0.5 * rows[3 * i + 2 : 3 * i + 3], 0.0))
    out = [planes[1]] * BX
    out[0] = planes[1] * geo.x_share(0) + 0.5 * planes[0]
    out[BX - 1] = planes[1] * geo.x_share(BX - 1) + 0.5 * planes[2]
    return out


def with_coarse(lay, row, gram_ref):
    return row + jnp.dot(row, gram_ref[...], precision=HIGHEST, preferred_element_type=F32)


def coarse_inner(lay, row):
    lane = lax.broadcasted_iota(jnp.int32, row.shape, 1)
    both = row * pltpu.roll(row, lay.offset, 1)
    return jnp.sum(jnp.where(lane >= lay.offset, both, 0.0), axis=1, keepdims=True)


def all_rows(v):
    return tree([v[8 * i : 8 * i + 8] for i in range(ROWS // 8)])


def weighted_rows(geo, v):
    yz = geo.yz_weight()
    parts = []
    for x in range(BX):
        weight = geo.x_weight(x)
        part = v[x * BY : (x + 1) * BY]
        if not (isinstance(weight, float) and weight == 1.0):
            part = part * weight
        parts.append(part)
    total = tree(parts)
    total = total * yz
    return total[0:8] + total[8:16]


def weak_form(level, tab, zt, work):
    gx, gy, gz = along_x(level, "d"), along_y(level, "d", tab, work.at[0]), along_z(level, "d", zt)
    inv_norm = lax.rsqrt(1.0 + gx * gx + gy * gy + gz * gz)
    coef = bmass_of(tab) * (level * (1.0 - level) * inv_norm - INTERFACE_WIDTH)
    out = along_x(coef * gx, "t") + along_y(coef * gy, "t", tab, work.at[1])
    return out + along_z(coef * gz, "t", zt)


def stiffness(v, scaled, tab, zt, work, final):
    bm = bmass_of(tab)
    gx, gy, gz = along_x(v, "d"), along_y(v, "d", tab, work.at[0]), along_z(v, "d", zt)
    tx, ty, tz = scaled * gx, scaled * gy, scaled * gz
    if final:
        return None, all_rows(bm * v * v + (tx * gx + ty * gy + tz * gz))
    out = bm * v + along_x(tx, "t") + along_y(ty, "t", tab, work.at[1])
    out = out + along_z(tz, "t", zt)
    return out, all_rows(v * out)


def local_step(geo, lay, residual, dinv, scaled, state, image, refs):
    tab, zt, hot, u_ref, f_ref, send_ref, xs, ys, q_ref, state_ref, work, zwork, final = refs
    s_row, ts_row, gamma, curvature = state
    jacobi = residual * dinv
    planes = spread(geo, s_row, hot)
    u = jnp.concatenate([jacobi[x * BY : (x + 1) * BY] + planes[x] for x in range(BX)], axis=0)
    u_ref[...] = u
    local, energy = stiffness(u, scaled, tab, zt, work, final)
    sums = [weighted_rows(geo, residual * jacobi), energy]
    if image is not None:
        sums.append(weighted_rows(geo, u * image))
    ones = jnp.ones_like(s_row)
    coarse = coarse_inner(lay, s_row)
    state_ref[...] = jnp.concatenate(
        [s_row, ts_row, ones * gamma, ones * curvature, ones * coarse, jnp.zeros((3, lay.lanes), F32)],
        axis=0,
    )
    if final:
        scalars = jnp.sum(plain_sums(sums, hot), axis=0, keepdims=True)
        rows = [scalars[:, i * 128 : (i + 1) * 128] for i in range(lay.scalar_rows)]
        rows = jnp.concatenate(rows, axis=0)
        send_ref[...] = jnp.broadcast_to(rows[None], send_ref.shape)
        return
    scalars = partial_sums(geo, local, sums, q_ref, hot)
    local = local_sum_xy(local)
    f_ref[...] = local_sum_z(local)
    send_field(geo, lay, f_ref, local, zwork, scalars, send_ref, xs, ys)


def step_sizes(lay, recv_ref, state_ref, first):
    row = received_scalars(lay, recv_ref)
    lane = lax.broadcasted_iota(jnp.int32, row.shape, 1)

    def pick(which):
        return jnp.sum(jnp.where(lane == lay.plain + which, row, 0.0), axis=1, keepdims=True)

    gamma = pick(0) + state_ref[4:5, 0:1]
    if first:
        curvature = pick(1)
        beta = None
    else:
        beta = gamma / state_ref[2:3, 0:1]
        curvature = pick(1) + beta * (2.0 * pick(2) + beta * state_ref[3:4, 0:1])
    return row, gamma, curvature, beta, gamma / curvature


def build(mesh):
    sizes = tuple(int(mesh.shape[a]) for a in AXES)
    lay = Layout(sizes)
    steps = [face_steps(sizes[0]), face_steps(sizes[1])]
    nx, ny = len(steps[0]), len(steps[1])
    tab_np, zt_np = const_tables(), z_tables()
    number = np.arange(lay.lanes)
    places_np = np.full((8, lay.lanes), -9.0, np.float32)
    for half in range(2):
        lanes = slice(half * lay.offset, half * lay.offset + lay.devices)
        for a, place in enumerate(np.unravel_index(np.arange(lay.devices), sizes)):
            places_np[3 * half + a, lanes] = place
    block = jax.ShapeDtypeStruct((ROWS, BZ), F32)

    def like(*shape):
        return jax.ShapeDtypeStruct(shape, F32)

    def outgoing(fields):
        return (
            [like(lay.devices, lay.slot_rows, 128)]
            + [like(BY * fields, BZ)] * nx
            + [like(BX * fields, BZ)] * ny
        )

    def call(kernel, ins, outs, scratch, name, from_hbm=()):
        spec = pl.BlockSpec(memory_space=pltpu.VMEM)
        hbm = pl.BlockSpec(memory_space=pltpu.HBM)
        ins = [pltpu.with_memory_space_constraint(v, pltpu.HBM) if i in from_hbm else v for i, v in enumerate(ins)]
        return pl.pallas_call(
            kernel,
            out_shape=outs,
            in_specs=[hbm if i in from_hbm else spec for i in range(len(ins))],
            out_specs=[spec] * len(outs),
            scratch_shapes=scratch,
            compiler_params=pltpu.CompilerParams(vmem_limit_bytes=48 * 1024 * 1024),
            cost_estimate=pl.CostEstimate(flops=4000000, bytes_accessed=1000000, transcendentals=0),
            name=name,
        )(*ins)

    work = pltpu.VMEM((ROWS, BZ), F32)
    qrows = pltpu.VMEM((32, BZ), F32)
    pair = pltpu.VMEM((2, ROWS, BZ), F32)
    tiles = pltpu.VMEM((48, BZ), F32)

    def ring(v, axis, n, step):
        if step == "swap":
            pairs = [(0, 1), (1, 0)]
        else:
            d = 1 if step == "up" else n - 1
            pairs = [(i, (i + d) % n) for i in range(n)]
        return lax.ppermute(v, axis, pairs)

    def exchange(out):
        send, faces = out[0], out[1:]
        recv = lax.all_to_all(send, AXES, 0, 0, tiled=True)
        xs = [ring(faces[i], "gx", sizes[0], s) for i, s in enumerate(steps[0])]
        ys = [ring(faces[nx + i], "gy", sizes[1], s) for i, s in enumerate(steps[1])]
        return [recv, *xs, *ys]

    n_out = 1 + nx + ny

    def split(refs):
        return refs[0], refs[1 : 1 + nx], refs[1 + nx : 1 + nx + ny]

    def start_kernel(level_any, vel_any, tab_any, zt_any, *rest):
        send, xs, ys = split(rest[:n_out])
        f_ref, work, zwork = rest[n_out : n_out + 3]
        level_ref, zt_ref, tab_ref, vel_ref, sems = rest[n_out + 3 :]
        sources = (level_any, zt_any.at[0 : 2 * BZ], tab_any, vel_any)
        copies = [
            pltpu.make_async_copy(source, target, sems.at[i])
            for i, (source, target) in enumerate(zip(sources, (level_ref, zt_ref, tab_ref, vel_ref)))
        ]
        for copy in copies:
            copy.start()
        for copy in copies[:3]:
            copy.wait()
        geo = Geometry(sizes)
        level = level_ref[...]
        gx, gy, gz = along_x(level, "d"), along_y(level, "d", tab_ref, work.at[0]), along_z(level, "d", zt_ref)
        copies[3].wait()
        advect = bmass_of(tab_ref) * (vel_ref[0] * gx + vel_ref[1] * gy + vel_ref[2] * gz)
        finish(geo, advect, f_ref, zwork, send, xs, ys)

    def finish(geo, v, f_ref, zwork, send, xs, ys, scalars=None, extra=None):
        v = local_sum_xy(v)
        f_ref[...] = local_sum_z(v)
        if scalars is None:
            scalars = jnp.zeros((1, lay.lanes), F32)
        send_field(geo, lay, f_ref, v, zwork, scalars, send, xs, ys, extra)

    def source_kernel(vel_ref, source_ref, factor_ref, tab_ref, zt_ref, places_ref, _, *rest):
        slots, xs, ys = split(rest[:n_out])
        f_ref, hot_ref, row_ref, q_ref, work, zwork = rest[n_out:]
        geo = Geometry(sizes)
        bm = bmass_of(tab_ref)
        div = bm * source_ref[...] + along_x(bm * vel_ref[0], "t")
        div = div + along_y(bm * vel_ref[1], "t", tab_ref, work.at[1])
        div = div + along_z(bm * vel_ref[2], "t", zt_ref)
        hot_ref[...] = coarse_tables(geo, lay, places_ref)
        row_ref[0:1, :] = partial_sums(geo, div, [], q_ref, hot_ref)
        factor = factor_ref[...]
        if lay.lanes > lay.devices:
            pad = jnp.zeros((1, lay.lanes - lay.devices), F32)
            factor = jnp.concatenate([factor, pad], axis=1)
        row_ref[1:2, :] = factor
        row_ref[2:8, :] = jnp.zeros((6, lay.lanes), F32)
        div = local_sum_xy(div)
        f_ref[...] = local_sum_z(div)
        slots[...] = jnp.zeros(slots.shape, F32)
        fill_field(geo, lay, f_ref, div, zwork, slots, 1)
        slots[geo.me] = jnp.zeros(slots.shape[1:], F32)
        fill_faces(geo, lay, f_ref, xs, ys)

    def first_kernel(recv, *rest):
        xs, ys = rest[:nx], rest[nx : nx + ny]
        level_ref, fa_ref, tab_ref, zt_ref, row_ref = rest[nx + ny : nx + ny + 5]
        out = rest[nx + ny + 5 :]
        send, oxs, oys = split(out[:n_out])
        level_out, f_ref, w_ref, work, zwork = out[n_out:]
        geo = Geometry(sizes)
        received(geo, lay, fa_ref[...], recv, xs, ys, w_ref, 0)
        level = level_ref[...] - TIME_STEP * w_ref[...] * inverse_mass(geo, tab_ref)
        level_out[...] = level
        weak = weak_form(level, tab_ref, zt_ref, work)
        finish(geo, weak, f_ref, zwork, send, oxs, oys, row_ref[0:1, :], row_ref[1:2, :])

    def rhs_kernel(recv, *rest):
        xs, ys = rest[:nx], rest[nx : nx + ny]
        rows_ref, fd_ref, hot_ref, r_ref, s_ref, hot_out, w_ref, gram_ref = rest[nx + ny :]
        geo = Geometry(sizes)
        at = lay.scalar_rows + 2
        factor = [rows_ref[:, at + i, :] for i in range(lay.scalar_rows)]
        factor = jnp.concatenate(factor, axis=1)
        after = lay.lanes - lay.offset - lay.devices
        shifted = [jnp.zeros((lay.offset, lay.lanes), F32), factor]
        if after:
            shifted.append(jnp.zeros((after, lay.lanes), F32))
        plain = [factor, jnp.zeros((lay.lanes - lay.devices, lay.lanes), F32)]
        gram_ref[...] = lax.dot_general(
            jnp.concatenate(shifted, axis=0),
            jnp.concatenate(plain, axis=0),
            (((1,), (1,)), ((), ())),
            precision=HIGHEST,
            preferred_element_type=F32,
        )
        received(geo, lay, fd_ref[...], recv, xs, ys, w_ref, 1)
        r_ref[...] = SOURCE_SCALE * w_ref[...]
        row = with_coarse(lay, SOURCE_SCALE * received_scalars(lay, rows_ref), gram_ref)
        s_ref[...] = jnp.broadcast_to(row, s_ref.shape)
        hot_out[...] = hot_ref[...]
        hot_out[48:144, :] = with_coarse(lay, hot_ref[48:144, :], gram_ref)

    def new_level(geo, recv, xs, ys, level_ref, f_ref, tab_ref, w_ref):
        received(geo, lay, f_ref[...], recv, xs, ys, w_ref, 0)
        return level_ref[...] + PSEUDO_STEP * w_ref[...] * inverse_mass(geo, tab_ref)

    def sweep_kernel(recv, *rest):
        xs, ys = rest[:nx], rest[nx : nx + ny]
        level_ref, fin_ref, tab_ref, zt_ref = rest[nx + ny : nx + ny + 4]
        slots, sxs, sys = split(rest[nx + ny + 4 : nx + ny + 4 + n_out])
        out = rest[nx + ny + 4 + n_out :]
        send, oxs, oys = split(out[:n_out])
        level_out, f_ref, w_ref, work, zwork = out[n_out:]
        geo = Geometry(sizes)
        level = new_level(geo, recv, xs, ys, level_ref, fin_ref, tab_ref, w_ref)
        level_out[...] = level
        v = local_sum_xy(weak_form(level, tab_ref, zt_ref, work))
        f_ref[...] = local_sum_z(v)
        send[...] = slots[...]
        fill_field(geo, lay, f_ref, v, zwork, send, 0)
        send[geo.me] = slots[geo.me]
        fill_faces(geo, lay, f_ref, oxs, oys)
        for to, part in zip((*oxs, *oys), (*sxs, *sys)):
            to[BY : 2 * BY, :] = part[...]

    def diagonal_kernel(recv, *rest):
        xs, ys = rest[:nx], rest[nx : nx + ny]
        level_ref, fin_ref, tab_ref, zt_ref = rest[nx + ny : nx + ny + 4]
        out = rest[nx + ny + 4 :]
        send, oxs, oys = split(out[:n_out])
        level_out, f_ref, scaled_ref, w_ref, work, zwork = out[n_out:]
        geo = Geometry(sizes)
        level = new_level(geo, recv, xs, ys, level_ref, fin_ref, tab_ref, w_ref)
        level_out[...] = level
        bm = bmass_of(tab_ref)
        scaled = bm / (GAS_DENSITY + (1.0 - GAS_DENSITY) * jnp.clip(level, 0.0, 1.0))
        scaled_ref[...] = scaled
        diag = bm + along_x(scaled, "s") + along_y(scaled, "s", tab_ref, work.at[0])
        diag = diag + along_z(scaled, "s", zt_ref)
        finish(geo, diag, f_ref, zwork, send, oxs, oys)

    def solve_kernel(recv, *rest):
        xs, ys = rest[:nx], rest[nx : nx + ny]
        fin_ref, r_ref, scaled_ref, s_ref, tab_ref, zt_ref, hot_ref = rest[nx + ny : nx + ny + 7]
        out = rest[nx + ny + 7 :]
        send, oxs, oys = split(out[:n_out])
        dinv_ref, u_ref, f_ref, state_ref, w_ref, work, zwork, q_ref = out[n_out:]
        geo = Geometry(sizes)
        received(geo, lay, fin_ref[...], recv, xs, ys, w_ref, 0)
        dinv = 1.0 / w_ref[...]
        dinv_ref[...] = dinv
        zero = jnp.zeros((1, 1), F32)
        s_row = s_ref[0:1, :]
        state = (s_row, jnp.zeros_like(s_row), zero, zero)
        refs = (tab_ref, zt_ref, hot_ref, u_ref, f_ref, send, oxs, oys)
        local_step(
            geo, lay, r_ref[...], dinv, scaled_ref[...], state, None, (*refs, q_ref, state_ref, work, zwork, False)
        )

    def make_iterate(first, final):
        def iterate_kernel(recv, *rest):
            xs, ys = rest[:nx], rest[nx : nx + ny]
            n_in = 9 + (0 if first else 3)
            ins = rest[nx + ny : nx + ny + n_in]
            fin_ref, r_ref, u_in, dinv_ref, scaled_ref, state_in = ins[:6]
            tab_ref, zt_ref, hot_ref = ins[6:9]
            p_in, si_in, x_in = (None, None, None) if first else ins[9:12]
            out = rest[nx + ny + n_in :]
            if final:
                send, oxs, oys = out[0], (), ()
                out = out[1:]
                u_ref, state_ref, p_ref, x_ref, w_ref, work, zwork, q_ref = out
                f_ref = r_out = si_ref = None
            else:
                send, oxs, oys = split(out[:n_out])
                u_ref, state_ref, p_ref, x_ref, r_out, si_ref, f_ref, w_ref, work, zwork, q_ref = out[
                    n_out:
                ]
            geo = Geometry(sizes)
            row, gamma, curvature, beta, alpha = step_sizes(lay, recv, state_in, first)
            received(geo, lay, fin_ref[...], recv, xs, ys, w_ref, 0)
            image = w_ref[...]
            p = u_in[...]
            s_row, ts_row = state_in[0:1, :], row
            if not first:
                p = p + beta * p_in[...]
                image = image + beta * si_in[...]
                ts_row = ts_row + beta * state_in[1:2, :]
            p_ref[...] = p
            x_ref[...] = alpha * p if first else x_in[...] + alpha * p
            residual = r_ref[...] - alpha * image
            if not final:
                si_ref[...] = image
                r_out[...] = residual
            lane = lax.broadcasted_iota(jnp.int32, row.shape, 1)
            ts_row = jnp.where((lane < lay.devices) | (lane >= lay.offset), ts_row, 0.0)
            state = (s_row - alpha * ts_row, ts_row, gamma, curvature)
            refs = (tab_ref, zt_ref, hot_ref, u_ref, f_ref, send)
            local_step(
                geo,
                lay,
                residual,
                dinv_ref[...],
                scaled_ref[...],
                state,
                image,
                (*refs, oxs, oys, q_ref, state_ref, work, zwork, final),
            )

        return iterate_kernel

    def last_kernel(recv, state_in, u_in, p_in, x_in, out_ref):
        _, _, _, beta, alpha = step_sizes(lay, recv, state_in, False)
        out_ref[...] = x_in[...] + alpha * (u_in[...] + beta * p_in[...])

    def body(level_set, velocity, source, coarse_factor):
        level = level_set.reshape(ROWS, BZ)
        vel = velocity.reshape(3, ROWS, BZ)
        src = source.reshape(ROWS, BZ)
        tab, zt, places = jnp.asarray(tab_np), jnp.asarray(zt_np), jnp.asarray(places_np)
        out = call(
            start_kernel,
            [level, vel, tab, zt],
            outgoing(1) + [block],
            [pair, tiles]
            + [pltpu.VMEM(a, d) for a, d in ((level.shape, F32), ((2 * BZ, 2 * BZ), BF16), (tab.shape, F32), (vel.shape, F32))]
            + [pltpu.SemaphoreType.DMA((4,))],
            "advect",
            range(4),
        )
        fa = out[n_out]
        got = exchange(out[:n_out])
        side = call(
            source_kernel,
            [vel, src, coarse_factor, tab, zt, places, fa],
            outgoing(1) + [block, like(HOT_ROWS, lay.lanes), like(8, lay.lanes)],
            [qrows, pair, tiles],
            "source",
        )
        fd, hot, row = side[n_out:]
        out = call(
            first_kernel,
            [*got, level, fa, tab, zt, row],
            outgoing(1) + [block, block],
            [work, pair, tiles],
            "sweep_first",
        )
        level, f = out[n_out:]
        got = rows = exchange(out[:n_out])
        out = call(
            sweep_kernel,
            [*got, level, f, tab, zt, *side[:n_out]],
            outgoing(2) + [block, block],
            [work, pair, tiles],
            "sweep",
        )
        level, f = out[n_out:]
        got = exchange(out[:n_out])
        residual, s_rows, hot = call(
            rhs_kernel,
            [*got, rows[0], fd, hot],
            [block, like(8, lay.lanes), like(HOT_ROWS, lay.lanes)],
            [work, pltpu.VMEM((lay.lanes, lay.lanes), F32)],
            "rhs",
        )
        out = call(
            diagonal_kernel,
            [*got, level, f, tab, zt],
            outgoing(1) + [block, block, block],
            [work, pair, tiles],
            "diagonal",
        )
        level, f, scaled = out[n_out:]
        got = exchange(out[:n_out])
        out = call(
            solve_kernel,
            [*got, f, residual, scaled, s_rows, tab, zt, hot],
            outgoing(1) + [block, block, block, like(8, lay.lanes)],
            [work, pair, tiles, qrows],
            "solve_start",
        )
        dinv, u, f, state = out[n_out:]
        p = image = x = None
        for step in range(ITERS - 1):
            first, final = step == 0, step == ITERS - 2
            got = exchange(out[:n_out])
            ins = [*got, f, residual, u, dinv, scaled, state, tab, zt, hot]
            if not first:
                ins += [p, image, x]
            fields = [block, like(8, lay.lanes), block, block]
            if final:
                outs = [like(lay.devices, lay.scalar_rows, 128)] + fields
            else:
                outs = outgoing(1) + fields + [block, block, block]
            out = call(make_iterate(first, final), ins, outs, [work, pair, tiles, qrows], "iterate")
            if final:
                u, state, p, x = out[1:]
            else:
                u, state, p, x, residual, image, f = out[n_out:]
        recv = lax.all_to_all(out[0], AXES, 0, 0, tiled=True)
        (x,) = call(last_kernel, [recv, state, u, p, x], [block], [], "pressure")
        return level.reshape(BX, BY, BZ), x.reshape(BX, BY, BZ)

    return body


def solution(mesh):
    in_specs = (
        P("gx", "gy", "gz"),
        P(None, "gx", "gy", "gz"),
        P("gx", "gy", "gz"),
        P(("gx", "gy", "gz"), None),
    )
    out_specs = (P("gx", "gy", "gz"), P("gx", "gy", "gz"))
    return jax.shard_map(
        build(mesh), mesh=mesh, in_specs=in_specs, out_specs=out_specs, check_vma=False
    )
```

```python
import jax
import jax.numpy as jnp
import ml_dtypes
import numpy as np
from jax import lax
from jax.experimental import pallas as pl
from jax.experimental.pallas import tpu as pltpu
from jax.sharding import PartitionSpec as P

NP = 8
ITERS = 6
AXES = ("gx", "gy", "gz")

GLL_POINTS = (
    -1.0,
    -0.8717401485096066,
    -0.5917001814331423,
    -0.2092992179024789,
    0.2092992179024789,
    0.5917001814331423,
    0.8717401485096066,
    1.0,
)
GLL_WEIGHTS = (
    0.03571428571428571,
    0.21070422714350603,
    0.3411226924835044,
    0.4124587946587038,
    0.4124587946587038,
    0.3411226924835044,
    0.21070422714350603,
    0.03571428571428571,
)
HIGHEST = lax.Precision.HIGHEST
TIME_STEP = 0.02
PSEUDO_STEP = 0.004
INTERFACE_WIDTH = 0.5
GAS_DENSITY = 0.1
SOURCE_SCALE = 20.0
F32 = jnp.float32
BF16 = jnp.bfloat16


def node_tables():
    points = np.array(GLL_POINTS)
    amount = points.shape[0]
    barycentric = np.ones(amount)
    for target in range(amount):
        for partner in range(amount):
            if partner != target:
                barycentric[target] = barycentric[target] / (points[target] - points[partner])
    derivative = np.zeros((amount, amount))
    for target in range(amount):
        for partner in range(amount):
            if partner != target:
                derivative[target, partner] = (
                    barycentric[partner] / barycentric[target] / (points[target] - points[partner])
                )
        derivative[target, target] = -np.sum(derivative[target])
    return derivative


DERIV = node_tables()
TRANS = DERIV.T.copy()
SQUARE = (DERIV * DERIV).T.copy()
WEIGHTS = np.array(GLL_WEIGHTS)

BX, BY, BZ = 16, 16, 128
ROWS = BX * BY


def split_bf16(matrix):
    full = matrix.astype(np.float32)
    high = full.astype(ml_dtypes.bfloat16)
    low = (full - high.astype(np.float32)).astype(ml_dtypes.bfloat16)
    return high, low


def const_tables():
    parts = []
    for matrix in (DERIV, TRANS, SQUARE):
        for column in matrix.T:
            parts.append(np.repeat(column[:, None], BZ, axis=1))
    wy = np.tile(WEIGHTS, BY // NP)
    wz = np.tile(WEIGHTS, BZ // NP)
    parts.append(wy[:, None] * wz[None, :])
    parts.append(1.0 / (wy[:, None] * wz[None, :]))
    return np.concatenate(parts, axis=0).astype(np.float32)


def z_tables():
    out = []
    for matrix in (DERIV, TRANS, SQUARE):
        high, low = split_bf16(np.kron(np.eye(BZ // NP), matrix.T))
        top = np.concatenate([high, low], axis=1)
        out += [top, np.concatenate([high, np.zeros_like(low)], axis=1)]
    return np.concatenate(out, axis=0)


KIND = {"d": 0, "t": 1, "s": 2}
MATS = {"d": DERIV, "t": TRANS, "s": SQUARE}


def along_x(v, kind):
    matrix = MATS[kind]
    sign = 1.0 if abs(matrix[7, 7] - matrix[0, 0]) < abs(matrix[7, 7] + matrix[0, 0]) else -1.0
    out = [None] * BX
    for e in range(BX // NP):
        part = [v[(e * NP + i) * BY : (e * NP + i + 1) * BY] for i in range(NP)]
        even = [part[j] + part[7 - j] for j in range(4)]
        odd = [part[j] - part[7 - j] for j in range(4)]
        for i in range(4):
            a = b = None
            for j in range(4):
                ca = float(0.5 * (matrix[i, j] + matrix[i, 7 - j]))
                cb = float(0.5 * (matrix[i, j] - matrix[i, 7 - j]))
                a = ca * even[j] if a is None else a + ca * even[j]
                b = cb * odd[j] if b is None else b + cb * odd[j]
            out[e * NP + i] = a + b
            out[e * NP + 7 - i] = a - b if sign > 0 else b - a
    return jnp.concatenate(out, axis=0)


def along_y(v, kind, tab, work):
    work[...] = v
    base = KIND[kind] * NP * NP
    columns = [tab[base + s * NP : base + (s + 1) * NP, :] for s in range(NP)]
    out = []
    for q in range(ROWS // NP):
        total = None
        for s in range(NP):
            part = columns[s] * work[NP * q + s : NP * q + s + 1, :]
            total = part if total is None else total + part
        out.append(total)
    return jnp.concatenate(out, axis=0)


def along_z(v, kind, zt):
    base = KIND[kind] * 2 * BZ
    vh = v.astype(BF16)
    vl = (v - vh.astype(F32)).astype(BF16)
    both = jnp.dot(
        jnp.concatenate([vh, vl], axis=1), zt[base : base + 2 * BZ, :], preferred_element_type=F32
    )
    return both[:, :BZ] + both[:, BZ:]


def bmass_of(tab):
    base = 3 * NP * NP
    yz = tab[base : base + BY, :]
    return jnp.concatenate([yz * float(WEIGHTS[x % NP]) for x in range(BX)], axis=0)


def local_sum_xy(v):
    parts = [v[x * BY : (x + 1) * BY] for x in range(BX)]
    for x in range(NP, BX, NP):
        both = parts[x - 1] + parts[x]
        parts[x - 1] = both
        parts[x] = both
    sub = lax.broadcasted_iota(jnp.int32, (NP, BZ), 0)
    out = []
    for x in range(BX):
        a, b = parts[x][:NP], parts[x][NP:]
        out.append(jnp.where(sub == NP - 1, a + pltpu.roll(b, NP - 1, 0), a))
        out.append(jnp.where(sub == 0, b + pltpu.roll(a, 1, 0), b))
    return jnp.concatenate(out, axis=0)


def local_sum_z(v):
    lane = lax.broadcasted_iota(jnp.int32, (NP, BZ), 1)
    last = (lane % NP == NP - 1) & (lane < BZ - 1)
    first = (lane % NP == 0) & (lane > 0)
    swap = jnp.where(last, lane + 1, jnp.where(first, lane - 1, lane))
    out = []
    for q in range(v.shape[0] // NP):
        part = v[NP * q : NP * q + NP]
        other = jnp.take_along_axis(part, swap, axis=1, mode="promise_in_bounds")
        out.append(part + jnp.where(last | first, other, 0.0))
    return jnp.concatenate(out, axis=0)


def tree(parts):
    while len(parts) > 1:
        rest = parts[len(parts) // 2 * 2 :]
        parts = [a + b for a, b in zip(parts[0::2], parts[1::2])] + rest
    return parts[0]


class Geometry:
    def __init__(self, sizes):
        self.sizes = sizes
        self.at = [lax.axis_index(a) for a in AXES]
        self.low = [g > 0 for g in self.at]
        self.high = [g < n - 1 for g, n in zip(self.at, sizes)]
        self.me = (self.at[0] * sizes[1] + self.at[1]) * sizes[2] + self.at[2]

    def neighbour(self, *step):
        ok = None
        number = self.me
        strides = (self.sizes[1] * self.sizes[2], self.sizes[2], 1)
        for a in range(3):
            if step[a]:
                there = self.high[a] if step[a] > 0 else self.low[a]
                ok = there if ok is None else jnp.logical_and(ok, there)
                number = number + step[a] * strides[a]
        return jnp.where(ok, number, self.me)

    def across(self, dy, dz):
        plane = self.sizes[1] * self.sizes[2]
        there = self.neighbour(0, dy, dz)
        other = jnp.where(self.at[0] == 0, there + plane, there - plane)
        return other if dy == 0 and dz == 0 else jnp.where(there == self.me, self.me, other)

    def x_sides(self):
        return (2,) if self.sizes[0] == 2 else (-1, 1)

    def beside(self, dx, dy, dz):
        return self.across(dy, dz) if dx == 2 else self.neighbour(dx, dy, dz)

    def half(self, flag):
        return jnp.where(flag, 0.5, 1.0).astype(F32)

    def x_share(self, x):
        if x == 0:
            return self.half(self.low[0])
        if x == BX - 1:
            return self.half(self.high[0])
        return None

    def y_share(self):
        row = lax.broadcasted_iota(jnp.int32, (BY, BZ), 0)
        one = jnp.where(row == 0, self.half(self.low[1]), 1.0)
        return jnp.where(row == BY - 1, self.half(self.high[1]), one)

    def z_share(self, shape, dim):
        lane = lax.broadcasted_iota(jnp.int32, shape, dim)
        one = jnp.where(lane == 0, self.half(self.low[2]), 1.0)
        return jnp.where(lane == BZ - 1, self.half(self.high[2]), one)

    def yz_weight(self):
        row = lax.broadcasted_iota(jnp.int32, (BY, BZ), 0)
        lane = lax.broadcasted_iota(jnp.int32, (BY, BZ), 1)
        inside_y = ((row % NP == 0) & (row > 0)) | ((row % NP == NP - 1) & (row < BY - 1))
        inside_z = ((lane % NP == 0) & (lane > 0)) | ((lane % NP == NP - 1) & (lane < BZ - 1))
        wy = jnp.where(inside_y, 0.5, self.y_share())
        wz = jnp.where(inside_z, 0.5, self.z_share((BY, BZ), 1))
        return wy * wz

    def x_weight(self, x):
        if x in (0, BX - 1):
            return self.x_share(x)
        return 0.5 if x % NP in (0, NP - 1) else 1.0


def inverse_mass(geo, tab):
    base = 3 * NP * NP + BY
    yz = tab[base : base + BY, :] * geo.yz_weight()
    return jnp.concatenate(
        [yz * (geo.x_weight(x) * float(1.0 / WEIGHTS[x % NP])) for x in range(BX)], axis=0
    )


def face_steps(n):
    return ("swap",) if n == 2 else ("up", "down")


class Layout:
    def __init__(self, sizes):
        self.sizes = sizes
        self.devices = sizes[0] * sizes[1] * sizes[2]
        self.plain = self.devices
        self.offset = self.devices + 8
        self.lanes = -(-(self.offset + self.devices) // 128) * 128
        self.scalar_rows = self.lanes // 128

        need = 2 * self.scalar_rows + 2
        self.slot_rows = 4 if need <= 4 else -(-need // 8) * 8

    def field_rows(self, k):
        return (0, self.scalar_rows + 2) if k else (self.scalar_rows, self.scalar_rows + 1)


def pick_faces(geo, axis, n, low, high):
    if n == 2:
        return [jnp.where(geo.at[axis] == 0, high, low)]
    return [high, low]


def tile_iota():
    return lax.broadcasted_iota(jnp.int32, (8, BZ), 0), lax.broadcasted_iota(jnp.int32, (8, BZ), 1)


def pack_z_faces(v, work):
    sub, lane = tile_iota()
    parts = [pltpu.roll(v[8 * q : 8 * q + 8], (2 * q + 1) % BZ, 1) for q in range(ROWS // 8)]
    width = 2
    while len(parts) > 1:
        pairs = zip(parts[0::2], parts[1::2])
        parts = [jnp.where(lane & width == 0, a, b) for a, b in pairs]
        width *= 2
    tile = parts[0]
    turns = (-1, 0, 1, 63, 64, 65)
    for i, a in enumerate(turns):
        work[8 * i : 8 * i + 8, :] = tile if a == 0 else pltpu.roll(tile, a % BZ, 1)
    line = lane[0:1]
    out = []
    for side in (1, 0):
        pair = []
        for r in range(2):
            total = None
            for g in range(4):
                e, h = g % 2, g // 2
                at = 8 * turns.index(e - side + 64 * h) + 4 * r + g
                part = work[at : at + 1, :]
                keep = (line % 2 == e) & (line // 64 == h)
                total = part if total is None else jnp.where(keep, part, total)
            pair.append(total)
        out.append(pair)
    return out


def unpack_z_faces(sides):
    sub, lane = tile_iota()
    low, high = [
        jnp.where(sub < 4, jnp.broadcast_to(s[0], (8, BZ)), jnp.broadcast_to(s[1], (8, BZ)))
        for s in sides
    ]
    tile = None
    for g in range(4):
        shift = g % 2 + 64 * (g // 2)
        a = high if shift == 0 else pltpu.roll(high, -shift % BZ, 1)
        b = low if shift == 1 else pltpu.roll(low, (1 - shift) % BZ, 1)
        part = jnp.where(lane % 2 == 0, a, b)
        tile = part if tile is None else jnp.where(sub % 4 == g, part, tile)
    return tile


def send_field(geo, lay, f_ref, z, work, scalars, send_ref, xs, ys, extra=None):
    rows = lay.slot_rows
    base = [scalars[:, i * 128 : (i + 1) * 128] for i in range(lay.scalar_rows)]
    base.append(jnp.zeros((2, 128), F32))
    if extra is not None:
        base += [extra[:, i * 128 : (i + 1) * 128] for i in range(lay.scalar_rows)]
    used = sum(b.shape[0] for b in base)
    if used < rows:
        base.append(jnp.zeros((rows - used, 128), F32))
    base = jnp.concatenate(base, axis=0)
    send_ref[...] = jnp.broadcast_to(base[None], (lay.devices, rows, 128))
    fill_field(geo, lay, f_ref, z, work, send_ref, 0)
    fill_faces(geo, lay, f_ref, xs, ys)
    send_ref[geo.me] = base


def fill_field(geo, lay, f_ref, z, work, send_ref, k):
    row0, row1 = lay.field_rows(k)
    pairs = pack_z_faces(z, work)
    for dz in (-1, 1):
        pair = pairs[0 if dz < 0 else 1]
        for dx in (0, *geo.x_sides()):
            for dy in (-1, 0, 1):
                there = geo.beside(dx, dy, dz)
                send_ref[there, row0 : row0 + 1, :] = pair[0]
                send_ref[there, row1 : row1 + 1, :] = pair[1]
    for dx in geo.x_sides():
        for dy in (-1, 1):
            low = BY - 1 if dy > 0 else 0
            high = low + (BX - 1) * BY
            if dx == 2:
                edge = jnp.where(geo.at[0] == 0, f_ref[high : high + 1, :], f_ref[low : low + 1, :])
            else:
                row = high if dx > 0 else low
                edge = f_ref[row : row + 1, :]
            send_ref[geo.beside(dx, dy, 0), row0 : row0 + 1, :] = edge


def fill_faces(geo, lay, f_ref, xs, ys):
    lowx, highx = f_ref[0:BY, :], f_ref[ROWS - BY : ROWS, :]
    for ref, face in zip(xs, pick_faces(geo, 0, lay.sizes[0], lowx, highx)):
        ref[0:BY, :] = face
    lowy = f_ref[pl.ds(0, BX, stride=BY), :]
    highy = f_ref[pl.ds(BY - 1, BX, stride=BY), :]
    for ref, face in zip(ys, pick_faces(geo, 1, lay.sizes[1], lowy, highy)):
        ref[0:BX, :] = face


def came_from(geo, axis, n, refs, k, size):
    if n == 2:
        face = refs[0][k * size : (k + 1) * size, :]
        return (
            jnp.where(geo.low[axis], face, 0.0),
            jnp.where(geo.high[axis], face, 0.0),
        )
    up = refs[0][k * size : (k + 1) * size, :]
    down = refs[1][k * size : (k + 1) * size, :]
    return jnp.where(geo.low[axis], up, 0.0), jnp.where(geo.high[axis], down, 0.0)


def received(geo, lay, f, recv_ref, xs, ys, w_ref, k):
    at = lay.field_rows(k)
    line = lax.broadcasted_iota(jnp.int32, (1, BZ), 1)
    sides = []
    for dz in (-1, 1):
        pair = []
        for r in range(2):
            total = None
            for dy in (0, 1 if r else -1):
                for dx in (0, *geo.x_sides()):
                    source = 1 - r if dy else r
                    part = recv_ref[geo.beside(dx, dy, dz), at[source] : at[source] + 1, :]
                    keep = None
                    shift = (60 * dx + 67 * dy) % BZ
                    if dx == 2:
                        first = jnp.where(geo.at[0] == 0, 60, 0)
                        keep = (line % 64 >= first) & (line % 64 < first + 4)
                        shift = jnp.where(geo.at[0] == 0, (60 + 67 * dy) % BZ, (67 * dy - 60) % BZ)
                    elif dx:
                        keep = line % 64 >= 60 if dx > 0 else line % 64 < 4
                    if dy > 0:
                        want = (line >= 64) & (line % 4 == 3)
                        keep = want if keep is None else keep & want
                    if dy < 0:
                        want = (line < 64) & (line % 4 == 0)
                        keep = want if keep is None else keep & want
                    if keep is not None:
                        part = jnp.where(keep, pltpu.roll(part, shift, 1), 0.0)
                    total = part if total is None else total + part
            pair.append(total)
        sides.append(pair)
    tile = unpack_z_faces(sides)
    _, lane = tile_iota()
    ends = (lane == 0) | (lane == BZ - 1)
    parts = []
    for q in range(ROWS // 8):
        part = pltpu.roll(tile, (BZ - 1 - 2 * q) % BZ, 1)
        parts.append(f[8 * q : 8 * q + 8] + jnp.where(ends, part, 0.0))
    w_ref[...] = jnp.concatenate(parts, axis=0)
    lowx, highx = came_from(geo, 0, lay.sizes[0], xs, k, BY)
    w_ref[0:BY, :] += lowx
    w_ref[ROWS - BY : ROWS, :] += highx
    lowy, highy = came_from(geo, 1, lay.sizes[1], ys, k, BX)
    w_ref[pl.ds(0, BX, stride=BY), :] += lowy
    w_ref[pl.ds(BY - 1, BX, stride=BY), :] += highy
    for dx in geo.x_sides():
        for dy in (-1, 1):
            edge = recv_ref[geo.beside(dx, dy, 0), at[0] : at[0] + 1, :]
            low = BY - 1 if dy > 0 else 0
            high = low + (BX - 1) * BY
            if dx == 2:
                w_ref[low : low + 1, :] += jnp.where(geo.at[0] == 0, 0.0, edge)
                w_ref[high : high + 1, :] += jnp.where(geo.at[0] == 0, edge, 0.0)
            else:
                row = high if dx > 0 else low
                w_ref[row : row + 1, :] += edge


def received_scalars(lay, recv_ref):
    total = recv_ref[...]
    while total.shape[0] % 2 == 0:
        half = total.shape[0] // 2
        total = total[:half] + total[half:]
    total = jnp.sum(total, axis=0)
    return jnp.concatenate([total[i : i + 1] for i in range(lay.scalar_rows)], axis=1)


def coarse_tables(geo, lay, places):
    out = []
    for half in range(2):
        size = 32 if half else 16
        row = lax.broadcasted_iota(jnp.int32, (size, lay.lanes), 0)
        steps = [
            jnp.broadcast_to(places[3 * half + a : 3 * half + a + 1, :], row.shape)
            - geo.at[a].astype(F32)
            for a in range(3)
        ]
        if half:
            row_dx = jnp.where(row < 24, row // 8 - 1, (row - 24) // 2 - 1)
            row_dy = jnp.where(row < 24, 0, row % 2 * 2 - 1)
            row_dx = jnp.where(row < 30, row_dx, 1000)
        else:
            row_dx, row_dy = row // 3 - 1, row % 3 - 1
            row_dx = jnp.where(row < 9, row_dx, 1000)
        near = (steps[0] == row_dx.astype(F32)) & (steps[1] == row_dy.astype(F32))
        for dz in (-1.0, 0.0, 1.0):
            out.append(jnp.where(near & (steps[2] == dz), 1.0, 0.0))
    row = lax.broadcasted_iota(jnp.int32, (24, lay.lanes), 0)
    lane = lax.broadcasted_iota(jnp.int32, (24, lay.lanes), 1)
    out.append(jnp.where(lane == lay.plain + row // 8, 1.0, 0.0))
    return jnp.concatenate(out, axis=0)


HOT_ROWS = 48 + 96 + 24


def partial_sums(geo, v, sums, q_ref, hot_ref):
    first, last = v[0:BY], v[ROWS - BY : ROWS]
    inner = [v[x * BY : (x + 1) * BY] for x in range(1, BX - 1)]
    middle = tree([first * geo.x_share(0), last * geo.x_share(BX - 1), *inner])
    share = geo.y_share()
    for i, part in enumerate((0.5 * first, middle, 0.5 * last)):
        shared = part * share
        q_ref[8 * i : 8 * i + 8, :] = shared[0:8] + shared[8:16]
        q_ref[24 + 2 * i : 25 + 2 * i, :] = 0.5 * part[0:1]
        q_ref[25 + 2 * i : 26 + 2 * i, :] = 0.5 * part[BY - 1 : BY]
    q_ref[30:32, :] = jnp.zeros((2, BZ), F32)
    q = q_ref[...]
    own = jnp.sum(q * geo.z_share(q.shape, 1), axis=1, keepdims=True)
    below, above = 0.5 * q[:, 0:1], 0.5 * q[:, BZ - 1 : BZ]
    rows = hot_ref[48:80, :] * below + hot_ref[80:112, :] * own + hot_ref[112:144, :] * above
    rows = rows[0:8] + rows[8:16] + rows[16:24] + rows[24:32]
    if sums:
        rows = rows + plain_sums(sums, hot_ref)
    return jnp.sum(rows, axis=0, keepdims=True)


def plain_sums(sums, hot_ref):
    parts = []
    for i, total in enumerate(sums):
        at = 144 + 8 * i
        parts.append(hot_ref[at : at + 8, :] * jnp.sum(total, axis=1, keepdims=True))
    return tree(parts)


def spread(geo, values, hot_ref):
    below, own, above = [
        jnp.sum(hot_ref[16 * i : 16 * i + 16, :] * values, axis=1, keepdims=True) for i in range(3)
    ]
    lane = lax.broadcasted_iota(jnp.int32, (16, BZ), 1)
    rows = own * geo.z_share((16, BZ), 1)
    rows = rows + jnp.where(lane == 0, 0.5 * below, 0.0)
    rows = rows + jnp.where(lane == BZ - 1, 0.5 * above, 0.0)
    y = lax.broadcasted_iota(jnp.int32, (BY, BZ), 0)
    share = geo.y_share()
    planes = []
    for i in range(3):
        plane = share * rows[3 * i + 1 : 3 * i + 2]
        plane = plane + jnp.where(y == 0, 0.5 * rows[3 * i : 3 * i + 1], 0.0)
        planes.append(plane + jnp.where(y == BY - 1, 0.5 * rows[3 * i + 2 : 3 * i + 3], 0.0))
    out = [planes[1]] * BX
    out[0] = planes[1] * geo.x_share(0) + 0.5 * planes[0]
    out[BX - 1] = planes[1] * geo.x_share(BX - 1) + 0.5 * planes[2]
    return out


def with_coarse(lay, row, gram_ref):
    return row + jnp.dot(row, gram_ref[...], precision=HIGHEST, preferred_element_type=F32)


def coarse_inner(lay, row):
    lane = lax.broadcasted_iota(jnp.int32, row.shape, 1)
    both = row * pltpu.roll(row, lay.offset, 1)
    return jnp.sum(jnp.where(lane >= lay.offset, both, 0.0), axis=1, keepdims=True)


def all_rows(v):
    return tree([v[8 * i : 8 * i + 8] for i in range(ROWS // 8)])


def weighted_rows(geo, v):
    yz = geo.yz_weight()
    parts = []
    for x in range(BX):
        weight = geo.x_weight(x)
        part = v[x * BY : (x + 1) * BY]
        if not (isinstance(weight, float) and weight == 1.0):
            part = part * weight
        parts.append(part)
    total = tree(parts)
    total = total * yz
    return total[0:8] + total[8:16]


def weak_form(level, tab, zt, work):
    gx, gy, gz = along_x(level, "d"), along_y(level, "d", tab, work.at[0]), along_z(level, "d", zt)
    inv_norm = lax.rsqrt(1.0 + gx * gx + gy * gy + gz * gz)
    coef = bmass_of(tab) * (level * (1.0 - level) * inv_norm - INTERFACE_WIDTH)
    out = along_x(coef * gx, "t") + along_y(coef * gy, "t", tab, work.at[1])
    return out + along_z(coef * gz, "t", zt)


def stiffness(v, scaled, tab, zt, work, final):
    bm = bmass_of(tab)
    gx, gy, gz = along_x(v, "d"), along_y(v, "d", tab, work.at[0]), along_z(v, "d", zt)
    tx, ty, tz = scaled * gx, scaled * gy, scaled * gz
    if final:
        return None, all_rows(bm * v * v + (tx * gx + ty * gy + tz * gz))
    out = bm * v + along_x(tx, "t") + along_y(ty, "t", tab, work.at[1])
    out = out + along_z(tz, "t", zt)
    return out, all_rows(v * out)


def local_step(geo, lay, residual, dinv, scaled, state, image, refs):
    tab, zt, hot, u_ref, f_ref, send_ref, xs, ys, q_ref, state_ref, work, zwork, final = refs
    s_row, ts_row, gamma, curvature = state
    jacobi = residual * dinv
    planes = spread(geo, s_row, hot)
    u = jnp.concatenate([jacobi[x * BY : (x + 1) * BY] + planes[x] for x in range(BX)], axis=0)
    u_ref[...] = u
    local, energy = stiffness(u, scaled, tab, zt, work, final)
    sums = [weighted_rows(geo, residual * jacobi), energy]
    if image is not None:
        sums.append(weighted_rows(geo, u * image))
    ones = jnp.ones_like(s_row)
    coarse = coarse_inner(lay, s_row)
    state_ref[...] = jnp.concatenate(
        [s_row, ts_row, ones * gamma, ones * curvature, ones * coarse, jnp.zeros((3, lay.lanes), F32)],
        axis=0,
    )
    if final:
        scalars = jnp.sum(plain_sums(sums, hot), axis=0, keepdims=True)
        rows = [scalars[:, i * 128 : (i + 1) * 128] for i in range(lay.scalar_rows)]
        rows = jnp.concatenate(rows, axis=0)
        send_ref[...] = jnp.broadcast_to(rows[None], send_ref.shape)
        return
    scalars = partial_sums(geo, local, sums, q_ref, hot)
    local = local_sum_xy(local)
    f_ref[...] = local_sum_z(local)
    send_field(geo, lay, f_ref, local, zwork, scalars, send_ref, xs, ys)


def step_sizes(lay, recv_ref, state_ref, first):
    row = received_scalars(lay, recv_ref)
    lane = lax.broadcasted_iota(jnp.int32, row.shape, 1)

    def pick(which):
        return jnp.sum(jnp.where(lane == lay.plain + which, row, 0.0), axis=1, keepdims=True)

    gamma = pick(0) + state_ref[4:5, 0:1]
    if first:
        curvature = pick(1)
        beta = None
    else:
        beta = gamma / state_ref[2:3, 0:1]
        curvature = pick(1) + beta * (2.0 * pick(2) + beta * state_ref[3:4, 0:1])
    return row, gamma, curvature, beta, gamma / curvature


def build(mesh):
    sizes = tuple(int(mesh.shape[a]) for a in AXES)
    lay = Layout(sizes)
    steps = [face_steps(sizes[0]), face_steps(sizes[1])]
    nx, ny = len(steps[0]), len(steps[1])
    tab_np, zt_np = const_tables(), z_tables()
    number = np.arange(lay.lanes)
    places_np = np.full((8, lay.lanes), -9.0, np.float32)
    for half in range(2):
        lanes = slice(half * lay.offset, half * lay.offset + lay.devices)
        for a, place in enumerate(np.unravel_index(np.arange(lay.devices), sizes)):
            places_np[3 * half + a, lanes] = place
    block = jax.ShapeDtypeStruct((ROWS, BZ), F32)

    def like(*shape):
        return jax.ShapeDtypeStruct(shape, F32)

    def outgoing(fields):
        return (
            [like(lay.devices, lay.slot_rows, 128)]
            + [like(BY * fields, BZ)] * nx
            + [like(BX * fields, BZ)] * ny
        )

    def call(kernel, ins, outs, scratch, name, from_hbm=()):
        spec = pl.BlockSpec(memory_space=pltpu.VMEM)
        hbm = pl.BlockSpec(memory_space=pltpu.HBM)
        ins = [pltpu.with_memory_space_constraint(v, pltpu.HBM) if i in from_hbm else v for i, v in enumerate(ins)]
        return pl.pallas_call(
            kernel,
            out_shape=outs,
            in_specs=[hbm if i in from_hbm else spec for i in range(len(ins))],
            out_specs=[spec] * len(outs),
            scratch_shapes=scratch,
            compiler_params=pltpu.CompilerParams(vmem_limit_bytes=48 * 1024 * 1024),
            cost_estimate=pl.CostEstimate(flops=4000000, bytes_accessed=1000000, transcendentals=0),
            name=name,
        )(*ins)

    work = pltpu.VMEM((ROWS, BZ), F32)
    qrows = pltpu.VMEM((32, BZ), F32)
    pair = pltpu.VMEM((2, ROWS, BZ), F32)
    tiles = pltpu.VMEM((48, BZ), F32)

    def ring(v, axis, n, step):
        if step == "swap":
            pairs = [(0, 1), (1, 0)]
        else:
            d = 1 if step == "up" else n - 1
            pairs = [(i, (i + d) % n) for i in range(n)]
        return lax.ppermute(v, axis, pairs)

    def exchange(out):
        send, faces = out[0], out[1:]
        recv = lax.all_to_all(send, AXES, 0, 0, tiled=True)
        xs = [ring(faces[i], "gx", sizes[0], s) for i, s in enumerate(steps[0])]
        ys = [ring(faces[nx + i], "gy", sizes[1], s) for i, s in enumerate(steps[1])]
        return [recv, *xs, *ys]

    n_out = 1 + nx + ny

    def split(refs):
        return refs[0], refs[1 : 1 + nx], refs[1 + nx : 1 + nx + ny]

    def start_kernel(level_any, vel_any, tab_any, zt_any, *rest):
        send, xs, ys = split(rest[:n_out])
        f_ref, work, zwork = rest[n_out : n_out + 3]
        level_ref, zt_ref, tab_ref, vel_ref, sems = rest[n_out + 3 :]
        sources = (level_any, zt_any.at[0 : 2 * BZ], tab_any, vel_any)
        copies = [
            pltpu.make_async_copy(source, target, sems.at[i])
            for i, (source, target) in enumerate(zip(sources, (level_ref, zt_ref, tab_ref, vel_ref)))
        ]
        for copy in copies:
            copy.start()
        for copy in copies[:3]:
            copy.wait()
        geo = Geometry(sizes)
        level = level_ref[...]
        gx, gy, gz = along_x(level, "d"), along_y(level, "d", tab_ref, work.at[0]), along_z(level, "d", zt_ref)
        copies[3].wait()
        advect = bmass_of(tab_ref) * (vel_ref[0] * gx + vel_ref[1] * gy + vel_ref[2] * gz)
        finish(geo, advect, f_ref, zwork, send, xs, ys)

    def finish(geo, v, f_ref, zwork, send, xs, ys, scalars=None, extra=None):
        v = local_sum_xy(v)
        f_ref[...] = local_sum_z(v)
        if scalars is None:
            scalars = jnp.zeros((1, lay.lanes), F32)
        send_field(geo, lay, f_ref, v, zwork, scalars, send, xs, ys, extra)

    def source_kernel(vel_ref, source_ref, factor_ref, tab_ref, zt_ref, places_ref, _, *rest):
        slots, xs, ys = split(rest[:n_out])
        f_ref, hot_ref, row_ref, q_ref, work, zwork = rest[n_out:]
        geo = Geometry(sizes)
        bm = bmass_of(tab_ref)
        div = bm * source_ref[...] + along_x(bm * vel_ref[0], "t")
        div = div + along_y(bm * vel_ref[1], "t", tab_ref, work.at[1])
        div = div + along_z(bm * vel_ref[2], "t", zt_ref)
        hot_ref[...] = coarse_tables(geo, lay, places_ref)
        row_ref[0:1, :] = partial_sums(geo, div, [], q_ref, hot_ref)
        factor = factor_ref[...]
        if lay.lanes > lay.devices:
            pad = jnp.zeros((1, lay.lanes - lay.devices), F32)
            factor = jnp.concatenate([factor, pad], axis=1)
        row_ref[1:2, :] = factor
        row_ref[2:8, :] = jnp.zeros((6, lay.lanes), F32)
        div = local_sum_xy(div)
        f_ref[...] = local_sum_z(div)
        slots[...] = jnp.zeros(slots.shape, F32)
        fill_field(geo, lay, f_ref, div, zwork, slots, 1)
        slots[geo.me] = jnp.zeros(slots.shape[1:], F32)
        fill_faces(geo, lay, f_ref, xs, ys)

    def first_kernel(recv, *rest):
        xs, ys = rest[:nx], rest[nx : nx + ny]
        level_ref, fa_ref, tab_ref, zt_ref, row_ref = rest[nx + ny : nx + ny + 5]
        out = rest[nx + ny + 5 :]
        send, oxs, oys = split(out[:n_out])
        level_out, f_ref, w_ref, work, zwork = out[n_out:]
        geo = Geometry(sizes)
        received(geo, lay, fa_ref[...], recv, xs, ys, w_ref, 0)
        level = level_ref[...] - TIME_STEP * w_ref[...] * inverse_mass(geo, tab_ref)
        level_out[...] = level
        weak = weak_form(level, tab_ref, zt_ref, work)
        finish(geo, weak, f_ref, zwork, send, oxs, oys, row_ref[0:1, :], row_ref[1:2, :])

    def rhs_kernel(recv, *rest):
        xs, ys = rest[:nx], rest[nx : nx + ny]
        rows_ref, fd_ref, hot_ref, r_ref, s_ref, hot_out, w_ref, gram_ref = rest[nx + ny :]
        geo = Geometry(sizes)
        at = lay.scalar_rows + 2
        factor = [rows_ref[:, at + i, :] for i in range(lay.scalar_rows)]
        factor = jnp.concatenate(factor, axis=1)
        after = lay.lanes - lay.offset - lay.devices
        shifted = [jnp.zeros((lay.offset, lay.lanes), F32), factor]
        if after:
            shifted.append(jnp.zeros((after, lay.lanes), F32))
        plain = [factor, jnp.zeros((lay.lanes - lay.devices, lay.lanes), F32)]
        gram_ref[...] = lax.dot_general(
            jnp.concatenate(shifted, axis=0),
            jnp.concatenate(plain, axis=0),
            (((1,), (1,)), ((), ())),
            precision=HIGHEST,
            preferred_element_type=F32,
        )
        received(geo, lay, fd_ref[...], recv, xs, ys, w_ref, 1)
        r_ref[...] = SOURCE_SCALE * w_ref[...]
        row = with_coarse(lay, SOURCE_SCALE * received_scalars(lay, rows_ref), gram_ref)
        s_ref[...] = jnp.broadcast_to(row, s_ref.shape)
        hot_out[...] = hot_ref[...]
        hot_out[48:144, :] = with_coarse(lay, hot_ref[48:144, :], gram_ref)

    def new_level(geo, recv, xs, ys, level_ref, f_ref, tab_ref, w_ref):
        received(geo, lay, f_ref[...], recv, xs, ys, w_ref, 0)
        return level_ref[...] + PSEUDO_STEP * w_ref[...] * inverse_mass(geo, tab_ref)

    def sweep_kernel(recv, *rest):
        xs, ys = rest[:nx], rest[nx : nx + ny]
        level_ref, fin_ref, tab_ref, zt_ref = rest[nx + ny : nx + ny + 4]
        slots, sxs, sys = split(rest[nx + ny + 4 : nx + ny + 4 + n_out])
        out = rest[nx + ny + 4 + n_out :]
        send, oxs, oys = split(out[:n_out])
        level_out, f_ref, w_ref, work, zwork = out[n_out:]
        geo = Geometry(sizes)
        level = new_level(geo, recv, xs, ys, level_ref, fin_ref, tab_ref, w_ref)
        level_out[...] = level
        v = local_sum_xy(weak_form(level, tab_ref, zt_ref, work))
        f_ref[...] = local_sum_z(v)
        send[...] = slots[...]
        fill_field(geo, lay, f_ref, v, zwork, send, 0)
        send[geo.me] = slots[geo.me]
        fill_faces(geo, lay, f_ref, oxs, oys)
        for to, part in zip((*oxs, *oys), (*sxs, *sys)):
            to[BY : 2 * BY, :] = part[...]

    def diagonal_kernel(recv, *rest):
        xs, ys = rest[:nx], rest[nx : nx + ny]
        level_ref, fin_ref, tab_ref, zt_ref = rest[nx + ny : nx + ny + 4]
        out = rest[nx + ny + 4 :]
        send, oxs, oys = split(out[:n_out])
        level_out, f_ref, scaled_ref, w_ref, work, zwork = out[n_out:]
        geo = Geometry(sizes)
        level = new_level(geo, recv, xs, ys, level_ref, fin_ref, tab_ref, w_ref)
        level_out[...] = level
        bm = bmass_of(tab_ref)
        scaled = bm / (GAS_DENSITY + (1.0 - GAS_DENSITY) * jnp.clip(level, 0.0, 1.0))
        scaled_ref[...] = scaled
        diag = bm + along_x(scaled, "s") + along_y(scaled, "s", tab_ref, work.at[0])
        diag = diag + along_z(scaled, "s", zt_ref)
        finish(geo, diag, f_ref, zwork, send, oxs, oys)

    def solve_kernel(recv, *rest):
        xs, ys = rest[:nx], rest[nx : nx + ny]
        fin_ref, r_ref, scaled_ref, s_ref, tab_ref, zt_ref, hot_ref = rest[nx + ny : nx + ny + 7]
        out = rest[nx + ny + 7 :]
        send, oxs, oys = split(out[:n_out])
        dinv_ref, u_ref, f_ref, state_ref, w_ref, work, zwork, q_ref = out[n_out:]
        geo = Geometry(sizes)
        received(geo, lay, fin_ref[...], recv, xs, ys, w_ref, 0)
        dinv = 1.0 / w_ref[...]
        dinv_ref[...] = dinv
        zero = jnp.zeros((1, 1), F32)
        s_row = s_ref[0:1, :]
        state = (s_row, jnp.zeros_like(s_row), zero, zero)
        refs = (tab_ref, zt_ref, hot_ref, u_ref, f_ref, send, oxs, oys)
        local_step(
            geo, lay, r_ref[...], dinv, scaled_ref[...], state, None, (*refs, q_ref, state_ref, work, zwork, False)
        )

    def make_iterate(first, final):
        def iterate_kernel(recv, *rest):
            xs, ys = rest[:nx], rest[nx : nx + ny]
            n_in = 9 + (0 if first else 3 if final else 1)
            ins = rest[nx + ny : nx + ny + n_in]
            fin_ref, r_ref, u_in, dinv_ref, scaled_ref, state_in = ins[:6]
            tab_ref, zt_ref, hot_ref = ins[6:9]
            si_in, p_in, x_in = (*ins[9:], None, None, None)[:3]
            out = rest[nx + ny + n_in :]
            if final:
                send, oxs, oys = out[0], (), ()
                out = out[1:]
                u_ref, state_ref, p_ref, x_ref, w_ref, work, zwork, q_ref = out
                f_ref = r_out = si_ref = None
            else:
                send, oxs, oys = split(out[:n_out])
                u_ref, state_ref, r_out, si_ref, f_ref, w_ref, work, zwork, q_ref = out[
                    n_out:
                ]
            geo = Geometry(sizes)
            row, gamma, curvature, beta, alpha = step_sizes(lay, recv, state_in, first)
            received(geo, lay, fin_ref[...], recv, xs, ys, w_ref, 0)
            image = w_ref[...]
            s_row, ts_row = state_in[0:1, :], row
            if not first:
                image = image + beta * si_in[...]
                ts_row = ts_row + beta * state_in[1:2, :]
            if final:
                p = u_in[...] + beta * p_in[...]
                p_ref[...] = p
                x_ref[...] = x_in[...] + alpha * p
            residual = r_ref[...] - alpha * image
            if not final:
                si_ref[...] = image
                r_out[...] = residual
            lane = lax.broadcasted_iota(jnp.int32, row.shape, 1)
            ts_row = jnp.where((lane < lay.devices) | (lane >= lay.offset), ts_row, 0.0)
            state = (s_row - alpha * ts_row, ts_row, gamma, curvature)
            refs = (tab_ref, zt_ref, hot_ref, u_ref, f_ref, send)
            local_step(
                geo,
                lay,
                residual,
                dinv_ref[...],
                scaled_ref[...],
                state,
                image,
                (*refs, oxs, oys, q_ref, state_ref, work, zwork, final),
            )

        return iterate_kernel

    def first_update_kernel(state_ref, u_in, p_ref, x_ref):
        p = u_in[...]
        p_ref[...] = p
        x_ref[...] = state_ref[2:3, 0:1] / state_ref[3:4, 0:1] * p

    def update_kernel(state_ref, u_in, old_ref, p_in, x_in, p_ref, x_ref):
        gamma = state_ref[2:3, 0:1]
        p = u_in[...] + gamma / old_ref[2:3, 0:1] * p_in[...]
        p_ref[...] = p
        x_ref[...] = x_in[...] + gamma / state_ref[3:4, 0:1] * p

    def last_kernel(recv, state_in, u_in, p_in, x_in, out_ref):
        _, _, _, beta, alpha = step_sizes(lay, recv, state_in, False)
        out_ref[...] = x_in[...] + alpha * (u_in[...] + beta * p_in[...])

    def body(level_set, velocity, source, coarse_factor):
        level = level_set.reshape(ROWS, BZ)
        vel = velocity.reshape(3, ROWS, BZ)
        src = source.reshape(ROWS, BZ)
        tab, zt, places = jnp.asarray(tab_np), jnp.asarray(zt_np), jnp.asarray(places_np)
        out = call(
            start_kernel,
            [level, vel, tab, zt],
            outgoing(1) + [block],
            [pair, tiles]
            + [pltpu.VMEM(a, d) for a, d in ((level.shape, F32), ((2 * BZ, 2 * BZ), BF16), (tab.shape, F32), (vel.shape, F32))]
            + [pltpu.SemaphoreType.DMA((4,))],
            "advect",
            range(4),
        )
        fa = out[n_out]
        got = exchange(out[:n_out])
        side = call(
            source_kernel,
            [vel, src, coarse_factor, tab, zt, places, fa],
            outgoing(1) + [block, like(HOT_ROWS, lay.lanes), like(8, lay.lanes)],
            [qrows, pair, tiles],
            "source",
        )
        fd, hot, row = side[n_out:]
        out = call(
            first_kernel,
            [*got, level, fa, tab, zt, row],
            outgoing(1) + [block, block],
            [work, pair, tiles],
            "sweep_first",
        )
        level, f = out[n_out:]
        got = rows = exchange(out[:n_out])
        out = call(
            sweep_kernel,
            [*got, level, f, tab, zt, *side[:n_out]],
            outgoing(2) + [block, block],
            [work, pair, tiles],
            "sweep",
        )
        level, f = out[n_out:]
        got = exchange(out[:n_out])
        residual, s_rows, hot = call(
            rhs_kernel,
            [*got, rows[0], fd, hot],
            [block, like(8, lay.lanes), like(HOT_ROWS, lay.lanes)],
            [work, pltpu.VMEM((lay.lanes, lay.lanes), F32)],
            "rhs",
        )
        out = call(
            diagonal_kernel,
            [*got, level, f, tab, zt],
            outgoing(1) + [block, block, block],
            [work, pair, tiles],
            "diagonal",
        )
        level, f, scaled = out[n_out:]
        got = exchange(out[:n_out])
        out = call(
            solve_kernel,
            [*got, f, residual, scaled, s_rows, tab, zt, hot],
            outgoing(1) + [block, block, block, like(8, lay.lanes)],
            [work, pair, tiles, qrows],
            "solve_start",
        )
        dinv, u, f, state = out[n_out:]
        p = image = x = None
        for step in range(ITERS - 1):
            first, final = step == 0, step == ITERS - 2
            got = exchange(out[:n_out])
            ins = [*got, f, residual, u, dinv, scaled, state, tab, zt, hot]
            if not first:
                ins.append(image)
            if final:
                ins += [p, x]
            fields = [block, like(8, lay.lanes), block, block]
            if final:
                outs = [like(lay.devices, lay.scalar_rows, 128)] + fields
            else:
                outs = outgoing(1) + fields + [block]
            out = call(make_iterate(first, final), ins, outs, [work, pair, tiles, qrows], "iterate")
            if final:
                u, state, p, x = out[1:]
            else:
                old, u_old = state, u
                u, state, residual, image, f = out[n_out:]
                more = [] if first else [old, p, x]
                kernel = first_update_kernel if first else update_kernel
                p, x = call(kernel, [state, u_old, *more], [block, block], [], "update")
        recv = lax.all_to_all(out[0], AXES, 0, 0, tiled=True)
        (x,) = call(last_kernel, [recv, state, u, p, x], [block], [], "pressure")
        return level.reshape(BX, BY, BZ), x.reshape(BX, BY, BZ)

    return body


def solution(mesh):
    in_specs = (
        P("gx", "gy", "gz"),
        P(None, "gx", "gy", "gz"),
        P("gx", "gy", "gz"),
        P(("gx", "gy", "gz"), None),
    )
    out_specs = (P("gx", "gy", "gz"), P("gx", "gy", "gz"))
    return jax.shard_map(
        build(mesh), mesh=mesh, in_specs=in_specs, out_specs=out_specs, check_vma=False
    )
```

```python
import jax
import jax.numpy as jnp
import ml_dtypes
import numpy as np
from jax import lax
from jax.experimental import pallas as pl
from jax.experimental.pallas import tpu as pltpu
from jax.sharding import PartitionSpec as P

NP = 8
ITERS = 6
AXES = ("gx", "gy", "gz")

GLL_POINTS = (
    -1.0,
    -0.8717401485096066,
    -0.5917001814331423,
    -0.2092992179024789,
    0.2092992179024789,
    0.5917001814331423,
    0.8717401485096066,
    1.0,
)
GLL_WEIGHTS = (
    0.03571428571428571,
    0.21070422714350603,
    0.3411226924835044,
    0.4124587946587038,
    0.4124587946587038,
    0.3411226924835044,
    0.21070422714350603,
    0.03571428571428571,
)
HIGHEST = lax.Precision.HIGHEST
TIME_STEP = 0.02
PSEUDO_STEP = 0.004
INTERFACE_WIDTH = 0.5
GAS_DENSITY = 0.1
SOURCE_SCALE = 20.0
F32 = jnp.float32
BF16 = jnp.bfloat16


def node_tables():
    points = np.array(GLL_POINTS)
    amount = points.shape[0]
    barycentric = np.ones(amount)
    for target in range(amount):
        for partner in range(amount):
            if partner != target:
                barycentric[target] = barycentric[target] / (points[target] - points[partner])
    derivative = np.zeros((amount, amount))
    for target in range(amount):
        for partner in range(amount):
            if partner != target:
                derivative[target, partner] = (
                    barycentric[partner] / barycentric[target] / (points[target] - points[partner])
                )
        derivative[target, target] = -np.sum(derivative[target])
    return derivative


DERIV = node_tables()
TRANS = DERIV.T.copy()
SQUARE = (DERIV * DERIV).T.copy()
WEIGHTS = np.array(GLL_WEIGHTS)

BX, BY, BZ = 16, 16, 128
ROWS = BX * BY


def split_bf16(matrix):
    full = matrix.astype(np.float32)
    high = full.astype(ml_dtypes.bfloat16)
    low = (full - high.astype(np.float32)).astype(ml_dtypes.bfloat16)
    return high, low


def const_tables():
    parts = []
    for matrix in (DERIV, TRANS, SQUARE):
        for column in matrix.T:
            parts.append(np.repeat(column[:, None], BZ, axis=1))
    wy = np.tile(WEIGHTS, BY // NP)
    wz = np.tile(WEIGHTS, BZ // NP)
    parts.append(wy[:, None] * wz[None, :])
    parts.append(1.0 / (wy[:, None] * wz[None, :]))
    return np.concatenate(parts, axis=0).astype(np.float32)


def z_tables():
    out = []
    for matrix in (DERIV, TRANS, SQUARE):
        high, low = split_bf16(np.kron(np.eye(BZ // NP), matrix.T))
        top = np.concatenate([high, low], axis=1)
        out += [top, np.concatenate([high, np.zeros_like(low)], axis=1)]
    return np.concatenate(out, axis=0)


KIND = {"d": 0, "t": 1, "s": 2}
MATS = {"d": DERIV, "t": TRANS, "s": SQUARE}


def along_x(v, kind):
    matrix = MATS[kind]
    sign = 1.0 if abs(matrix[7, 7] - matrix[0, 0]) < abs(matrix[7, 7] + matrix[0, 0]) else -1.0
    out = [None] * BX
    for e in range(BX // NP):
        part = [v[(e * NP + i) * BY : (e * NP + i + 1) * BY] for i in range(NP)]
        even = [part[j] + part[7 - j] for j in range(4)]
        odd = [part[j] - part[7 - j] for j in range(4)]
        for i in range(4):
            a = b = None
            for j in range(4):
                ca = float(0.5 * (matrix[i, j] + matrix[i, 7 - j]))
                cb = float(0.5 * (matrix[i, j] - matrix[i, 7 - j]))
                a = ca * even[j] if a is None else a + ca * even[j]
                b = cb * odd[j] if b is None else b + cb * odd[j]
            out[e * NP + i] = a + b
            out[e * NP + 7 - i] = a - b if sign > 0 else b - a
    return jnp.concatenate(out, axis=0)


def along_y(v, kind, tab, work):
    work[...] = v
    base = KIND[kind] * NP * NP
    columns = [tab[base + s * NP : base + (s + 1) * NP, :] for s in range(NP)]
    out = []
    for q in range(ROWS // NP):
        total = None
        for s in range(NP):
            part = columns[s] * work[NP * q + s : NP * q + s + 1, :]
            total = part if total is None else total + part
        out.append(total)
    return jnp.concatenate(out, axis=0)


def along_z(v, kind, zt):
    base = KIND[kind] * 2 * BZ
    vh = v.astype(BF16)
    vl = (v - vh.astype(F32)).astype(BF16)
    both = jnp.dot(
        jnp.concatenate([vh, vl], axis=1), zt[base : base + 2 * BZ, :], preferred_element_type=F32
    )
    return both[:, :BZ] + both[:, BZ:]


def bmass_of(tab):
    base = 3 * NP * NP
    yz = tab[base : base + BY, :]
    return jnp.concatenate([yz * float(WEIGHTS[x % NP]) for x in range(BX)], axis=0)


def local_sum_xy(v):
    parts = [v[x * BY : (x + 1) * BY] for x in range(BX)]
    for x in range(NP, BX, NP):
        both = parts[x - 1] + parts[x]
        parts[x - 1] = both
        parts[x] = both
    sub = lax.broadcasted_iota(jnp.int32, (NP, BZ), 0)
    out = []
    for x in range(BX):
        a, b = parts[x][:NP], parts[x][NP:]
        out.append(jnp.where(sub == NP - 1, a + pltpu.roll(b, NP - 1, 0), a))
        out.append(jnp.where(sub == 0, b + pltpu.roll(a, 1, 0), b))
    return jnp.concatenate(out, axis=0)


def local_sum_z(v):
    lane = lax.broadcasted_iota(jnp.int32, (NP, BZ), 1)
    last = (lane % NP == NP - 1) & (lane < BZ - 1)
    first = (lane % NP == 0) & (lane > 0)
    swap = jnp.where(last, lane + 1, jnp.where(first, lane - 1, lane))
    out = []
    for q in range(v.shape[0] // NP):
        part = v[NP * q : NP * q + NP]
        other = jnp.take_along_axis(part, swap, axis=1, mode="promise_in_bounds")
        out.append(part + jnp.where(last | first, other, 0.0))
    return jnp.concatenate(out, axis=0)


def tree(parts):
    while len(parts) > 1:
        rest = parts[len(parts) // 2 * 2 :]
        parts = [a + b for a, b in zip(parts[0::2], parts[1::2])] + rest
    return parts[0]


class Geometry:
    def __init__(self, sizes):
        self.sizes = sizes
        self.at = [lax.axis_index(a) for a in AXES]
        self.low = [g > 0 for g in self.at]
        self.high = [g < n - 1 for g, n in zip(self.at, sizes)]
        self.me = (self.at[0] * sizes[1] + self.at[1]) * sizes[2] + self.at[2]

    def neighbour(self, *step):
        ok = None
        number = self.me
        strides = (self.sizes[1] * self.sizes[2], self.sizes[2], 1)
        for a in range(3):
            if step[a]:
                there = self.high[a] if step[a] > 0 else self.low[a]
                ok = there if ok is None else jnp.logical_and(ok, there)
                number = number + step[a] * strides[a]
        return jnp.where(ok, number, self.me)

    def across(self, dy, dz):
        plane = self.sizes[1] * self.sizes[2]
        there = self.neighbour(0, dy, dz)
        other = jnp.where(self.at[0] == 0, there + plane, there - plane)
        return other if dy == 0 and dz == 0 else jnp.where(there == self.me, self.me, other)

    def x_sides(self):
        return (2,) if self.sizes[0] == 2 else (-1, 1)

    def beside(self, dx, dy, dz):
        return self.across(dy, dz) if dx == 2 else self.neighbour(dx, dy, dz)

    def half(self, flag):
        return jnp.where(flag, 0.5, 1.0).astype(F32)

    def x_share(self, x):
        if x == 0:
            return self.half(self.low[0])
        if x == BX - 1:
            return self.half(self.high[0])
        return None

    def y_share(self):
        row = lax.broadcasted_iota(jnp.int32, (BY, BZ), 0)
        one = jnp.where(row == 0, self.half(self.low[1]), 1.0)
        return jnp.where(row == BY - 1, self.half(self.high[1]), one)

    def z_share(self, shape, dim):
        lane = lax.broadcasted_iota(jnp.int32, shape, dim)
        one = jnp.where(lane == 0, self.half(self.low[2]), 1.0)
        return jnp.where(lane == BZ - 1, self.half(self.high[2]), one)

    def yz_weight(self):
        row = lax.broadcasted_iota(jnp.int32, (BY, BZ), 0)
        lane = lax.broadcasted_iota(jnp.int32, (BY, BZ), 1)
        inside_y = ((row % NP == 0) & (row > 0)) | ((row % NP == NP - 1) & (row < BY - 1))
        inside_z = ((lane % NP == 0) & (lane > 0)) | ((lane % NP == NP - 1) & (lane < BZ - 1))
        wy = jnp.where(inside_y, 0.5, self.y_share())
        wz = jnp.where(inside_z, 0.5, self.z_share((BY, BZ), 1))
        return wy * wz

    def x_weight(self, x):
        if x in (0, BX - 1):
            return self.x_share(x)
        return 0.5 if x % NP in (0, NP - 1) else 1.0


def inverse_mass(geo, tab):
    base = 3 * NP * NP + BY
    yz = tab[base : base + BY, :] * geo.yz_weight()
    return jnp.concatenate(
        [yz * (geo.x_weight(x) * float(1.0 / WEIGHTS[x % NP])) for x in range(BX)], axis=0
    )


def face_steps(n):
    return ("swap",) if n == 2 else ("up", "down")


class Layout:
    def __init__(self, sizes):
        self.sizes = sizes
        self.devices = sizes[0] * sizes[1] * sizes[2]
        self.plain = self.devices
        self.offset = self.devices + 8
        self.lanes = -(-(self.offset + self.devices) // 128) * 128
        self.scalar_rows = self.lanes // 128

        need = 2 * self.scalar_rows + 2
        self.slot_rows = 4 if need <= 4 else -(-need // 8) * 8

    def field_rows(self, k):
        return (0, self.scalar_rows + 2) if k else (self.scalar_rows, self.scalar_rows + 1)


def pick_faces(geo, axis, n, low, high):
    if n == 2:
        return [jnp.where(geo.at[axis] == 0, high, low)]
    return [high, low]


def tile_iota():
    return lax.broadcasted_iota(jnp.int32, (8, BZ), 0), lax.broadcasted_iota(jnp.int32, (8, BZ), 1)


def pack_z_faces(v, work):
    sub, lane = tile_iota()
    parts = [pltpu.roll(v[8 * q : 8 * q + 8], (2 * q + 1) % BZ, 1) for q in range(ROWS // 8)]
    width = 2
    while len(parts) > 1:
        pairs = zip(parts[0::2], parts[1::2])
        parts = [jnp.where(lane & width == 0, a, b) for a, b in pairs]
        width *= 2
    tile = parts[0]
    turns = (-1, 0, 1, 63, 64, 65)
    for i, a in enumerate(turns):
        work[8 * i : 8 * i + 8, :] = tile if a == 0 else pltpu.roll(tile, a % BZ, 1)
    line = lane[0:1]
    out = []
    for side in (1, 0):
        pair = []
        for r in range(2):
            total = None
            for g in range(4):
                e, h = g % 2, g // 2
                at = 8 * turns.index(e - side + 64 * h) + 4 * r + g
                part = work[at : at + 1, :]
                keep = (line % 2 == e) & (line // 64 == h)
                total = part if total is None else jnp.where(keep, part, total)
            pair.append(total)
        out.append(pair)
    return out


def unpack_z_faces(sides):
    sub, lane = tile_iota()
    low, high = [
        jnp.where(sub < 4, jnp.broadcast_to(s[0], (8, BZ)), jnp.broadcast_to(s[1], (8, BZ)))
        for s in sides
    ]
    tile = None
    for g in range(4):
        shift = g % 2 + 64 * (g // 2)
        a = high if shift == 0 else pltpu.roll(high, -shift % BZ, 1)
        b = low if shift == 1 else pltpu.roll(low, (1 - shift) % BZ, 1)
        part = jnp.where(lane % 2 == 0, a, b)
        tile = part if tile is None else jnp.where(sub % 4 == g, part, tile)
    return tile


def send_field(geo, lay, f_ref, z, work, scalars, send_ref, xs, ys, extra=None):
    rows = lay.slot_rows
    base = [scalars[:, i * 128 : (i + 1) * 128] for i in range(lay.scalar_rows)]
    base.append(jnp.zeros((2, 128), F32))
    if extra is not None:
        base += [extra[:, i * 128 : (i + 1) * 128] for i in range(lay.scalar_rows)]
    used = sum(b.shape[0] for b in base)
    if used < rows:
        base.append(jnp.zeros((rows - used, 128), F32))
    base = jnp.concatenate(base, axis=0)
    send_ref[...] = jnp.broadcast_to(base[None], (lay.devices, rows, 128))
    fill_field(geo, lay, f_ref, z, work, send_ref, 0)
    fill_faces(geo, lay, f_ref, xs, ys)
    send_ref[geo.me] = base


def fill_field(geo, lay, f_ref, z, work, send_ref, k):
    row0, row1 = lay.field_rows(k)
    pairs = pack_z_faces(z, work)
    for dz in (-1, 1):
        pair = pairs[0 if dz < 0 else 1]
        for dx in (0, *geo.x_sides()):
            for dy in (-1, 0, 1):
                there = geo.beside(dx, dy, dz)
                send_ref[there, row0 : row0 + 1, :] = pair[0]
                send_ref[there, row1 : row1 + 1, :] = pair[1]
    for dx in geo.x_sides():
        for dy in (-1, 1):
            low = BY - 1 if dy > 0 else 0
            high = low + (BX - 1) * BY
            if dx == 2:
                edge = jnp.where(geo.at[0] == 0, f_ref[high : high + 1, :], f_ref[low : low + 1, :])
            else:
                row = high if dx > 0 else low
                edge = f_ref[row : row + 1, :]
            send_ref[geo.beside(dx, dy, 0), row0 : row0 + 1, :] = edge


def fill_faces(geo, lay, f_ref, xs, ys):
    lowx, highx = f_ref[0:BY, :], f_ref[ROWS - BY : ROWS, :]
    for ref, face in zip(xs, pick_faces(geo, 0, lay.sizes[0], lowx, highx)):
        ref[0:BY, :] = face
    lowy = f_ref[pl.ds(0, BX, stride=BY), :]
    highy = f_ref[pl.ds(BY - 1, BX, stride=BY), :]
    for ref, face in zip(ys, pick_faces(geo, 1, lay.sizes[1], lowy, highy)):
        ref[0:BX, :] = face


def came_from(geo, axis, n, refs, k, size):
    if n == 2:
        face = refs[0][k * size : (k + 1) * size, :]
        return (
            jnp.where(geo.low[axis], face, 0.0),
            jnp.where(geo.high[axis], face, 0.0),
        )
    up = refs[0][k * size : (k + 1) * size, :]
    down = refs[1][k * size : (k + 1) * size, :]
    return jnp.where(geo.low[axis], up, 0.0), jnp.where(geo.high[axis], down, 0.0)


def received(geo, lay, f, recv_ref, xs, ys, w_ref, k):
    at = lay.field_rows(k)
    line = lax.broadcasted_iota(jnp.int32, (1, BZ), 1)
    sides = []
    for dz in (-1, 1):
        pair = []
        for r in range(2):
            total = None
            for dy in (0, 1 if r else -1):
                for dx in (0, *geo.x_sides()):
                    source = 1 - r if dy else r
                    part = recv_ref[geo.beside(dx, dy, dz), at[source] : at[source] + 1, :]
                    keep = None
                    shift = (60 * dx + 67 * dy) % BZ
                    if dx == 2:
                        first = jnp.where(geo.at[0] == 0, 60, 0)
                        keep = (line % 64 >= first) & (line % 64 < first + 4)
                        shift = jnp.where(geo.at[0] == 0, (60 + 67 * dy) % BZ, (67 * dy - 60) % BZ)
                    elif dx:
                        keep = line % 64 >= 60 if dx > 0 else line % 64 < 4
                    if dy > 0:
                        want = (line >= 64) & (line % 4 == 3)
                        keep = want if keep is None else keep & want
                    if dy < 0:
                        want = (line < 64) & (line % 4 == 0)
                        keep = want if keep is None else keep & want
                    if keep is not None:
                        part = jnp.where(keep, pltpu.roll(part, shift, 1), 0.0)
                    total = part if total is None else total + part
            pair.append(total)
        sides.append(pair)
    tile = unpack_z_faces(sides)
    _, lane = tile_iota()
    ends = (lane == 0) | (lane == BZ - 1)
    parts = []
    for q in range(ROWS // 8):
        part = pltpu.roll(tile, (BZ - 1 - 2 * q) % BZ, 1)
        parts.append(f[8 * q : 8 * q + 8] + jnp.where(ends, part, 0.0))
    w_ref[...] = jnp.concatenate(parts, axis=0)
    lowx, highx = came_from(geo, 0, lay.sizes[0], xs, k, BY)
    w_ref[0:BY, :] += lowx
    w_ref[ROWS - BY : ROWS, :] += highx
    lowy, highy = came_from(geo, 1, lay.sizes[1], ys, k, BX)
    w_ref[pl.ds(0, BX, stride=BY), :] += lowy
    w_ref[pl.ds(BY - 1, BX, stride=BY), :] += highy
    for dx in geo.x_sides():
        for dy in (-1, 1):
            edge = recv_ref[geo.beside(dx, dy, 0), at[0] : at[0] + 1, :]
            low = BY - 1 if dy > 0 else 0
            high = low + (BX - 1) * BY
            if dx == 2:
                w_ref[low : low + 1, :] += jnp.where(geo.at[0] == 0, 0.0, edge)
                w_ref[high : high + 1, :] += jnp.where(geo.at[0] == 0, edge, 0.0)
            else:
                row = high if dx > 0 else low
                w_ref[row : row + 1, :] += edge


def received_scalars(lay, recv_ref):
    total = recv_ref[...]
    while total.shape[0] % 2 == 0:
        half = total.shape[0] // 2
        total = total[:half] + total[half:]
    total = jnp.sum(total, axis=0)
    return jnp.concatenate([total[i : i + 1] for i in range(lay.scalar_rows)], axis=1)


def coarse_tables(geo, lay, places):
    out = []
    for half in range(2):
        size = 32 if half else 16
        row = lax.broadcasted_iota(jnp.int32, (size, lay.lanes), 0)
        steps = [
            jnp.broadcast_to(places[3 * half + a : 3 * half + a + 1, :], row.shape)
            - geo.at[a].astype(F32)
            for a in range(3)
        ]
        if half:
            row_dx = jnp.where(row < 24, row // 8 - 1, (row - 24) // 2 - 1)
            row_dy = jnp.where(row < 24, 0, row % 2 * 2 - 1)
            row_dx = jnp.where(row < 30, row_dx, 1000)
        else:
            row_dx, row_dy = row // 3 - 1, row % 3 - 1
            row_dx = jnp.where(row < 9, row_dx, 1000)
        near = (steps[0] == row_dx.astype(F32)) & (steps[1] == row_dy.astype(F32))
        for dz in (-1.0, 0.0, 1.0):
            out.append(jnp.where(near & (steps[2] == dz), 1.0, 0.0))
    row = lax.broadcasted_iota(jnp.int32, (24, lay.lanes), 0)
    lane = lax.broadcasted_iota(jnp.int32, (24, lay.lanes), 1)
    out.append(jnp.where(lane == lay.plain + row // 8, 1.0, 0.0))
    return jnp.concatenate(out, axis=0)


HOT_ROWS = 48 + 96 + 24


def partial_sums(geo, v, sums, q_ref, hot_ref):
    first, last = v[0:BY], v[ROWS - BY : ROWS]
    inner = [v[x * BY : (x + 1) * BY] for x in range(1, BX - 1)]
    middle = tree([first * geo.x_share(0), last * geo.x_share(BX - 1), *inner])
    share = geo.y_share()
    for i, part in enumerate((0.5 * first, middle, 0.5 * last)):
        shared = part * share
        q_ref[8 * i : 8 * i + 8, :] = shared[0:8] + shared[8:16]
        q_ref[24 + 2 * i : 25 + 2 * i, :] = 0.5 * part[0:1]
        q_ref[25 + 2 * i : 26 + 2 * i, :] = 0.5 * part[BY - 1 : BY]
    q_ref[30:32, :] = jnp.zeros((2, BZ), F32)
    q = q_ref[...]
    own = jnp.sum(q * geo.z_share(q.shape, 1), axis=1, keepdims=True)
    below, above = 0.5 * q[:, 0:1], 0.5 * q[:, BZ - 1 : BZ]
    rows = hot_ref[48:80, :] * below + hot_ref[80:112, :] * own + hot_ref[112:144, :] * above
    rows = rows[0:8] + rows[8:16] + rows[16:24] + rows[24:32]
    if sums:
        rows = rows + plain_sums(sums, hot_ref)
    return jnp.sum(rows, axis=0, keepdims=True)


def plain_sums(sums, hot_ref):
    parts = []
    for i, total in enumerate(sums):
        at = 144 + 8 * i
        parts.append(hot_ref[at : at + 8, :] * jnp.sum(total, axis=1, keepdims=True))
    return tree(parts)


def spread(geo, values, hot_ref):
    below, own, above = [
        jnp.sum(hot_ref[16 * i : 16 * i + 16, :] * values, axis=1, keepdims=True) for i in range(3)
    ]
    lane = lax.broadcasted_iota(jnp.int32, (16, BZ), 1)
    rows = own * geo.z_share((16, BZ), 1)
    rows = rows + jnp.where(lane == 0, 0.5 * below, 0.0)
    rows = rows + jnp.where(lane == BZ - 1, 0.5 * above, 0.0)
    y = lax.broadcasted_iota(jnp.int32, (BY, BZ), 0)
    share = geo.y_share()
    planes = []
    for i in range(3):
        plane = share * rows[3 * i + 1 : 3 * i + 2]
        plane = plane + jnp.where(y == 0, 0.5 * rows[3 * i : 3 * i + 1], 0.0)
        planes.append(plane + jnp.where(y == BY - 1, 0.5 * rows[3 * i + 2 : 3 * i + 3], 0.0))
    out = [planes[1]] * BX
    out[0] = planes[1] * geo.x_share(0) + 0.5 * planes[0]
    out[BX - 1] = planes[1] * geo.x_share(BX - 1) + 0.5 * planes[2]
    return out


def with_coarse(lay, row, gram_ref):
    return row + jnp.dot(row, gram_ref[...], precision=HIGHEST, preferred_element_type=F32)


def coarse_inner(lay, row):
    lane = lax.broadcasted_iota(jnp.int32, row.shape, 1)
    both = row * pltpu.roll(row, lay.offset, 1)
    return jnp.sum(jnp.where(lane >= lay.offset, both, 0.0), axis=1, keepdims=True)


def all_rows(v):
    return tree([v[8 * i : 8 * i + 8] for i in range(ROWS // 8)])


def weighted_rows(geo, v):
    yz = geo.yz_weight()
    parts = []
    for x in range(BX):
        weight = geo.x_weight(x)
        part = v[x * BY : (x + 1) * BY]
        if not (isinstance(weight, float) and weight == 1.0):
            part = part * weight
        parts.append(part)
    total = tree(parts)
    total = total * yz
    return total[0:8] + total[8:16]


def weak_form(level, tab, zt, work):
    gx, gy, gz = along_x(level, "d"), along_y(level, "d", tab, work.at[0]), along_z(level, "d", zt)
    inv_norm = lax.rsqrt(1.0 + gx * gx + gy * gy + gz * gz)
    coef = bmass_of(tab) * (level * (1.0 - level) * inv_norm - INTERFACE_WIDTH)
    out = along_x(coef * gx, "t") + along_y(coef * gy, "t", tab, work.at[1])
    return out + along_z(coef * gz, "t", zt)


def stiffness(v, scaled, tab, zt, work, final):
    bm = bmass_of(tab)
    gx, gy, gz = along_x(v, "d"), along_y(v, "d", tab, work.at[0]), along_z(v, "d", zt)
    tx, ty, tz = scaled * gx, scaled * gy, scaled * gz
    if final:
        return None, all_rows(bm * v * v + (tx * gx + ty * gy + tz * gz))
    out = bm * v + along_x(tx, "t") + along_y(ty, "t", tab, work.at[1])
    out = out + along_z(tz, "t", zt)
    return out, all_rows(v * out)


def local_step(geo, lay, residual, dinv, scaled, state, image, refs):
    tab, zt, hot, u_ref, f_ref, send_ref, xs, ys, q_ref, state_ref, work, zwork, final = refs
    s_row, ts_row, gamma, curvature = state
    jacobi = residual * dinv
    planes = spread(geo, s_row, hot)
    u = jnp.concatenate([jacobi[x * BY : (x + 1) * BY] + planes[x] for x in range(BX)], axis=0)
    u_ref[...] = u
    local, energy = stiffness(u, scaled, tab, zt, work, final)
    sums = [weighted_rows(geo, residual * jacobi), energy]
    if image is not None:
        sums.append(weighted_rows(geo, u * image))
    ones = jnp.ones_like(s_row)
    coarse = coarse_inner(lay, s_row)
    state_ref[...] = jnp.concatenate(
        [s_row, ts_row, ones * gamma, ones * curvature, ones * coarse, jnp.zeros((3, lay.lanes), F32)],
        axis=0,
    )
    if final:
        scalars = jnp.sum(plain_sums(sums, hot), axis=0, keepdims=True)
        rows = [scalars[:, i * 128 : (i + 1) * 128] for i in range(lay.scalar_rows)]
        rows = jnp.concatenate(rows, axis=0)
        send_ref[...] = jnp.broadcast_to(rows[None], send_ref.shape)
        return
    scalars = partial_sums(geo, local, sums, q_ref, hot)
    local = local_sum_xy(local)
    f_ref[...] = local_sum_z(local)
    send_field(geo, lay, f_ref, local, zwork, scalars, send_ref, xs, ys)


def step_sizes(lay, recv_ref, state_ref, first):
    row = received_scalars(lay, recv_ref)
    lane = lax.broadcasted_iota(jnp.int32, row.shape, 1)

    def pick(which):
        return jnp.sum(jnp.where(lane == lay.plain + which, row, 0.0), axis=1, keepdims=True)

    gamma = pick(0) + state_ref[4:5, 0:1]
    if first:
        curvature = pick(1)
        beta = None
    else:
        beta = gamma / state_ref[2:3, 0:1]
        curvature = pick(1) + beta * (2.0 * pick(2) + beta * state_ref[3:4, 0:1])
    return row, gamma, curvature, beta, gamma / curvature


def build(mesh):
    sizes = tuple(int(mesh.shape[a]) for a in AXES)
    lay = Layout(sizes)
    steps = [face_steps(sizes[0]), face_steps(sizes[1])]
    nx, ny = len(steps[0]), len(steps[1])
    tab_np, zt_np = const_tables(), z_tables()
    number = np.arange(lay.lanes)
    places_np = np.full((8, lay.lanes), -9.0, np.float32)
    for half in range(2):
        lanes = slice(half * lay.offset, half * lay.offset + lay.devices)
        for a, place in enumerate(np.unravel_index(np.arange(lay.devices), sizes)):
            places_np[3 * half + a, lanes] = place
    block = jax.ShapeDtypeStruct((ROWS, BZ), F32)

    def like(*shape):
        return jax.ShapeDtypeStruct(shape, F32)

    def outgoing(fields):
        return (
            [like(lay.devices, lay.slot_rows, 128)]
            + [like(BY * fields, BZ)] * nx
            + [like(BX * fields, BZ)] * ny
        )

    def call(kernel, ins, outs, scratch, name, from_hbm=()):
        spec = pl.BlockSpec(memory_space=pltpu.VMEM)
        hbm = pl.BlockSpec(memory_space=pltpu.HBM)
        ins = [pltpu.with_memory_space_constraint(v, pltpu.HBM) if i in from_hbm else v for i, v in enumerate(ins)]
        return pl.pallas_call(
            kernel,
            out_shape=outs,
            in_specs=[hbm if i in from_hbm else spec for i in range(len(ins))],
            out_specs=[hbm if name == "pressure" else spec] * len(outs),
            scratch_shapes=scratch,
            compiler_params=pltpu.CompilerParams(vmem_limit_bytes=48 * 1024 * 1024),
            cost_estimate=pl.CostEstimate(flops=4000000, bytes_accessed=1000000, transcendentals=0),
            name=name,
        )(*ins)

    work = pltpu.VMEM((ROWS, BZ), F32)
    qrows = pltpu.VMEM((32, BZ), F32)
    pair = pltpu.VMEM((2, ROWS, BZ), F32)
    tiles = pltpu.VMEM((48, BZ), F32)

    def ring(v, axis, n, step):
        if step == "swap":
            pairs = [(0, 1), (1, 0)]
        else:
            d = 1 if step == "up" else n - 1
            pairs = [(i, (i + d) % n) for i in range(n)]
        return lax.ppermute(v, axis, pairs)

    def exchange(out):
        send, faces = out[0], out[1:]
        recv = lax.all_to_all(send, AXES, 0, 0, tiled=True)
        xs = [ring(faces[i], "gx", sizes[0], s) for i, s in enumerate(steps[0])]
        ys = [ring(faces[nx + i], "gy", sizes[1], s) for i, s in enumerate(steps[1])]
        return [recv, *xs, *ys]

    n_out = 1 + nx + ny

    def split(refs):
        return refs[0], refs[1 : 1 + nx], refs[1 + nx : 1 + nx + ny]

    def start_kernel(level_any, vel_any, tab_any, zt_any, *rest):
        send, xs, ys = split(rest[:n_out])
        f_ref, work, zwork = rest[n_out : n_out + 3]
        level_ref, zt_ref, tab_ref, vel_ref, sems = rest[n_out + 3 :]
        sources = (level_any, zt_any.at[0 : 2 * BZ], tab_any, vel_any)
        copies = [
            pltpu.make_async_copy(source, target, sems.at[i])
            for i, (source, target) in enumerate(zip(sources, (level_ref, zt_ref, tab_ref, vel_ref)))
        ]
        for copy in copies:
            copy.start()
        for copy in copies[:3]:
            copy.wait()
        geo = Geometry(sizes)
        level = level_ref[...]
        gx, gy, gz = along_x(level, "d"), along_y(level, "d", tab_ref, work.at[0]), along_z(level, "d", zt_ref)
        copies[3].wait()
        advect = bmass_of(tab_ref) * (vel_ref[0] * gx + vel_ref[1] * gy + vel_ref[2] * gz)
        finish(geo, advect, f_ref, zwork, send, xs, ys)

    def finish(geo, v, f_ref, zwork, send, xs, ys, scalars=None, extra=None):
        v = local_sum_xy(v)
        f_ref[...] = local_sum_z(v)
        if scalars is None:
            scalars = jnp.zeros((1, lay.lanes), F32)
        send_field(geo, lay, f_ref, v, zwork, scalars, send, xs, ys, extra)

    def source_kernel(vel_ref, source_ref, factor_ref, tab_ref, zt_ref, places_ref, _, *rest):
        slots, xs, ys = split(rest[:n_out])
        f_ref, hot_ref, row_ref, q_ref, work, zwork = rest[n_out:]
        geo = Geometry(sizes)
        bm = bmass_of(tab_ref)
        div = bm * source_ref[...] + along_x(bm * vel_ref[0], "t")
        div = div + along_y(bm * vel_ref[1], "t", tab_ref, work.at[1])
        div = div + along_z(bm * vel_ref[2], "t", zt_ref)
        hot_ref[...] = coarse_tables(geo, lay, places_ref)
        row_ref[0:1, :] = partial_sums(geo, div, [], q_ref, hot_ref)
        factor = factor_ref[...]
        if lay.lanes > lay.devices:
            pad = jnp.zeros((1, lay.lanes - lay.devices), F32)
            factor = jnp.concatenate([factor, pad], axis=1)
        row_ref[1:2, :] = factor
        row_ref[2:8, :] = jnp.zeros((6, lay.lanes), F32)
        div = local_sum_xy(div)
        f_ref[...] = local_sum_z(div)
        slots[...] = jnp.zeros(slots.shape, F32)
        fill_field(geo, lay, f_ref, div, zwork, slots, 1)
        slots[geo.me] = jnp.zeros(slots.shape[1:], F32)
        fill_faces(geo, lay, f_ref, xs, ys)

    def first_kernel(recv, *rest):
        xs, ys = rest[:nx], rest[nx : nx + ny]
        level_ref, fa_ref, tab_ref, zt_ref, row_ref = rest[nx + ny : nx + ny + 5]
        out = rest[nx + ny + 5 :]
        send, oxs, oys = split(out[:n_out])
        level_out, f_ref, w_ref, work, zwork = out[n_out:]
        geo = Geometry(sizes)
        received(geo, lay, fa_ref[...], recv, xs, ys, w_ref, 0)
        level = level_ref[...] - TIME_STEP * w_ref[...] * inverse_mass(geo, tab_ref)
        level_out[...] = level
        weak = weak_form(level, tab_ref, zt_ref, work)
        finish(geo, weak, f_ref, zwork, send, oxs, oys, row_ref[0:1, :], row_ref[1:2, :])

    def rhs_kernel(recv, *rest):
        xs, ys = rest[:nx], rest[nx : nx + ny]
        rows_ref, fd_ref, hot_ref, r_ref, s_ref, hot_out, w_ref, gram_ref = rest[nx + ny :]
        geo = Geometry(sizes)
        at = lay.scalar_rows + 2
        factor = [rows_ref[:, at + i, :] for i in range(lay.scalar_rows)]
        factor = jnp.concatenate(factor, axis=1)
        after = lay.lanes - lay.offset - lay.devices
        shifted = [jnp.zeros((lay.offset, lay.lanes), F32), factor]
        if after:
            shifted.append(jnp.zeros((after, lay.lanes), F32))
        plain = [factor, jnp.zeros((lay.lanes - lay.devices, lay.lanes), F32)]
        gram_ref[...] = lax.dot_general(
            jnp.concatenate(shifted, axis=0),
            jnp.concatenate(plain, axis=0),
            (((1,), (1,)), ((), ())),
            precision=HIGHEST,
            preferred_element_type=F32,
        )
        received(geo, lay, fd_ref[...], recv, xs, ys, w_ref, 1)
        r_ref[...] = SOURCE_SCALE * w_ref[...]
        row = with_coarse(lay, SOURCE_SCALE * received_scalars(lay, rows_ref), gram_ref)
        s_ref[...] = jnp.broadcast_to(row, s_ref.shape)
        hot_out[...] = hot_ref[...]
        hot_out[48:144, :] = with_coarse(lay, hot_ref[48:144, :], gram_ref)

    def new_level(geo, recv, xs, ys, level_ref, f_ref, tab_ref, w_ref):
        received(geo, lay, f_ref[...], recv, xs, ys, w_ref, 0)
        return level_ref[...] + PSEUDO_STEP * w_ref[...] * inverse_mass(geo, tab_ref)

    def sweep_kernel(recv, *rest):
        xs, ys = rest[:nx], rest[nx : nx + ny]
        level_ref, fin_ref, tab_ref, zt_ref = rest[nx + ny : nx + ny + 4]
        slots, sxs, sys = split(rest[nx + ny + 4 : nx + ny + 4 + n_out])
        out = rest[nx + ny + 4 + n_out :]
        send, oxs, oys = split(out[:n_out])
        level_out, f_ref, w_ref, work, zwork = out[n_out:]
        geo = Geometry(sizes)
        level = new_level(geo, recv, xs, ys, level_ref, fin_ref, tab_ref, w_ref)
        level_out[...] = level
        v = local_sum_xy(weak_form(level, tab_ref, zt_ref, work))
        f_ref[...] = local_sum_z(v)
        send[...] = slots[...]
        fill_field(geo, lay, f_ref, v, zwork, send, 0)
        send[geo.me] = slots[geo.me]
        fill_faces(geo, lay, f_ref, oxs, oys)
        for to, part in zip((*oxs, *oys), (*sxs, *sys)):
            to[BY : 2 * BY, :] = part[...]

    def diagonal_kernel(recv, *rest):
        xs, ys = rest[:nx], rest[nx : nx + ny]
        level_ref, fin_ref, tab_ref, zt_ref = rest[nx + ny : nx + ny + 4]
        out = rest[nx + ny + 4 :]
        send, oxs, oys = split(out[:n_out])
        level_out, f_ref, scaled_ref, w_ref, work, zwork = out[n_out:]
        geo = Geometry(sizes)
        level = new_level(geo, recv, xs, ys, level_ref, fin_ref, tab_ref, w_ref)
        level_out[...] = level
        bm = bmass_of(tab_ref)
        scaled = bm / (GAS_DENSITY + (1.0 - GAS_DENSITY) * jnp.clip(level, 0.0, 1.0))
        scaled_ref[...] = scaled
        diag = bm + along_x(scaled, "s") + along_y(scaled, "s", tab_ref, work.at[0])
        diag = diag + along_z(scaled, "s", zt_ref)
        finish(geo, diag, f_ref, zwork, send, oxs, oys)

    def solve_kernel(recv, *rest):
        xs, ys = rest[:nx], rest[nx : nx + ny]
        fin_ref, r_ref, scaled_ref, s_ref, tab_ref, zt_ref, hot_ref = rest[nx + ny : nx + ny + 7]
        out = rest[nx + ny + 7 :]
        send, oxs, oys = split(out[:n_out])
        dinv_ref, u_ref, f_ref, state_ref, w_ref, work, zwork, q_ref = out[n_out:]
        geo = Geometry(sizes)
        received(geo, lay, fin_ref[...], recv, xs, ys, w_ref, 0)
        dinv = 1.0 / w_ref[...]
        dinv_ref[...] = dinv
        zero = jnp.zeros((1, 1), F32)
        s_row = s_ref[0:1, :]
        state = (s_row, jnp.zeros_like(s_row), zero, zero)
        refs = (tab_ref, zt_ref, hot_ref, u_ref, f_ref, send, oxs, oys)
        local_step(
            geo, lay, r_ref[...], dinv, scaled_ref[...], state, None, (*refs, q_ref, state_ref, work, zwork, False)
        )

    def make_iterate(first, final):
        def iterate_kernel(recv, *rest):
            xs, ys = rest[:nx], rest[nx : nx + ny]
            n_in = 9 + (0 if first else 3 if final else 1)
            ins = rest[nx + ny : nx + ny + n_in]
            fin_ref, r_ref, u_in, dinv_ref, scaled_ref, state_in = ins[:6]
            tab_ref, zt_ref, hot_ref = ins[6:9]
            si_in, p_in, x_in = (*ins[9:], None, None, None)[:3]
            out = rest[nx + ny + n_in :]
            if final:
                send, oxs, oys = out[0], (), ()
                out = out[1:]
                u_ref, state_ref, p_ref, x_ref, w_ref, work, zwork, q_ref = out
                f_ref = r_out = si_ref = None
            else:
                send, oxs, oys = split(out[:n_out])
                u_ref, state_ref, r_out, si_ref, f_ref, w_ref, work, zwork, q_ref = out[
                    n_out:
                ]
            geo = Geometry(sizes)
            row, gamma, curvature, beta, alpha = step_sizes(lay, recv, state_in, first)
            received(geo, lay, fin_ref[...], recv, xs, ys, w_ref, 0)
            image = w_ref[...]
            s_row, ts_row = state_in[0:1, :], row
            if not first:
                image = image + beta * si_in[...]
                ts_row = ts_row + beta * state_in[1:2, :]
            if final:
                p = u_in[...] + beta * p_in[...]
                p_ref[...] = p
                x_ref[...] = x_in[...] + alpha * p
            residual = r_ref[...] - alpha * image
            if not final:
                si_ref[...] = image
                r_out[...] = residual
            lane = lax.broadcasted_iota(jnp.int32, row.shape, 1)
            ts_row = jnp.where((lane < lay.devices) | (lane >= lay.offset), ts_row, 0.0)
            state = (s_row - alpha * ts_row, ts_row, gamma, curvature)
            refs = (tab_ref, zt_ref, hot_ref, u_ref, f_ref, send)
            local_step(
                geo,
                lay,
                residual,
                dinv_ref[...],
                scaled_ref[...],
                state,
                image,
                (*refs, oxs, oys, q_ref, state_ref, work, zwork, final),
            )

        return iterate_kernel

    def first_update_kernel(state_ref, u_in, p_ref, x_ref):
        p = u_in[...]
        p_ref[...] = p
        x_ref[...] = state_ref[2:3, 0:1] / state_ref[3:4, 0:1] * p

    def update_kernel(state_ref, u_in, old_ref, p_in, x_in, p_ref, x_ref):
        gamma = state_ref[2:3, 0:1]
        p = u_in[...] + gamma / old_ref[2:3, 0:1] * p_in[...]
        p_ref[...] = p
        x_ref[...] = x_in[...] + gamma / state_ref[3:4, 0:1] * p

    def last_kernel(recv, state_in, u_in, p_in, x_in, out_ref, work, sems):
        _, _, _, beta, alpha = step_sizes(lay, recv, state_in, False)
        copies = []
        for i in range(2):
            part = slice(i * ROWS // 2, (i + 1) * ROWS // 2)
            work[part, :] = x_in[part, :] + alpha * (u_in[part, :] + beta * p_in[part, :])
            copies.append(pltpu.make_async_copy(work.at[part], out_ref.at[part], sems.at[i]))
            copies[i].start()
        for copy in copies:
            copy.wait()

    def body(level_set, velocity, source, coarse_factor):
        level = level_set.reshape(ROWS, BZ)
        vel = velocity.reshape(3, ROWS, BZ)
        src = source.reshape(ROWS, BZ)
        tab, zt, places = jnp.asarray(tab_np), jnp.asarray(zt_np), jnp.asarray(places_np)
        out = call(
            start_kernel,
            [level, vel, tab, zt],
            outgoing(1) + [block],
            [pair, tiles]
            + [pltpu.VMEM(a, d) for a, d in ((level.shape, F32), ((2 * BZ, 2 * BZ), BF16), (tab.shape, F32), (vel.shape, F32))]
            + [pltpu.SemaphoreType.DMA((4,))],
            "advect",
            range(4),
        )
        fa = out[n_out]
        got = exchange(out[:n_out])
        side = call(
            source_kernel,
            [vel, src, coarse_factor, tab, zt, places, fa],
            outgoing(1) + [block, like(HOT_ROWS, lay.lanes), like(8, lay.lanes)],
            [qrows, pair, tiles],
            "source",
        )
        fd, hot, row = side[n_out:]
        out = call(
            first_kernel,
            [*got, level, fa, tab, zt, row],
            outgoing(1) + [block, block],
            [work, pair, tiles],
            "sweep_first",
        )
        level, f = out[n_out:]
        got = rows = exchange(out[:n_out])
        out = call(
            sweep_kernel,
            [*got, level, f, tab, zt, *side[:n_out]],
            outgoing(2) + [block, block],
            [work, pair, tiles],
            "sweep",
        )
        level, f = out[n_out:]
        got = exchange(out[:n_out])
        residual, s_rows, hot = call(
            rhs_kernel,
            [*got, rows[0], fd, hot],
            [block, like(8, lay.lanes), like(HOT_ROWS, lay.lanes)],
            [work, pltpu.VMEM((lay.lanes, lay.lanes), F32)],
            "rhs",
        )
        out = call(
            diagonal_kernel,
            [*got, level, f, tab, zt],
            outgoing(1) + [block, block, block],
            [work, pair, tiles],
            "diagonal",
        )
        level, f, scaled = out[n_out:]
        got = exchange(out[:n_out])
        out = call(
            solve_kernel,
            [*got, f, residual, scaled, s_rows, tab, zt, hot],
            outgoing(1) + [block, block, block, like(8, lay.lanes)],
            [work, pair, tiles, qrows],
            "solve_start",
        )
        dinv, u, f, state = out[n_out:]
        p = image = x = None
        for step in range(ITERS - 1):
            first, final = step == 0, step == ITERS - 2
            got = exchange(out[:n_out])
            ins = [*got, f, residual, u, dinv, scaled, state, tab, zt, hot]
            if not first:
                ins.append(image)
            if final:
                ins += [p, x]
            fields = [block, like(8, lay.lanes), block, block]
            if final:
                outs = [like(lay.devices, lay.scalar_rows, 128)] + fields
            else:
                outs = outgoing(1) + fields + [block]
            out = call(make_iterate(first, final), ins, outs, [work, pair, tiles, qrows], "iterate")
            if final:
                u, state, p, x = out[1:]
            else:
                old, u_old = state, u
                u, state, residual, image, f = out[n_out:]
                more = [] if first else [old, p, x]
                kernel = first_update_kernel if first else update_kernel
                p, x = call(kernel, [state, u_old, *more], [block, block], [], "update")
        recv = lax.all_to_all(out[0], AXES, 0, 0, tiled=True)
        (x,) = call(last_kernel, [recv, state, u, p, x], [block], [work, pltpu.SemaphoreType.DMA((2,))], "pressure")
        return level.reshape(BX, BY, BZ), x.reshape(BX, BY, BZ)

    return body


def solution(mesh):
    in_specs = (
        P("gx", "gy", "gz"),
        P(None, "gx", "gy", "gz"),
        P("gx", "gy", "gz"),
        P(("gx", "gy", "gz"), None),
    )
    out_specs = (P("gx", "gy", "gz"), P("gx", "gy", "gz"))
    return jax.shard_map(
        build(mesh), mesh=mesh, in_specs=in_specs, out_specs=out_specs, check_vma=False
    )
```
